32 devices in a mesh: parts: 2 (over y), group: 8 (over z, x), tensor: 2 (over core).
Axes of the slice: x: 2, y: 2, z: 4, core: 2. Of those that a mesh axis runs over, the one named last changes fastest.
Arguments:
- normed_hidden_states: bfloat16 [1024, 2, 8192], P(('parts', 'group'), None, 'tensor'), parts along dimension 0, may hold values from -6 to 6
- query_matrix: bfloat16 [8192, 512], P('tensor', 'group'), may hold values from -0.0625 to 0.0625
- factor_down: bfloat16 [8, 8192, 64], P('group', None, 'tensor'), may hold values from -0.0625 to 0.0625
- factor_up: bfloat16 [8, 64, 512], P('group', None, 'tensor'), may hold values from -0.75 to 0.75
- kv_cache: bfloat16 [1024, 32, 256], P(('parts', 'group'), 'tensor'), parts along dimension 0, may hold values from -500 to 500
- incoming_key_value: bfloat16 [1024, 2, 256], P(('parts', 'group')), parts along dimension 0, may hold values from -6 to 6
- kv_lengths: int32 [1024], P(('parts', 'group')), parts along dimension 0, may hold values from 1 to 32, 8192 in all
- request_adapter: int32 [1024], P(('parts', 'group')), parts along dimension 0, may hold values from 0 to 7, as said below
- adapter_owner: int32 [16], P('parts'), parts along dimension 0, may hold values from 0 to 7, as said below
Outputs:
- queries: bfloat16 [1024, 2, 512], P(('parts', 'group')), parts along dimension 0
- attended: bfloat16 [1024, 2, 512], P(('parts', 'group')), parts along dimension 0
The draws below stay inside these ranges and needn't reach their ends.
There are 2 independent parts, one for each index of `parts`. The reference program is written for one: setup_inputs(seed, part) draws one part's arguments, and reference() takes and returns one part's arrays. A program takes and returns all parts, laid end to end along the dimension named above; an argument that names none is the same for every part. Nothing has to cross between parts.
Inputs may be any that keep to these rules, and one draw needn't show every extreme that they name: `adapter_owner`: each owner holds exactly one adapter. `request_adapter`: within each aligned block of 64 requests (the requests of one device), at most 8 requests name adapters of one owner, and in every block some owner is named by exactly 8.
All inputs are finite; a program needn't handle non-finite values. No bound on the sum of `kv_lengths` on one device may be relied on, other than what follows from the above.
Results may differ from the reference program's by a relative error of at most 0.01695.
Values may be sent and summed in bfloat16 or wider, within the bound.
No kernel may reach another device: no remote copies, remote signals or barrier semaphores. Data moves between devices by JAX's collectives and lax.ppermute only.
A program may use at most 64 MiB of HBM per device.

```python
import math
import jax
import jax.numpy as jnp
import numpy as np
from jax import lax

D = 8192
HD = 128
RANK = 64
QHEADS = 4
STEPS = 2
REQ_DEV = 64
CTX = 32
QW = 512
ADAPTERS = 8
REQUESTS = 512
CAPR = 8


favored = 2


def owner_table(key):
    return jax.random.permutation(key, ADAPTERS).astype(jnp.int32)


def draw_adapter_owner(key, part):
    return owner_table(key)


def draw_request_adapter(key, part):
    lookup = owner_table(key)
    key = jax.random.fold_in(key, 5)
    adapter_at = jnp.argsort(lookup).astype(jnp.int32)
    popular_key, device_key = jax.random.split(key)
    popular = jax.random.permutation(popular_key, ADAPTERS)[:favored].astype(jnp.int32)
    owner_ids = jnp.arange(ADAPTERS, dtype=jnp.int32)
    favored_rank = jnp.sum(jnp.where(popular[:, None] == owner_ids[None, :], jnp.arange(favored, dtype=jnp.int32)[:, None] + 1, 0), axis=0)

    def device_owners(device):
        own_key = jax.random.fold_in(device_key, device)
        order_key, place_key = jax.random.split(own_key)
        shuffle = jax.random.permutation(order_key, ADAPTERS).astype(jnp.int32)
        priority = jnp.where(favored_rank > 0, favored_rank - 1, favored + shuffle)
        ranking = jnp.argsort(priority).astype(jnp.int32)
        chosen = ranking[jnp.arange(REQ_DEV, dtype=jnp.int32) // CAPR]
        placing = jax.random.permutation(place_key, REQ_DEV)
        return chosen[placing]
    owners_all = jax.vmap(device_owners)(jnp.arange(ADAPTERS, dtype=jnp.int32)).reshape(-1)
    return adapter_at[owners_all].astype(jnp.int32)


def draw_kv_cache(key, part):
    key = jax.random.fold_in(key, 11)
    base_key = jax.random.fold_in(key, 0)
    entries = jnp.clip(jax.random.normal(base_key, (REQUESTS, CTX, 2 * HD), jnp.float32), -6.0, 6.0)
    return entries.astype(jnp.bfloat16)


def block_levels(key, shape, pieces, smallest, top_value):
    factor_of, own = 1.0, jax.random.fold_in(key, 6)
    for dim, parts in pieces:
        steps = jnp.exp(jax.random.uniform(jax.random.fold_in(own, dim), (parts,), jnp.float32, smallest / len(pieces), top_value / len(pieces)))
        factor_of = factor_of * jnp.repeat(steps, shape[dim] // parts).reshape([-1 if axis == dim else 1 for axis in range(len(shape))])
    return factor_of


def split_up(number_of, total, most, slope):
    portions = [(1 << 20) // math.isqrt(standing ** slope) + 1 for standing in range(2, number_of + 1)]
    surplus, counts = total - most - (number_of - 1), [1] * (number_of - 1)
    while surplus > 0:
        candidates = [i for i in range(number_of - 1) if counts[i] < most]
        pool, budget = sum([portions[i] for i in candidates]), surplus
        for i in candidates:
            addition = min(most - counts[i], max(1, budget * portions[i] // pool), surplus)
            counts[i] = counts[i] + addition
            surplus = surplus - addition
    return np.array([most] + counts)


def uneven(key, number_of, total, reach, lean):
    if number_of == 2:
        one = jax.random.randint(key, (), max(1, total - reach), min(reach, total - 1) + 1)
        return jnp.stack([one, total - one])
    lengths = jnp.asarray(split_up(number_of, total, reach, lean), jnp.int32)
    pairs = (number_of - 1) // 2
    source_of, receiver = lengths[1:1 + 2 * pairs:2], lengths[2:2 + 2 * pairs:2]
    margin = jnp.minimum(source_of - 1, reach - receiver)
    passed = jax.random.randint(jax.random.fold_in(key, 1), (pairs,), 0, 1 << 20) % (margin + 1)
    lengths = lengths.at[1:1 + 2 * pairs:2].set(source_of - passed).at[2:2 + 2 * pairs:2].set(receiver + passed)
    return lengths[jax.random.permutation(jax.random.fold_in(key, 2), number_of)]


def scatter_about(key, extent, scale, reach, cuts=(), kind=jnp.bfloat16):
    drawn = scale * jax.random.normal(key, extent, jnp.float32)
    if cuts:
        drawn = drawn * block_levels(key, extent, cuts, -0.22, 0.18)
    return jnp.clip(drawn, -reach, reach).astype(kind)


def setup_inputs(seed: int = 0, part: int = 0) -> dict:
    streams_of = jax.random.split(jax.random.key(seed), 10)
    part_keys = jax.random.split(jax.random.fold_in(streams_of[9], part), 10)
    return {
        "normed_hidden_states": scatter_about(part_keys[0], (REQUESTS, STEPS, D), 1.0, 6.0, ((0, 8), (2, 2))),
        "query_matrix": scatter_about(streams_of[1], (D, QW), D ** -0.5, 0.0625, ((0, 2), (1, 8))),
        "factor_down": scatter_about(streams_of[2], (ADAPTERS, D, RANK), D ** -0.5, 0.0625, ((0, 8), (2, 2))),
        "factor_up": scatter_about(streams_of[3], (ADAPTERS, RANK, QW), RANK ** -0.5, 0.75, ((0, 8), (2, 2))),
        "kv_cache": draw_kv_cache(jax.random.fold_in(jax.random.fold_in(streams_of[9], part), 71), part),
        "incoming_key_value": scatter_about(part_keys[5], (REQUESTS, STEPS, 2 * HD), 1.0, 6.0, ((0, 8),)),
        "kv_lengths": uneven(part_keys[6], REQUESTS, REQUESTS * CTX // 2, CTX, 2).astype(jnp.int32),
        "request_adapter": draw_request_adapter(jax.random.fold_in(jax.random.fold_in(streams_of[9], part), 71), part),
        "adapter_owner": draw_adapter_owner(jax.random.fold_in(jax.random.fold_in(streams_of[9], part), 71), part),
    }


def reference(normed_hidden_states, query_matrix, factor_down, factor_up, kv_cache, incoming_key_value, kv_lengths, request_adapter, adapter_owner):
    holder = jnp.take(adapter_owner, request_adapter).astype(jnp.int32)
    flattened = normed_hidden_states.reshape(REQUESTS * STEPS, D)
    base_part = jnp.dot(flattened, query_matrix, preferred_element_type=jnp.float32).reshape(REQUESTS, STEPS, QW)

    def adapt(request_number):
        owner_id = holder[request_number]
        shrink = jnp.dot(normed_hidden_states[request_number], factor_down[owner_id], preferred_element_type=jnp.float32).astype(jnp.bfloat16)
        return jnp.dot(shrink, factor_up[owner_id], preferred_element_type=jnp.float32)
    adapted = lax.map(adapt, jnp.arange(REQUESTS, dtype=jnp.int32))
    queries = (base_part + adapted).astype(jnp.bfloat16)
    stored = lax.optimization_barrier(queries)
    scaling = 1.0 / math.sqrt(HD)

    def attend(request_number):
        projected_query_rows = stored[request_number].astype(jnp.float32).reshape(STEPS, QHEADS, HD)
        cache_rows = kv_cache[request_number].astype(jnp.float32)
        fresh_rows = incoming_key_value[request_number].astype(jnp.float32)
        key_rows = jnp.concatenate([cache_rows[:, :HD], fresh_rows[:, :HD]], axis=0)
        value_rows = jnp.concatenate([cache_rows[:, HD:], fresh_rows[:, HD:]], axis=0)
        scores = jnp.einsum('shd,pd->shp', projected_query_rows, key_rows) * scaling
        position = jnp.arange(CTX + STEPS, dtype=jnp.int32)
        step_ids = jnp.arange(STEPS, dtype=jnp.int32)
        usable = jnp.where(position[None, :] < CTX, position[None, :] < kv_lengths[request_number], position[None, :] - CTX <= step_ids[:, None])
        masked = jnp.where(usable[:, None, :], scores, -1e+30)
        highest = lax.optimization_barrier(jnp.max(masked, axis=2, keepdims=True))
        attention_weights = jnp.where(usable[:, None, :], jnp.exp(masked - highest), 0.0)
        totals = lax.optimization_barrier(jnp.sum(attention_weights, axis=2, keepdims=True))
        rounded = lax.optimization_barrier(attention_weights.astype(jnp.bfloat16)).astype(jnp.float32)
        mixture = jnp.einsum('shp,pd->shd', rounded, value_rows) / totals
        return mixture.reshape(STEPS, QW).astype(jnp.bfloat16)
    attended = lax.map(attend, jnp.arange(REQUESTS, dtype=jnp.int32))
    return (queries, attended)
```

```python
import functools
import math

import jax
import jax.numpy as jnp
from jax import lax
from jax.experimental import pallas as pl
from jax.experimental.pallas import tpu as pltpu
from jax.sharding import PartitionSpec as P

SWAP = [(0, 1), (1, 0)]
FAR = -1e30


def nt_dot(a, b):
    return lax.dot_general(a, b, (((1,), (1,)), ((), ())), preferred_element_type=jnp.float32)


def pair_product_kernel(own_ref, near_ref, first_ref, second_ref, out_ref):
    rows, half = own_ref.shape[0], first_ref.shape[0]
    weights = jnp.concatenate([first_ref[...], second_ref[...]], axis=0)
    out_ref[:rows, :] = nt_dot(own_ref[...], weights)
    out_ref[rows:, :] = nt_dot(near_ref[...], weights)


def pair_product(own, near, first, second):
    return pl.pallas_call(
        pair_product_kernel,
        out_shape=jax.ShapeDtypeStruct((2 * own.shape[0], 2 * first.shape[0]), jnp.float32),
        compiler_params=pltpu.CompilerParams(vmem_limit_bytes=24 << 20),
    )(own, near, first, second)


def last_product_kernel(
    where_ref, own_ref, near_ref, first_ref, second_ref, t0_ref, t1_ref, t2_ref, holder_ref, out_ref, t3_ref
):
    z, x, y = where_ref[0], where_ref[1], where_ref[2]
    pair_product_kernel(own_ref, near_ref, first_ref, second_ref, t3_ref)
    low_pair = z < 2
    places = (z, z + 1 - 2 * lax.rem(z, 2), jnp.where(low_pair, 2, 1), jnp.where(low_pair, 3, 0))
    rows, width = t3_ref.shape
    half = width // 2
    low_lanes = lax.broadcasted_iota(jnp.int32, (rows, width), 1) < half
    holder = holder_ref[...]
    columns = [jnp.zeros((rows, width), jnp.float32) for _ in range(4)]
    shrink = jnp.zeros((rows, width), jnp.float32)
    for j, ref in enumerate((t0_ref, t1_ref, t2_ref, t3_ref)):
        t = ref[...]
        if j > 0:
            t = jnp.where(y == 0, t, pltpu.roll(t, half, 1))
        shrink = shrink + jnp.where(holder == places[j] * 2 + x, t, 0.0)
        columns = [jnp.where(places[j] == k, t, columns[k]) for k in range(4)]
    out_ref[:, :width] = jnp.where(low_lanes, columns[0], pltpu.roll(columns[1], half, 1))
    out_ref[:, width : 2 * width] = jnp.where(low_lanes, columns[2], pltpu.roll(columns[3], half, 1))
    out_ref[:, 2 * width :] = jnp.where(low_lanes, 0.0, shrink)


def last_product(where, own, near, first, second, t0, t1, t2, holder):
    rows, width = t0.shape
    vmem = pl.BlockSpec(memory_space=pltpu.VMEM)
    return pl.pallas_call(
        last_product_kernel,
        out_shape=jax.ShapeDtypeStruct((rows, 3 * width), jnp.float32),
        in_specs=[pl.BlockSpec(memory_space=pltpu.SMEM)] + [vmem] * 8,
        out_specs=vmem,
        scratch_shapes=[pltpu.VMEM((rows, width), jnp.float32)],
        compiler_params=pltpu.CompilerParams(vmem_limit_bytes=24 << 20),
    )(where, own, near, first, second, t0, t1, t2, holder)


def attend_block(queries, keys, values, masks, scaling):
    scores = [jnp.where(m, nt_dot(queries, k) * scaling, FAR) for k, m in zip(keys, masks)]
    highest = scores[0].max(axis=1, keepdims=True)
    for s in scores[1:]:
        highest = jnp.maximum(highest, s.max(axis=1, keepdims=True))
    weights = [jnp.where(m, jnp.exp(s - highest), 0.0) for s, m in zip(scores, masks)]
    totals = sum(w.sum(axis=1, keepdims=True) for w in weights)
    sums = sum(
        jnp.dot(w.astype(jnp.bfloat16), v, preferred_element_type=jnp.float32)
        for w, v in zip(weights, values)
    )
    return sums / totals


def attend(queries, caches, fresh_ref, lengths_ref, out_ref, steps, head, per):
    rows = queries.shape[0]
    requests = rows // steps
    heads = queries.shape[1] // head
    scaling = 1.0 / math.sqrt(head)
    take = per * steps
    for b in range(requests // per):
        part = queries[b * take : (b + 1) * take, :]
        stacked = jnp.concatenate([part[:, h * head : (h + 1) * head] for h in range(heads)], axis=0)
        limit = jnp.concatenate([lengths_ref[b * take : (b + 1) * take, :]] * heads, axis=0)
        keys, values, masks = [], [], []
        for c, cache_ref in enumerate(caches):
            count = cache_ref.shape[0] // requests
            block = cache_ref[b * per * count : (b + 1) * per * count, :]
            shape = (heads * take, per * count)
            request = lax.rem(lax.broadcasted_iota(jnp.int32, shape, 0), take) // steps
            column = lax.broadcasted_iota(jnp.int32, shape, 1)
            position = lax.rem(column, count) + c * count
            masks.append(jnp.logical_and(column // count == request, position < limit))
            keys.append(block[:, :head])
            values.append(block[:, head:])
        block = fresh_ref[b * take : (b + 1) * take, :]
        shape = (heads * take, take)
        row = lax.rem(lax.broadcasted_iota(jnp.int32, shape, 0), take)
        column = lax.broadcasted_iota(jnp.int32, shape, 1)
        masks.append(jnp.logical_and(row // steps == column // steps, column <= row))
        keys.append(block[:, :head])
        values.append(block[:, head:])
        mixed = attend_block(stacked, keys, values, masks, scaling).astype(jnp.bfloat16)
        for h in range(heads):
            out_ref[b * take : (b + 1) * take, h * head : (h + 1) * head] = mixed[
                h * take : (h + 1) * take, :
            ]


def finish_kernel(
    steps, per, where_ref, mine_ref, other_ref, got_ref, holder_ref, up_ref,
    low_ref, high_ref, fresh_ref, lengths_ref, queries_ref, out_ref,
):
    x = where_ref[1]
    rows = got_ref.shape[0]
    width = got_ref.shape[1] // 3
    half = width // 2
    here = mine_ref[...] + other_ref[...]
    there = got_ref[...]
    even = jnp.where(x == 0, here, there)
    odd = jnp.where(x == 0, there, here)
    low_lanes = lax.broadcasted_iota(jnp.int32, (rows, width), 1) < half
    groups = []
    for k in range(4):
        g = (k // 2) * width
        left, right = even[:, g : g + width], odd[:, g : g + width]
        if k % 2 == 0:
            groups.append(jnp.where(low_lanes, left, pltpu.roll(right, half, 1)))
        else:
            groups.append(jnp.where(low_lanes, pltpu.roll(left, half, 1), right))
    base = jnp.concatenate(groups, axis=1)
    shrink = here[:, 2 * width :] + there[:, 2 * width :]
    shrink = jnp.where(low_lanes, pltpu.roll(shrink, half, 1), shrink)
    holder = holder_ref[...]
    owners = up_ref.shape[0] // half
    lane_owner = (lax.broadcasted_iota(jnp.int32, (rows, width), 1) >= half).astype(jnp.int32)
    spread = jnp.concatenate(
        [jnp.where(holder == lane_owner + 2 * k, shrink, 0.0) for k in range(owners // 2)], axis=1
    ).astype(jnp.bfloat16)
    adapted = jnp.dot(spread, up_ref[...], preferred_element_type=jnp.float32)
    queries = (base + adapted).astype(jnp.bfloat16)
    queries_ref[...] = queries
    head = fresh_ref.shape[1] // 2
    attend(queries, (low_ref, high_ref), fresh_ref, lengths_ref, out_ref, steps, head, per)


def finish(steps, where, mine, other, got, holder, up, low, high, fresh, lengths):
    rows = got.shape[0]
    vmem = pl.BlockSpec(memory_space=pltpu.VMEM)
    shape = jax.ShapeDtypeStruct((rows, up.shape[1]), jnp.bfloat16)
    return pl.pallas_call(
        functools.partial(finish_kernel, steps, 8),
        out_shape=(shape, shape),
        in_specs=[pl.BlockSpec(memory_space=pltpu.SMEM)] + [vmem] * 9,
        out_specs=(vmem, vmem),
        compiler_params=pltpu.CompilerParams(vmem_limit_bytes=24 << 20),
    )(where, mine, other, got, holder, up, low, high, fresh, lengths)


def attend_kernel(steps, per, q_ref, low_ref, high_ref, fresh_ref, lengths_ref, out_ref):
    head = fresh_ref.shape[1] // 2
    attend(q_ref[...], (low_ref, high_ref), fresh_ref, lengths_ref, out_ref, steps, head, per)


def line_pairs(groups, moves):
    return [(a * 2 + x, b * 2 + x) for a, b in moves for x in range(2)]


def holders_of(request_adapter, adapter_owner):
    ids = jnp.arange(adapter_owner.shape[0], dtype=jnp.int32)
    lookup = request_adapter[:, None] == ids[None, :]
    return jnp.sum(jnp.where(lookup, adapter_owner[None, :], 0), axis=1)


def body(
    normed_hidden_states,
    query_matrix,
    factor_down,
    factor_up,
    kv_cache,
    incoming_key_value,
    kv_lengths,
    request_adapter,
    adapter_owner,
):
    groups = lax.axis_size("group")
    core = lax.axis_index("tensor")
    requests, steps, features = normed_hidden_states.shape
    rows = requests * steps
    holder = holders_of(request_adapter, adapter_owner)
    holder_rows = jnp.repeat(holder, steps)[:, None]
    lengths_rows = jnp.repeat(kv_lengths, steps)[:, None]

    down = factor_down[0].T
    kept = lax.dynamic_slice_in_dim(down, core * features, features, 1)
    given = lax.dynamic_slice_in_dim(down, (1 - core) * features, features, 1)
    taken = lax.ppermute(given, "tensor", SWAP)
    down_block = jnp.where(
        core == 0, jnp.concatenate([kept, taken], 0), jnp.concatenate([taken, kept], 0)
    )
    query_block = query_matrix.T

    other_cache = lax.ppermute(kv_cache, "tensor", SWAP)
    low = jnp.where(core == 0, kv_cache, other_cache).reshape(-1, kv_cache.shape[2])
    high = jnp.where(core == 0, other_cache, kv_cache).reshape(-1, kv_cache.shape[2])
    fresh = incoming_key_value.reshape(rows, -1)

    up = lax.all_gather(factor_up[0], "group", axis=0, tiled=True)
    up_other = lax.ppermute(up, "tensor", SWAP)
    up_full = jnp.where(
        core == 0, jnp.concatenate([up, up_other], 1), jnp.concatenate([up_other, up], 1)
    )
    own = normed_hidden_states.reshape(rows, features)
    width = query_matrix.shape[1] * groups
    out_shape = (requests, steps, width)

    if groups == 8 and lax.axis_size("parts") == 2 and query_block.shape == down_block.shape:
        place = lax.axis_index("group")
        z, x, y = place // 2, lax.rem(place, 2), lax.axis_index("parts")
        where = jnp.stack([z, x, y]).astype(jnp.int32)
        middle = jnp.logical_or(z == 1, z == 2)
        along = lambda a, moves: lax.ppermute(a, "group", line_pairs(groups, moves))
        ends, inner = ((0, 1), (1, 0), (2, 3), (3, 2)), ((1, 2), (2, 1))
        outward = ((1, 0), (2, 3))
        beside = [(i, i ^ 1) for i in range(groups)]
        mine = jnp.where(y == 0, query_block, down_block)
        near = lax.ppermute(normed_hidden_states, "group", beside).reshape(rows, features)
        near_holder = lax.ppermute(holder_rows, "group", beside)
        both_holders = jnp.concatenate([holder_rows, near_holder], axis=0)
        e1 = along(mine, ends)
        m1 = along(mine, inner)
        m2 = along(e1, inner)
        p1 = along(m1, outward)
        p2 = along(m2, outward)
        r1, r2, r3 = e1, jnp.where(middle, m1, p1), jnp.where(middle, m2, p2)
        s1, s2, s3 = (lax.ppermute(r, "parts", SWAP) for r in (r1, r2, r3))
        t0 = pair_product(own, near, query_block, down_block)
        t1 = pair_product(own, near, r1, s1)
        t2 = pair_product(own, near, r2, s2)
        total = last_product(where, own, near, r3, s3, t0, t1, t2, both_holders)
        total_other = lax.ppermute(total, "tensor", SWAP)
        got = lax.ppermute(total[rows:] + total_other[rows:], "group", beside)
        queries, attended = finish(
            steps, where, total[:rows], total_other[:rows], got,
            holder_rows, up_full, low, high, fresh, lengths_rows,
        )
        return queries.reshape(out_shape), attended.reshape(out_shape)

    place = lax.axis_index("group")
    ring = [(i, (i + 1) % groups) for i in range(groups)]

    def step(k, carry):
        q_part, d_part, base, shrink = carry
        at = lax.rem(place - k + groups, groups)
        base = lax.dynamic_update_slice_in_dim(base, nt_dot(own, q_part), at * q_part.shape[0], 1)
        shrink = shrink + jnp.where(holder_rows == at, nt_dot(own, d_part), 0.0)
        q_part, d_part = (lax.ppermute(w, "group", ring) for w in (q_part, d_part))
        return q_part, d_part, base, shrink

    start = (
        query_block,
        down_block,
        jnp.zeros((rows, width), jnp.float32),
        jnp.zeros((rows, down_block.shape[0]), jnp.float32),
    )
    _, _, base, shrink = lax.fori_loop(0, groups, step, start)
    base = base + lax.ppermute(base, "tensor", SWAP)
    shrink = (shrink + lax.ppermute(shrink, "tensor", SWAP)).astype(jnp.bfloat16)
    named = holder_rows == jnp.arange(groups, dtype=jnp.int32)[None, :]
    spread = jnp.where(named[:, :, None], shrink[:, None, :], 0).reshape(rows, -1)
    adapted = jnp.dot(spread, up_full, preferred_element_type=jnp.float32)
    queries = (base + adapted).astype(jnp.bfloat16)
    attended = pl.pallas_call(
        functools.partial(attend_kernel, steps, 8),
        out_shape=jax.ShapeDtypeStruct(queries.shape, jnp.bfloat16),
        compiler_params=pltpu.CompilerParams(vmem_limit_bytes=24 << 20),
    )(queries, low, high, fresh, lengths_rows)
    return queries.reshape(out_shape), attended.reshape(out_shape)


def solution(mesh):
    placed = (
        P(("parts", "group"), None, "tensor"),
        P("tensor", "group"),
        P("group", None, "tensor"),
        P("group", None, "tensor"),
        P(("parts", "group"), "tensor", None),
        P(("parts", "group"), None, None),
        P(("parts", "group")),
        P(("parts", "group")),
        P("parts"),
    )
    return jax.shard_map(
        body,
        mesh=mesh,
        in_specs=placed,
        out_specs=(P(("parts", "group"), None, None), P(("parts", "group"), None, None)),
        check_vma=False,
    )
```

```python
import functools
import math

import jax
import jax.numpy as jnp
from jax import lax
from jax.experimental import pallas as pl
from jax.experimental.pallas import tpu as pltpu
from jax.sharding import PartitionSpec as P

SWAP = [(0, 1), (1, 0)]
FAR = -1e30


def nt_dot(a, b):
    return lax.dot_general(a, b, (((1,), (1,)), ((), ())), preferred_element_type=jnp.float32)


def first_kernel(*refs):
    *halves, w0_ref, w1_ref, w2_ref, out_ref = refs
    weights = jnp.concatenate([w[...] for w in (w0_ref, w1_ref, w2_ref)], axis=0)
    known = jnp.concatenate([h[...] for h in halves], axis=0)
    out_ref[:, : weights.shape[0]] = nt_dot(known, weights)


def last_kernel(core_ref, *refs):
    *known, late0_ref, late1_ref, w0_ref, w1_ref, w2_ref, w3_ref, t_ref, kept_ref, given_ref = refs
    half, count = known[0].shape[0], w3_ref.shape[0]
    weights = jnp.concatenate([w[...] for w in (w0_ref, w1_ref, w2_ref, w3_ref)], axis=0)
    late = nt_dot(jnp.concatenate([late0_ref[...], late1_ref[...]], axis=0), weights)
    fresh = nt_dot(jnp.concatenate([h[...] for h in known], axis=0), w3_ref[...])
    first = core_ref[0] == 0

    def value(k):
        at = slice(k * half, (k + 1) * half)
        return jnp.concatenate([t_ref[at, : 3 * count], fresh[at]], axis=1)

    halves = (
        (value(0), value(1)), (late[:half], value(2)), (value(3), late[half:]), (value(4), value(5)),
    )
    for k, (low, high) in enumerate(halves):
        kept_ref[k] = jnp.where(first, low, high)
        given_ref[k] = jnp.where(first, high, low)


def first_products(known, *weights):
    rows, count = known[0].shape[0], weights[0].shape[0]
    return pl.pallas_call(
        first_kernel,
        out_shape=jax.ShapeDtypeStruct((len(known) * rows, 4 * count), jnp.float32),
        cost_estimate=pl.CostEstimate(
            flops=36 * rows * count * known[0].shape[1], bytes_accessed=5 << 20, transcendentals=0
        ),
        compiler_params=pltpu.CompilerParams(vmem_limit_bytes=12 << 20),
    )(*known, *weights)


def last_products(core, known, late, weights, t):
    rows, count = known[0].shape[0], weights[0].shape[0]
    vmem = pl.BlockSpec(memory_space=pltpu.VMEM)
    shape = jax.ShapeDtypeStruct((4, rows, 4 * count), jnp.float32)
    return pl.pallas_call(
        last_kernel,
        out_shape=(shape, shape),
        in_specs=[pl.BlockSpec(memory_space=pltpu.SMEM)] + [vmem] * (len(known) + len(late) + 5),
        out_specs=(vmem, vmem),
        compiler_params=pltpu.CompilerParams(vmem_limit_bytes=12 << 20),
    )(core, *known, *late, *weights, t)


def add_kernel(a_ref, b_ref, *outs):
    for k, out in enumerate(outs):
        out[...] = a_ref[k + 1] + b_ref[k + 1]


def add_halves(a, b):
    shape = jax.ShapeDtypeStruct(a.shape[1:], a.dtype)
    return pl.pallas_call(
        add_kernel,
        out_shape=(shape,) * (a.shape[0] - 1),
        compiler_params=pltpu.CompilerParams(vmem_limit_bytes=2 << 20),
    )(a, b)


def attend_block(queries, keys, values, masks, scaling):
    scores = [jnp.where(m, nt_dot(queries, k) * scaling, FAR) for k, m in zip(keys, masks)]
    highest = scores[0].max(axis=1, keepdims=True)
    for s in scores[1:]:
        highest = jnp.maximum(highest, s.max(axis=1, keepdims=True))
    weights = [jnp.where(m, jnp.exp(s - highest), 0.0) for s, m in zip(scores, masks)]
    totals = sum(w.sum(axis=1, keepdims=True) for w in weights)
    sums = sum(
        jnp.dot(w.astype(jnp.bfloat16), v, preferred_element_type=jnp.float32)
        for w, v in zip(weights, values)
    )
    return sums / totals


def attend(queries, caches, fresh_ref, lengths_ref, out_ref, steps, head, per):
    rows = queries.shape[0]
    requests = rows // steps
    heads = queries.shape[1] // head
    scaling = 1.0 / math.sqrt(head)
    take = per * steps
    for b in range(requests // per):
        part = queries[b * take : (b + 1) * take, :]
        stacked = jnp.concatenate([part[:, h * head : (h + 1) * head] for h in range(heads)], axis=0)
        limit = jnp.concatenate([lengths_ref[b * take : (b + 1) * take, :]] * heads, axis=0)
        keys, values, masks = [], [], []
        for c, cache_ref in enumerate(caches):
            count = cache_ref.shape[0] // requests
            block = cache_ref[b * per * count : (b + 1) * per * count, :]
            shape = (heads * take, per * count)
            request = lax.rem(lax.broadcasted_iota(jnp.int32, shape, 0), take) // steps
            column = lax.broadcasted_iota(jnp.int32, shape, 1)
            position = lax.rem(column, count) + c * count
            masks.append(jnp.logical_and(column // count == request, position < limit))
            keys.append(block[:, :head])
            values.append(block[:, head:])
        block = fresh_ref[b * take : (b + 1) * take, :]
        shape = (heads * take, take)
        row = lax.rem(lax.broadcasted_iota(jnp.int32, shape, 0), take)
        column = lax.broadcasted_iota(jnp.int32, shape, 1)
        masks.append(jnp.logical_and(row // steps == column // steps, column <= row))
        keys.append(block[:, :head])
        values.append(block[:, head:])
        mixed = attend_block(stacked, keys, values, masks, scaling).astype(jnp.bfloat16)
        for h in range(heads):
            out_ref[b * take : (b + 1) * take, h * head : (h + 1) * head] = mixed[
                h * take : (h + 1) * take, :
            ]


def finish_kernel(
    steps, per, where_ref, own_ref, other_ref, beside_ref, across_ref, both_ref,
    holder_ref, up_ref, low_ref, high_ref, fresh_ref, lengths_ref, out_ref,
):
    rows = own_ref.shape[1]
    x, part = where_ref[0], where_ref[1]
    width = 128
    half = width // 2
    own = own_ref[0] + other_ref[0]
    beside, across, both = beside_ref[...], across_ref[...], both_ref[...]
    queries_here = part == 0
    columns = jnp.where(queries_here, own, across), jnp.where(queries_here, beside, both)
    ranks = jnp.where(queries_here, across, own), jnp.where(queries_here, both, beside)
    low_lanes = lax.broadcasted_iota(jnp.int32, (rows, width), 1) < half
    even = jnp.where(x == 0, columns[0], columns[1])
    odd = jnp.where(x == 0, columns[1], columns[0])

    def spaced(wide):
        out = []
        for j in range(4):
            pair = wide[:, (j // 2) * width : (j // 2 + 1) * width]
            out.append((pair, pltpu.roll(pair, half, 1)) if j % 2 == 0 else (pltpu.roll(pair, half, 1), pair))
        return out

    even, odd = spaced(even), spaced(odd)
    merged = [jnp.where(low_lanes, e[0], o[1]) for e, o in zip(even, odd)]
    groups = []
    for k in range(4):
        group = merged[3]
        for j in range(3):
            group = jnp.where(where_ref[2 + j] == 2 * k + x, merged[j], group)
        groups.append(group)
    base = jnp.concatenate(groups, axis=1)
    holder = holder_ref[...]
    spread = []
    for m in range(4):
        lane_owner = jnp.where(low_lanes, where_ref[2 + 2 * m], where_ref[3 + 2 * m])
        shrink = ranks[m // 2][:, (m % 2) * width : (m % 2 + 1) * width]
        spread.append(jnp.where(holder == lane_owner, shrink, 0.0).astype(jnp.bfloat16))
    adapted = jnp.dot(
        jnp.concatenate(spread, axis=1), up_ref[...], preferred_element_type=jnp.float32
    )
    queries = (base + adapted).astype(jnp.bfloat16)
    out_ref[0] = queries
    head = fresh_ref.shape[1] // 2
    attend(
        queries, (low_ref, high_ref), fresh_ref, lengths_ref, out_ref.at[1], steps, head, per
    )


def finish(steps, where, *arrays):
    rows, up = arrays[0].shape[1], arrays[6]
    vmem = pl.BlockSpec(memory_space=pltpu.VMEM)
    return pl.pallas_call(
        functools.partial(finish_kernel, steps, 8),
        out_shape=jax.ShapeDtypeStruct((2, rows, up.shape[1]), jnp.bfloat16),
        in_specs=[pl.BlockSpec(memory_space=pltpu.SMEM)] + [vmem] * len(arrays),
        out_specs=vmem,
        compiler_params=pltpu.CompilerParams(vmem_limit_bytes=16 << 20),
    )(where, *arrays)


def attend_kernel(steps, per, q_ref, low_ref, high_ref, fresh_ref, lengths_ref, out_ref):
    head = fresh_ref.shape[1] // 2
    attend(q_ref[...], (low_ref, high_ref), fresh_ref, lengths_ref, out_ref, steps, head, per)


def line_pairs(groups, moves):
    return [(a * 2 + x, b * 2 + x) for a, b in moves for x in range(2)]


def holders_of(request_adapter, adapter_owner):
    ids = jnp.arange(adapter_owner.shape[0], dtype=jnp.int32)
    lookup = request_adapter[:, None] == ids[None, :]
    return jnp.sum(jnp.where(lookup, adapter_owner[None, :], 0), axis=1)


def body(
    normed_hidden_states,
    query_matrix,
    factor_down,
    factor_up,
    kv_cache,
    incoming_key_value,
    kv_lengths,
    request_adapter,
    adapter_owner,
):
    groups = lax.axis_size("group")
    core = lax.axis_index("tensor")
    requests, steps, features = normed_hidden_states.shape
    rows = requests * steps
    holder = holders_of(request_adapter, adapter_owner)

    down = factor_down[0].T
    down_other = lax.ppermute(factor_down, "tensor", SWAP)[0].T
    mine_down = lax.dynamic_slice_in_dim(down, core * features, features, 1)
    other_down = lax.dynamic_slice_in_dim(down_other, core * features, features, 1)
    down_block = jnp.where(
        core == 0,
        jnp.concatenate([mine_down, other_down], 0),
        jnp.concatenate([other_down, mine_down], 0),
    )
    query_block = query_matrix.T
    width = query_matrix.shape[1] * groups
    out_shape = (requests, steps, width)

    if groups == 8 and lax.axis_size("parts") == 2 and query_block.shape == down_block.shape:
        place = lax.axis_index("group")
        z, x, part = place // 2, lax.rem(place, 2), lax.axis_index("parts")
        pair_low = z < 2
        places = (z, z + 1 - 2 * lax.rem(z, 2), jnp.where(pair_low, 2, 1), jnp.where(pair_low, 3, 0))
        where = [x, part] + [p * 2 + x for p in places] + [p * 2 + 1 - x for p in places]
        where = jnp.stack(where).astype(jnp.int32)
        middle = jnp.logical_or(z == 1, z == 2)
        bar = lambda *a: lax.optimization_barrier(a)
        along = lambda a, moves: lax.ppermute(a, "group", line_pairs(groups, moves))
        across = lambda a: lax.ppermute(a, "parts", SWAP)
        beside = lambda a: lax.ppermute(a, "group", [(i, i ^ 1) for i in range(groups)])
        corner = [(p * groups + i, (1 - p) * groups + (i ^ 1)) for p in range(2) for i in range(groups)]
        ends, inner = ((0, 1), (1, 0), (2, 3), (3, 2)), ((1, 2), (2, 1))
        outward = ((1, 0), (2, 3))
        mid, at = requests // 2, rows // 2

        w0 = jnp.where(part == 0, query_block, down_block)
        hidden = normed_hidden_states.reshape(rows, features)
        h0, h1 = hidden[:at], hidden[at:]
        w1, m1 = along(w0, ends), along(w0, inner)
        b1, a0 = beside(h1), across(h0)
        up_pair = along(factor_up[0], ends)
        w1, m1, b1, a0 = bar(w1, m1, b1, a0)
        m2, p1 = along(w1, inner), along(m1, outward)
        c0, c1 = beside(a0), across(b1)
        b0, a1 = beside(h0), across(h1)
        up_two = jnp.concatenate([factor_up[0], up_pair], axis=0)
        up_far = along(up_two, inner)
        w2 = jnp.where(middle, m1, p1)
        m2, p1, c0, c1, up_far = bar(m2, p1, c0, c1, up_far)
        p2 = along(m2, outward)
        up_far = jnp.where(middle, up_far, along(up_far, outward))
        w3 = jnp.where(middle, m2, p2)
        up_four = jnp.concatenate([up_two, up_far], axis=0)
        up_all = jnp.concatenate([up_four, beside(up_four)], axis=0)
        up_other = lax.ppermute(up_all, "tensor", SWAP)
        up_full = jnp.where(
            core == 0,
            jnp.concatenate([up_all, up_other], 1),
            jnp.concatenate([up_other, up_all], 1),
        )
        known = h0, h1, b1, a0, c0, c1
        t = first_products(known, w0, w1, w2)

        half = lambda a, k: lax.dynamic_slice_in_dim(a, k * mid, mid, 0)
        cache, given = half(kv_cache, core), half(kv_cache, 1 - core)
        got_cache = lax.ppermute(given, "tensor", SWAP)
        low = jnp.where(core == 0, cache, got_cache).reshape(-1, kv_cache.shape[2])
        high = jnp.where(core == 0, got_cache, cache).reshape(-1, kv_cache.shape[2])
        spread_rows = lambda a: jnp.repeat(half(a, core), steps)[:, None]
        fresh = half(incoming_key_value, core).reshape(rows // 2, -1)
        holder_rows, lengths_rows = spread_rows(holder), spread_rows(kv_lengths)
        p2, b0, a1, t, low, high, fresh, holder_rows, lengths_rows = bar(
            p2, b0, a1, t, low, high, fresh, holder_rows, lengths_rows
        )
        w3 = jnp.where(middle, m2, p2)
        core_at = jnp.reshape(core, (1,)).astype(jnp.int32)
        kept, given = last_products(core_at, known, (b0, a1), (w0, w1, w2, w3), t)
        got = lax.ppermute(given, "tensor", SWAP)
        t_beside, t_across, t_both = add_halves(kept, got)
        t_beside, t_across = beside(t_beside), across(t_across)
        t_both = lax.ppermute(t_both, ("parts", "group"), corner)
        done = finish(
            steps, where, kept, got, t_beside, t_across, t_both,
            holder_rows, up_full, low, high, fresh, lengths_rows,
        )
        done_other = lax.ppermute(done, "tensor", SWAP)
        outs = jnp.where(
            core == 0,
            jnp.concatenate([done, done_other], 1),
            jnp.concatenate([done_other, done], 1),
        )
        return outs[0].reshape(out_shape), outs[1].reshape(out_shape)

    holder_rows = jnp.repeat(holder, steps)[:, None]
    lengths_rows = jnp.repeat(kv_lengths, steps)[:, None]
    own = normed_hidden_states.reshape(rows, features)
    other_cache = lax.ppermute(kv_cache, "tensor", SWAP)
    low = jnp.where(core == 0, kv_cache, other_cache).reshape(-1, kv_cache.shape[2])
    high = jnp.where(core == 0, other_cache, kv_cache).reshape(-1, kv_cache.shape[2])
    fresh = incoming_key_value.reshape(rows, -1)
    up = lax.all_gather(factor_up[0], "group", axis=0, tiled=True)
    up_other = lax.ppermute(up, "tensor", SWAP)
    up_full = jnp.where(
        core == 0, jnp.concatenate([up, up_other], 1), jnp.concatenate([up_other, up], 1)
    )

    place = lax.axis_index("group")
    ring = [(i, (i + 1) % groups) for i in range(groups)]

    def step(k, carry):
        q_part, d_part, base, shrink = carry
        at = lax.rem(place - k + groups, groups)
        base = lax.dynamic_update_slice_in_dim(base, nt_dot(own, q_part), at * q_part.shape[0], 1)
        shrink = shrink + jnp.where(holder_rows == at, nt_dot(own, d_part), 0.0)
        q_part, d_part = (lax.ppermute(w, "group", ring) for w in (q_part, d_part))
        return q_part, d_part, base, shrink

    start = (
        query_block,
        down_block,
        jnp.zeros((rows, width), jnp.float32),
        jnp.zeros((rows, down_block.shape[0]), jnp.float32),
    )
    _, _, base, shrink = lax.fori_loop(0, groups, step, start)
    base = base + lax.ppermute(base, "tensor", SWAP)
    shrink = (shrink + lax.ppermute(shrink, "tensor", SWAP)).astype(jnp.bfloat16)
    named = holder_rows == jnp.arange(groups, dtype=jnp.int32)[None, :]
    spread = jnp.where(named[:, :, None], shrink[:, None, :], 0).reshape(rows, -1)
    adapted = jnp.dot(spread, up_full, preferred_element_type=jnp.float32)
    queries = (base + adapted).astype(jnp.bfloat16)
    attended = pl.pallas_call(
        functools.partial(attend_kernel, steps, 8),
        out_shape=jax.ShapeDtypeStruct(queries.shape, jnp.bfloat16),
        compiler_params=pltpu.CompilerParams(vmem_limit_bytes=24 << 20),
    )(queries, low, high, fresh, lengths_rows)
    return queries.reshape(out_shape), attended.reshape(out_shape)


def solution(mesh):
    placed = (
        P(("parts", "group"), None, "tensor"),
        P("tensor", "group"),
        P("group", None, "tensor"),
        P("group", None, "tensor"),
        P(("parts", "group"), "tensor", None),
        P(("parts", "group"), None, None),
        P(("parts", "group")),
        P(("parts", "group")),
        P("parts"),
    )
    return jax.shard_map(
        body,
        mesh=mesh,
        in_specs=placed,
        out_specs=(P(("parts", "group"), None, None), P(("parts", "group"), None, None)),
        check_vma=False,
    )
```

```python
import functools
import math

import jax
import jax.numpy as jnp
from jax import lax
from jax.experimental import pallas as pl
from jax.experimental.pallas import tpu as pltpu
from jax.sharding import PartitionSpec as P

SWAP = [(0, 1), (1, 0)]
FAR = -1e30
PER = 8


def nt_dot(a, b):
    return lax.dot_general(a, b, (((1,), (1,)), ((), ())), preferred_element_type=jnp.float32)


def copy_all(copies, sems):
    started = [pltpu.make_async_copy(source, target, sems.at[k]) for k, (source, target) in enumerate(copies)]
    for copy in started:
        copy.start()
    for copy in started:
        copy.wait()


def block_kernel(where_ref, query_ref, kept_ref, given_ref, up_ref, out_ref, sems):
    part, core = where_ref[2], where_ref[3]
    count, features = kept_ref.shape[0], query_ref.shape[1]
    up = (up_ref, out_ref.at[:, features:])
    top, bottom = out_ref.at[:count, :features], out_ref.at[count:, :features]

    @pl.when(part == 0)
    def _():
        copy_all([(query_ref, out_ref.at[:, :features]), up], sems)

    @pl.when(jnp.logical_and(part != 0, core == 0))
    def _():
        low = slice(0, features)
        copy_all([(kept_ref.at[:, low], top), (given_ref.at[:, low], bottom), up], sems)

    @pl.when(jnp.logical_and(part != 0, core != 0))
    def _():
        high = slice(features, 2 * features)
        copy_all([(given_ref.at[:, high], top), (kept_ref.at[:, high], bottom), up], sems)


def block_of(where, query, kept, given, up):
    return pl.pallas_call(
        block_kernel,
        out_shape=jax.ShapeDtypeStruct((query.shape[0], query.shape[1] + up.shape[1]), query.dtype),
        in_specs=[pl.BlockSpec(memory_space=pltpu.SMEM)] + [pl.BlockSpec(memory_space=pl.ANY)] * 4,
        out_specs=pl.BlockSpec(memory_space=pltpu.VMEM),
        scratch_shapes=[pltpu.SemaphoreType.DMA((3,))],
        compiler_params=pltpu.CompilerParams(vmem_limit_bytes=2 << 20),
    )(where, query, kept, given, up)


def rows_kernel(x_ref, out_ref):
    out_ref[...] = x_ref[...].reshape(out_ref.shape)


def rows_of(x):
    return pl.pallas_call(
        rows_kernel,
        out_shape=jax.ShapeDtypeStruct((x.shape[0] * x.shape[1], x.shape[2]), x.dtype),
        compiler_params=pltpu.CompilerParams(vmem_limit_bytes=4 << 20),
    )(x)


def ready_kernel(
    where_ref, lengths_ref, adapter_ref, owner_ref, mine_ref, other_ref, fresh_ref,
    low_ref, high_ref, new_ref, limits_ref, holder_ref, sems,
):
    core = where_ref[3]
    half = new_ref.shape[0]
    requests = lengths_ref.shape[0] // 2
    steps = half // requests
    many = low_ref.shape[0]
    for k, (low, high) in enumerate(((mine_ref, other_ref), (other_ref, mine_ref))):

        @pl.when(core == k)
        def _():
            rows = slice(k * many, (k + 1) * many)
            copy_all([(low.at[rows], low_ref), (high.at[rows], high_ref)], sems)
            new_ref[...] = fresh_ref[k * requests : (k + 1) * requests].reshape(new_ref.shape)

    first = core * requests
    per = limits_ref.shape[1] // (many // requests)
    column = lax.broadcasted_iota(jnp.int32, (1, limits_ref.shape[1]), 1) // (many // requests)
    for b in range(requests // per):
        limit = jnp.zeros(column.shape, jnp.int32)
        for r in range(per):
            limit = jnp.where(column == r, lengths_ref[first + b * per + r], limit)
        limits_ref[b : b + 1, :] = limit
    row = lax.broadcasted_iota(jnp.int32, holder_ref.shape, 0) // steps
    holder = jnp.zeros(holder_ref.shape, jnp.int32)
    for r in range(requests):
        holder = jnp.where(row == r, owner_ref[adapter_ref[first + r]], holder)
    holder_ref[...] = holder


def ready(where, lengths, adapter, owner, mine, other, fresh, steps):
    requests, count = lengths.shape[0] // 2, mine.shape[0] // lengths.shape[0]
    smem, vmem = (pl.BlockSpec(memory_space=m) for m in (pltpu.SMEM, pltpu.VMEM))
    anywhere = pl.BlockSpec(memory_space=pl.ANY)
    cache = jax.ShapeDtypeStruct((requests * count, mine.shape[1]), mine.dtype)
    return pl.pallas_call(
        ready_kernel,
        out_shape=(
            cache,
            cache,
            jax.ShapeDtypeStruct((requests * steps, fresh.shape[2]), fresh.dtype),
            jax.ShapeDtypeStruct((8, PER * count), jnp.int32),
            jax.ShapeDtypeStruct((requests * steps, 128), jnp.int32),
        ),
        in_specs=[smem] * 4 + [anywhere] * 2 + [vmem],
        out_specs=(vmem,) * 5,
        scratch_shapes=[pltpu.SemaphoreType.DMA((2,))],
        compiler_params=pltpu.CompilerParams(vmem_limit_bytes=4 << 20),
    )(where, lengths, adapter, owner, mine, other, fresh)


def products_kernel(sets, *refs):
    rows, weights, out_ref = refs[:sets], refs[sets:-1], refs[-1]
    features = rows[0].shape[1]
    columns = jnp.concatenate([w[:, :features] for w in weights], axis=0)
    out_ref[...] = nt_dot(jnp.concatenate([r[...] for r in rows], axis=0), columns)


def products(sets, weights):
    rows, columns = sum(r.shape[0] for r in sets), sum(w.shape[0] for w in weights)
    return pl.pallas_call(
        functools.partial(products_kernel, len(sets)),
        out_shape=jax.ShapeDtypeStruct((rows, columns), jnp.float32),
        cost_estimate=pl.CostEstimate(
            flops=2 * rows * columns * sets[0].shape[1],
            bytes_accessed=(rows + columns) * sets[0].shape[1] * 2,
            transcendentals=0,
        ),
        compiler_params=pltpu.CompilerParams(vmem_limit_bytes=12 << 20),
    )(*sets, *weights)


def last_kernel(where_ref, *refs):
    *sets, w_ref, near_up_ref, t_ref, late_ref, kept_ref, given_ref = refs
    features, half = sets[0].shape[1], kept_ref.shape[1]
    before = t_ref.shape[1] - w_ref.shape[0]
    middle = jnp.logical_or(where_ref[0] == 1, where_ref[0] == 2)
    total = nt_dot(jnp.concatenate([r[...] for r in sets], axis=0), w_ref[:, :features])
    first = where_ref[3] == 0
    known = t_ref.shape[0] // half

    def value(k):
        ref, at = (t_ref, k) if k < known else (late_ref, k - known)
        rows = ref[at * half : (at + 1) * half, :]
        last = jnp.where(middle, rows[:, before:], total[k * half : (k + 1) * half])
        return jnp.concatenate([rows[:, :before], last], axis=1)

    up = jnp.where(middle, near_up_ref[...], w_ref[:, features:])
    given_ref[4] = up.astype(jnp.float32)
    for k in range(4):
        low, high = value(2 * k), value(2 * k + 1)
        kept_ref[k] = jnp.where(first, low, high)
        given_ref[k] = jnp.where(first, high, low)


def last_products(where, sets, w, near_up, t, late):
    smem, vmem = (pl.BlockSpec(memory_space=m) for m in (pltpu.SMEM, pltpu.VMEM))
    shape = (4, sets[0].shape[0] // 2, t.shape[1])
    return pl.pallas_call(
        last_kernel,
        out_shape=(
            jax.ShapeDtypeStruct(shape, jnp.float32),
            jax.ShapeDtypeStruct((5,) + shape[1:], jnp.float32),
        ),
        in_specs=[smem] + [vmem] * (len(sets) + 4),
        out_specs=(vmem, vmem),
        compiler_params=pltpu.CompilerParams(vmem_limit_bytes=12 << 20),
    )(where, *sets, w, near_up, t, late)


def join_kernel(where_ref, mine_ref, other_ref, queries_ref, attended_ref, sems):
    core = where_ref[3]
    count = mine_ref.shape[1]
    mine, other = pl.ds(core * count, count), pl.ds((1 - core) * count, count)
    copy_all(
        [
            (mine_ref.at[0], queries_ref.at[mine]), (mine_ref.at[1], attended_ref.at[mine]),
            (other_ref.at[0], queries_ref.at[other]), (other_ref.at[1], attended_ref.at[other]),
        ],
        sems,
    )


def join(where, mine, other):
    anywhere = pl.BlockSpec(memory_space=pl.ANY)
    shape = jax.ShapeDtypeStruct((2 * mine.shape[1],) + mine.shape[2:], mine.dtype)
    return pl.pallas_call(
        join_kernel,
        out_shape=(shape, shape),
        in_specs=[pl.BlockSpec(memory_space=pltpu.SMEM), anywhere, anywhere],
        out_specs=(anywhere, anywhere),
        scratch_shapes=[pltpu.SemaphoreType.DMA((4,))],
        compiler_params=pltpu.CompilerParams(vmem_limit_bytes=2 << 20),
    )(where, mine, other)


def add_kernel(where_ref, kept_ref, given_ref, got_ref, beside_ref, across_ref, both_ref):
    half = kept_ref.shape[1]
    first = where_ref[3] == 0
    mine, other = given_ref[4], got_ref[4]
    beside_ref[:half] = kept_ref[1] + got_ref[1]
    beside_ref[half : 2 * half] = jnp.where(first, mine, other)
    beside_ref[2 * half :] = jnp.where(first, other, mine)
    across_ref[...] = kept_ref[2] + got_ref[2]
    both_ref[...] = kept_ref[3] + got_ref[3]


def add_halves(where, kept, given, got):
    rows, columns = kept.shape[1:]
    smem, vmem = (pl.BlockSpec(memory_space=m) for m in (pltpu.SMEM, pltpu.VMEM))
    shape = jax.ShapeDtypeStruct((rows, columns), kept.dtype)
    return pl.pallas_call(
        add_kernel,
        out_shape=(jax.ShapeDtypeStruct((3 * rows, columns), kept.dtype), shape, shape),
        in_specs=[smem] + [vmem] * 3,
        out_specs=(vmem,) * 3,
        compiler_params=pltpu.CompilerParams(vmem_limit_bytes=2 << 20),
    )(where, kept, given, got)


def attend_block(queries, keys, values, masks, scaling):
    scores = [jnp.where(m, nt_dot(queries, k) * scaling, FAR) for k, m in zip(keys, masks)]
    highest = scores[0].max(axis=1, keepdims=True)
    for s in scores[1:]:
        highest = jnp.maximum(highest, s.max(axis=1, keepdims=True))
    weights = [jnp.where(m, jnp.exp(s - highest), 0.0) for s, m in zip(scores, masks)]
    totals = sum(w.sum(axis=1, keepdims=True) for w in weights)
    sums = sum(
        jnp.dot(w.astype(jnp.bfloat16), v, preferred_element_type=jnp.float32)
        for w, v in zip(weights, values)
    )
    return sums / totals


def attend(queries, caches, fresh_ref, limit_of, put, steps, head, per):
    rows = queries.shape[0]
    requests = rows // steps
    heads = queries.shape[1] // head
    scaling = 1.0 / math.sqrt(head)
    take = per * steps
    for b in range(requests // per):
        part = queries[b * take : (b + 1) * take, :]
        stacked = jnp.concatenate([part[:, h * head : (h + 1) * head] for h in range(heads)], axis=0)
        limit = limit_of(b)
        keys, values, masks = [], [], []
        for c, cache_ref in enumerate(caches):
            count = cache_ref.shape[0] // requests
            block = cache_ref[b * per * count : (b + 1) * per * count, :]
            shape = (heads * take, per * count)
            request = lax.rem(lax.broadcasted_iota(jnp.int32, shape, 0), take) // steps
            column = lax.broadcasted_iota(jnp.int32, shape, 1)
            position = lax.rem(column, count) + c * count
            masks.append(jnp.logical_and(column // count == request, position < limit))
            keys.append(block[:, :head])
            values.append(block[:, head:])
        block = fresh_ref[b * take : (b + 1) * take, :]
        shape = (heads * take, take)
        row = lax.rem(lax.broadcasted_iota(jnp.int32, shape, 0), take)
        column = lax.broadcasted_iota(jnp.int32, shape, 1)
        masks.append(jnp.logical_and(row // steps == column // steps, column <= row))
        keys.append(block[:, :head])
        values.append(block[:, head:])
        mixed = attend_block(stacked, keys, values, masks, scaling).astype(jnp.bfloat16)
        put(
            b,
            jnp.concatenate([mixed[h * take : (h + 1) * take] for h in range(heads)], axis=1),
        )


def finish_kernel(
    steps, where_ref, own_ref, other_ref, sent_ref, beside_ref, across_ref, both_ref, holder_ref,
    up_ref, up_beside_ref, up_other_ref, up_both_ref, low_ref, high_ref, fresh_ref, limits_ref, out_ref,
):
    rows = own_ref.shape[1]
    x, part = where_ref[1], where_ref[2]
    width = 128
    half = width // 2
    own = own_ref[0] + other_ref[0]
    beside, across, both = beside_ref[:rows], across_ref[...], both_ref[...]
    queries_here = part == 0
    columns = jnp.where(queries_here, own, across), jnp.where(queries_here, beside, both)
    ranks = jnp.where(queries_here, across, own), jnp.where(queries_here, both, beside)
    low_lanes = lax.broadcasted_iota(jnp.int32, (rows, width), 1) < half
    even = jnp.where(x == 0, columns[0], columns[1])
    odd = jnp.where(x == 0, columns[1], columns[0])

    def spaced(wide):
        out = []
        for j in range(4):
            pair = wide[:, (j // 2) * width : (j // 2 + 1) * width]
            out.append((pair, pltpu.roll(pair, half, 1)) if j % 2 == 0 else (pltpu.roll(pair, half, 1), pair))
        return out

    even, odd = spaced(even), spaced(odd)
    merged = [jnp.where(low_lanes, e[0], o[1]) for e, o in zip(even, odd)]
    groups = []
    for k in range(4):
        group = merged[3]
        for j in range(3):
            group = jnp.where(where_ref[4 + j] == 2 * k + x, merged[j], group)
        groups.append(group)
    base = jnp.concatenate(groups, axis=1)
    holder = holder_ref[...]
    spread = []
    for m in range(4):
        lane_owner = jnp.where(low_lanes, where_ref[4 + 2 * m], where_ref[5 + 2 * m])
        shrink = ranks[m // 2][:, (m % 2) * width : (m % 2 + 1) * width]
        spread.append(jnp.where(holder == lane_owner, shrink, 0.0).astype(jnp.bfloat16))
    spread = [jnp.concatenate(spread[:2], axis=1), jnp.concatenate(spread[2:], axis=1)]

    first = where_ref[3] == 0

    def lift(side, a_ref, b_ref, last_ref):
        a, b = a_ref[: 3 * half], b_ref[: 3 * half]
        low = jnp.where(first, a, b), last_ref[rows : 2 * rows].astype(a.dtype)
        high = jnp.where(first, b, a), last_ref[2 * rows :].astype(a.dtype)
        up = jnp.concatenate([jnp.concatenate(low, axis=0), jnp.concatenate(high, axis=0)], axis=1)
        return jnp.dot(side, up, preferred_element_type=jnp.float32)

    adapted = lift(spread[0], up_ref, up_other_ref, sent_ref) + lift(
        spread[1], up_beside_ref, up_both_ref, beside_ref
    )
    queries = (base + adapted).astype(jnp.bfloat16)
    requests = rows // steps
    out_ref[0] = queries.reshape(requests, steps, -1)
    head = fresh_ref.shape[1] // 2

    def put(b, mixed):
        out_ref[1, b * PER : (b + 1) * PER] = mixed.reshape(PER, steps, -1)

    attend(
        queries, (low_ref, high_ref), fresh_ref, lambda b: limits_ref[b : b + 1, :], put, steps, head, PER
    )


def finish(steps, where, *arrays):
    rows, columns = arrays[0].shape[1:]
    vmem = pl.BlockSpec(memory_space=pltpu.VMEM)
    return pl.pallas_call(
        functools.partial(finish_kernel, steps),
        out_shape=jax.ShapeDtypeStruct((2, rows // steps, steps, 2 * columns), jnp.bfloat16),
        in_specs=[pl.BlockSpec(memory_space=pltpu.SMEM)] + [vmem] * len(arrays),
        out_specs=vmem,
        compiler_params=pltpu.CompilerParams(vmem_limit_bytes=8 << 20),
    )(where, *arrays)


def attend_kernel(steps, q_ref, low_ref, high_ref, fresh_ref, limits_ref, out_ref):
    head = fresh_ref.shape[1] // 2
    take = PER * steps

    def put(b, mixed):
        out_ref[b * take : (b + 1) * take, :] = mixed

    attend(
        q_ref[...], (low_ref, high_ref), fresh_ref, lambda b: limits_ref[b : b + 1, :], put, steps, head, PER
    )


def line_pairs(groups, moves):
    return [(a * 2 + x, b * 2 + x) for a, b in moves for x in range(2)]


def holders_of(request_adapter, adapter_owner):
    ids = jnp.arange(adapter_owner.shape[0], dtype=jnp.int32)
    lookup = request_adapter[:, None] == ids[None, :]
    return jnp.sum(jnp.where(lookup, adapter_owner[None, :], 0), axis=1)


def body(
    normed_hidden_states,
    query_matrix,
    factor_down,
    factor_up,
    kv_cache,
    incoming_key_value,
    kv_lengths,
    request_adapter,
    adapter_owner,
):
    groups = lax.axis_size("group")
    core = lax.axis_index("tensor")
    requests, steps, features = normed_hidden_states.shape
    rows = requests * steps

    down = factor_down[0].T
    down_other = lax.ppermute(factor_down, "tensor", SWAP)[0].T
    query_block = query_matrix.T
    width = query_matrix.shape[1] * groups
    out_shape = (requests, steps, width)

    if groups == 8 and lax.axis_size("parts") == 2 and query_matrix.shape[1] == 2 * down.shape[0]:
        place = lax.axis_index("group")
        z, x, part = place // 2, lax.rem(place, 2), lax.axis_index("parts")
        pair_low = z < 2
        places = (z, z + 1 - 2 * lax.rem(z, 2), jnp.where(pair_low, 2, 1), jnp.where(pair_low, 3, 0))
        where = [z, x, part, core] + [p * 2 + x for p in places] + [p * 2 + 1 - x for p in places]
        where = jnp.stack(where).astype(jnp.int32)
        middle = jnp.logical_or(z == 1, z == 2)
        bar = lambda *a: lax.optimization_barrier(a)
        along = lambda a, moves: lax.ppermute(a, "group", line_pairs(groups, moves))
        across = lambda a: lax.ppermute(a, "parts", SWAP)
        beside = lambda a: lax.ppermute(a, "group", [(i, i ^ 1) for i in range(groups)])
        inside = lambda a: lax.ppermute(a, "tensor", SWAP)
        corner = [(p * groups + i, (1 - p) * groups + (i ^ 1)) for p in range(2) for i in range(groups)]
        ends, inner = ((0, 1), (1, 0), (2, 3), (3, 2)), ((1, 2), (2, 1))
        outward = ((1, 0), (2, 3))

        mine = rows_of(normed_hidden_states)
        w0 = block_of(where, query_block, down, down_other, factor_up[0])
        w0, mine = bar(w0, mine)
        half = rows // 2
        m1, w1 = along(w0, inner), along(w0, ends)
        x_beside, x_across = beside(mine), across(mine)
        m2, p1 = along(w1, inner), along(m1, outward)
        w2 = jnp.where(middle, m1, p1)
        c0, c1 = beside(x_across[:half]), across(x_beside[half:])
        m2, p1, x_beside, x_across = bar(m2, p1, x_beside, x_across)
        p2 = along(m2, outward)
        up = jnp.concatenate([w[:, features:] for w in (w0, w1, w2)], axis=0)
        up_beside = beside(up)
        ups = up, up_beside, inside(up), inside(up_beside)
        near_up = m2[:, features:]
        sets, later = (mine, x_beside, x_across), (c0, c1)
        weights = w0, w1, w2, m2
        t, t_late = products(sets, weights), products(later, weights)

        cache = kv_cache.reshape(-1, kv_cache.shape[2])
        prepared = ready(
            where, kv_lengths, request_adapter, adapter_owner, cache, inside(cache), incoming_key_value, steps
        )
        p2, t, t_late, prepared, ups, near_up = bar(p2, t, t_late, prepared, ups, near_up)
        kept, given = last_products(where, sets + later, p2, near_up, t, t_late)
        got = inside(given)
        sent, t_across, t_both = add_halves(where, kept, given, got)
        t_beside, t_across = beside(sent), across(t_across)
        t_both = lax.ppermute(t_both, ("parts", "group"), corner)
        low, high, fresh, limits, holder_rows = prepared
        done = finish(
            steps, where, kept, got, sent, t_beside, t_across, t_both, holder_rows, *ups, low, high, fresh, limits
        )
        return join(where, done, inside(done))

    mine_down = lax.dynamic_slice_in_dim(down, core * features, features, 1)
    other_down = lax.dynamic_slice_in_dim(down_other, core * features, features, 1)
    down_block = jnp.where(
        core == 0,
        jnp.concatenate([mine_down, other_down], 0),
        jnp.concatenate([other_down, mine_down], 0),
    )
    holder = holders_of(request_adapter, adapter_owner)
    holder_rows = jnp.repeat(holder, steps)[:, None]
    limits = jnp.repeat(kv_lengths, kv_cache.shape[1]).reshape(requests // PER, -1)
    own = normed_hidden_states.reshape(rows, features)
    other_cache = lax.ppermute(kv_cache, "tensor", SWAP)
    low = jnp.where(core == 0, kv_cache, other_cache).reshape(-1, kv_cache.shape[2])
    high = jnp.where(core == 0, other_cache, kv_cache).reshape(-1, kv_cache.shape[2])
    fresh = incoming_key_value.reshape(rows, -1)
    up = lax.all_gather(factor_up[0], "group", axis=0, tiled=True)
    up_other = lax.ppermute(up, "tensor", SWAP)
    up_full = jnp.where(
        core == 0, jnp.concatenate([up, up_other], 1), jnp.concatenate([up_other, up], 1)
    )

    place = lax.axis_index("group")
    ring = [(i, (i + 1) % groups) for i in range(groups)]

    def step(k, carry):
        q_part, d_part, base, shrink = carry
        at = lax.rem(place - k + groups, groups)
        base = lax.dynamic_update_slice_in_dim(base, nt_dot(own, q_part), at * q_part.shape[0], 1)
        shrink = shrink + jnp.where(holder_rows == at, nt_dot(own, d_part), 0.0)
        q_part, d_part = (lax.ppermute(w, "group", ring) for w in (q_part, d_part))
        return q_part, d_part, base, shrink

    start = (
        query_block,
        down_block,
        jnp.zeros((rows, width), jnp.float32),
        jnp.zeros((rows, down_block.shape[0]), jnp.float32),
    )
    _, _, base, shrink = lax.fori_loop(0, groups, step, start)
    base = base + lax.ppermute(base, "tensor", SWAP)
    shrink = (shrink + lax.ppermute(shrink, "tensor", SWAP)).astype(jnp.bfloat16)
    named = holder_rows == jnp.arange(groups, dtype=jnp.int32)[None, :]
    spread = jnp.where(named[:, :, None], shrink[:, None, :], 0).reshape(rows, -1)
    adapted = jnp.dot(spread, up_full, preferred_element_type=jnp.float32)
    queries = (base + adapted).astype(jnp.bfloat16)
    attended = pl.pallas_call(
        functools.partial(attend_kernel, steps),
        out_shape=jax.ShapeDtypeStruct(queries.shape, jnp.bfloat16),
        compiler_params=pltpu.CompilerParams(vmem_limit_bytes=24 << 20),
    )(queries, low, high, fresh, limits)
    return queries.reshape(out_shape), attended.reshape(out_shape)


def solution(mesh):
    placed = (
        P(("parts", "group"), None, "tensor"),
        P("tensor", "group"),
        P("group", None, "tensor"),
        P("group", None, "tensor"),
        P(("parts", "group"), "tensor", None),
        P(("parts", "group"), None, None),
        P(("parts", "group")),
        P(("parts", "group")),
        P("parts"),
    )
    return jax.shard_map(
        body,
        mesh=mesh,
        in_specs=placed,
        out_specs=(P(("parts", "group"), None, None), P(("parts", "group"), None, None)),
        check_vma=False,
    )
```

```python
import functools
import math

import jax
import jax.numpy as jnp
from jax import lax
from jax.experimental import pallas as pl
from jax.experimental.pallas import tpu as pltpu
from jax.sharding import PartitionSpec as P

SWAP = [(0, 1), (1, 0)]
FAR = -1e30
PER = 8


def nt_dot(a, b):
    return lax.dot_general(a, b, (((1,), (1,)), ((), ())), preferred_element_type=jnp.float32)


def copy_all(copies, sems):
    started = [pltpu.make_async_copy(source, target, sems.at[k]) for k, (source, target) in enumerate(copies)]
    for copy in started:
        copy.start()
    for copy in started:
        copy.wait()


def block_kernel(
    where_ref, query_ref, kept_ref, given_ref, up_ref, up_beside_ref, a_ref, b_ref, sems
):
    part, core = where_ref[2], where_ref[3]
    count, features = kept_ref.shape[0], query_ref.shape[1]
    columns = up_ref.shape[1]
    chunks = [ref.at[:, :features] for ref in (a_ref, b_ref)]
    ups = []
    for ref, source in ((a_ref, up_ref), (b_ref, up_beside_ref)):
        ups.append((source.at[:count], ref.at[:, features : features + columns]))
        ups.append((source.at[count:], ref.at[:, features + columns :]))

    @pl.when(part == 0)
    def _():
        copy_all([(query_ref.at[:count], chunks[0]), (query_ref.at[count:], chunks[1])] + ups, sems)

    @pl.when(jnp.logical_and(part != 0, core == 0))
    def _():
        low = slice(0, features)
        copy_all([(kept_ref.at[:, low], chunks[0]), (given_ref.at[:, low], chunks[1])] + ups, sems)

    @pl.when(jnp.logical_and(part != 0, core != 0))
    def _():
        high = slice(features, 2 * features)
        copy_all([(given_ref.at[:, high], chunks[0]), (kept_ref.at[:, high], chunks[1])] + ups, sems)


def block_of(where, query, kept, given, up, up_beside):
    count, features = kept.shape[0], query.shape[1]
    vmem = pl.BlockSpec(memory_space=pltpu.VMEM)
    shape = jax.ShapeDtypeStruct((count, features + 2 * up.shape[1]), query.dtype)
    return pl.pallas_call(
        block_kernel,
        out_shape=(shape, shape),
        in_specs=[pl.BlockSpec(memory_space=pltpu.SMEM)] + [pl.BlockSpec(memory_space=pl.ANY)] * 5,
        out_specs=(vmem, vmem),
        scratch_shapes=[pltpu.SemaphoreType.DMA((6,))],
        compiler_params=pltpu.CompilerParams(vmem_limit_bytes=2 << 20),
    )(where, query, kept, given, up, up_beside)


def rows_kernel(x_ref, out_ref):
    out_ref[...] = x_ref[...].reshape(out_ref.shape)


def rows_of(x):
    return pl.pallas_call(
        rows_kernel,
        out_shape=jax.ShapeDtypeStruct((x.shape[0] * x.shape[1], x.shape[2]), x.dtype),
        compiler_params=pltpu.CompilerParams(vmem_limit_bytes=4 << 20),
    )(x)


def ready_kernel(
    where_ref, lengths_ref, adapter_ref, owner_ref, mine_ref, other_ref, fresh_ref,
    low_ref, high_ref, new_ref, limits_ref, holder_ref, sems,
):
    core = where_ref[3]
    half = new_ref.shape[0]
    requests = lengths_ref.shape[0] // 2
    steps = half // requests
    many = low_ref.shape[0]
    for k, (low, high) in enumerate(((mine_ref, other_ref), (other_ref, mine_ref))):

        @pl.when(core == k)
        def _():
            rows = slice(k * many, (k + 1) * many)
            copy_all([(low.at[rows], low_ref), (high.at[rows], high_ref)], sems)
            new_ref[...] = fresh_ref[k * requests : (k + 1) * requests].reshape(new_ref.shape)

    first = core * requests
    per = limits_ref.shape[1] // (many // requests)
    column = lax.broadcasted_iota(jnp.int32, (1, limits_ref.shape[1]), 1) // (many // requests)
    for b in range(requests // per):
        limit = jnp.zeros(column.shape, jnp.int32)
        for r in range(per):
            limit = jnp.where(column == r, lengths_ref[first + b * per + r], limit)
        limits_ref[b : b + 1, :] = limit
    row = lax.broadcasted_iota(jnp.int32, holder_ref.shape, 0) // steps
    holder = jnp.zeros(holder_ref.shape, jnp.int32)
    for r in range(requests):
        holder = jnp.where(row == r, owner_ref[adapter_ref[first + r]], holder)
    holder_ref[...] = holder


def ready(where, lengths, adapter, owner, mine, other, fresh, steps):
    requests, count = lengths.shape[0] // 2, mine.shape[0] // lengths.shape[0]
    smem, vmem = (pl.BlockSpec(memory_space=m) for m in (pltpu.SMEM, pltpu.VMEM))
    anywhere = pl.BlockSpec(memory_space=pl.ANY)
    cache = jax.ShapeDtypeStruct((requests * count, mine.shape[1]), mine.dtype)
    return pl.pallas_call(
        ready_kernel,
        out_shape=(
            cache,
            cache,
            jax.ShapeDtypeStruct((requests * steps, fresh.shape[2]), fresh.dtype),
            jax.ShapeDtypeStruct((8, PER * count), jnp.int32),
            jax.ShapeDtypeStruct((requests * steps, 128), jnp.int32),
        ),
        in_specs=[smem] * 4 + [anywhere] * 2 + [vmem],
        out_specs=(vmem,) * 5,
        scratch_shapes=[pltpu.SemaphoreType.DMA((2,))],
        compiler_params=pltpu.CompilerParams(vmem_limit_bytes=4 << 20),
    )(where, lengths, adapter, owner, mine, other, fresh)


def products_kernel(sets, *refs):
    rows, weights, out_ref = refs[:sets], refs[sets:-1], refs[-1]
    features = rows[0].shape[1]
    columns = jnp.concatenate([w[:, :features] for w in weights], axis=0)
    out_ref[...] = nt_dot(jnp.concatenate([r[...] for r in rows], axis=0), columns)


def products(sets, weights):
    rows, columns = sum(r.shape[0] for r in sets), sum(w.shape[0] for w in weights)
    return pl.pallas_call(
        functools.partial(products_kernel, len(sets)),
        out_shape=jax.ShapeDtypeStruct((rows, columns), jnp.float32),
        cost_estimate=pl.CostEstimate(
            flops=2 * rows * columns * sets[0].shape[1],
            bytes_accessed=(rows + columns) * sets[0].shape[1] * 2,
            transcendentals=0,
        ),
        compiler_params=pltpu.CompilerParams(vmem_limit_bytes=12 << 20),
    )(*sets, *weights)


def late_kernel(where_ref, low_ref, high_ref, *refs):
    weights, (t_ref, kept_ref, given_ref, up_ref) = refs[:-4], refs[-4:]
    half, features = low_ref.shape
    count, columns = weights[0].shape[0], up_ref.shape[1]
    for k, ref in enumerate(weights):
        at = (k % 2) * (len(weights) * count) + (k // 2) * (2 * count)
        for part in range(2):
            lanes = slice(features + part * columns, features + (part + 1) * columns)
            up_ref[at + part * count : at + (part + 1) * count] = ref[:, lanes]
    columns = jnp.concatenate([w[:, :features] for w in weights], axis=0)
    late = nt_dot(jnp.concatenate([low_ref[...], high_ref[...]], axis=0), columns)
    first = where_ref[3] == 0
    for k in range(4):
        if k < 3:
            low, high = (t_ref[at * half : (at + 1) * half] for at in (2 * k, 2 * k + 1))
        else:
            low, high = late[:half], late[half:]
        kept_ref[k] = jnp.where(first, low, high)
        given_ref[k] = jnp.where(first, high, low)


def late_products(where, low, high, weights, t):
    smem, vmem = (pl.BlockSpec(memory_space=m) for m in (pltpu.SMEM, pltpu.VMEM))
    shape = jax.ShapeDtypeStruct((4, low.shape[0], t.shape[1]), jnp.float32)
    count, lanes = weights[0].shape
    up = ((2 * len(weights)) * count, (lanes - low.shape[1]) // 2)
    return pl.pallas_call(
        late_kernel,
        out_shape=(shape, shape, jax.ShapeDtypeStruct(up, low.dtype)),
        in_specs=[smem] + [vmem] * (len(weights) + 3),
        out_specs=(vmem,) * 3,
        compiler_params=pltpu.CompilerParams(vmem_limit_bytes=12 << 20),
    )(where, low, high, *weights, t)


def join_kernel(where_ref, mine_ref, other_ref, queries_ref, attended_ref, sems):
    core = where_ref[3]
    count = mine_ref.shape[1]
    mine, other = pl.ds(core * count, count), pl.ds((1 - core) * count, count)
    copy_all(
        [
            (mine_ref.at[0], queries_ref.at[mine]), (mine_ref.at[1], attended_ref.at[mine]),
            (other_ref.at[0], queries_ref.at[other]), (other_ref.at[1], attended_ref.at[other]),
        ],
        sems,
    )


def join(where, mine, other):
    anywhere = pl.BlockSpec(memory_space=pl.ANY)
    shape = jax.ShapeDtypeStruct((2 * mine.shape[1],) + mine.shape[2:], mine.dtype)
    return pl.pallas_call(
        join_kernel,
        out_shape=(shape, shape),
        in_specs=[pl.BlockSpec(memory_space=pltpu.SMEM), anywhere, anywhere],
        out_specs=(anywhere, anywhere),
        scratch_shapes=[pltpu.SemaphoreType.DMA((4,))],
        compiler_params=pltpu.CompilerParams(vmem_limit_bytes=2 << 20),
    )(where, mine, other)


def add_kernel(a_ref, b_ref, *outs):
    for k, out in enumerate(outs):
        out[...] = a_ref[k + 1] + b_ref[k + 1]


def add_halves(a, b):
    shape = jax.ShapeDtypeStruct(a.shape[1:], a.dtype)
    return pl.pallas_call(
        add_kernel,
        out_shape=(shape,) * (a.shape[0] - 1),
        compiler_params=pltpu.CompilerParams(vmem_limit_bytes=2 << 20),
    )(a, b)


def attend_block(queries, keys, values, masks, scaling):
    scores = [jnp.where(m, nt_dot(queries, k) * scaling, FAR) for k, m in zip(keys, masks)]
    highest = scores[0].max(axis=1, keepdims=True)
    for s in scores[1:]:
        highest = jnp.maximum(highest, s.max(axis=1, keepdims=True))
    weights = [jnp.where(m, jnp.exp(s - highest), 0.0) for s, m in zip(scores, masks)]
    totals = sum(w.sum(axis=1, keepdims=True) for w in weights)
    sums = sum(
        jnp.dot(w.astype(jnp.bfloat16), v, preferred_element_type=jnp.float32)
        for w, v in zip(weights, values)
    )
    return sums / totals


def attend(queries, caches, fresh_ref, limit_of, put, steps, head, per):
    rows = queries.shape[0]
    requests = rows // steps
    heads = queries.shape[1] // head
    scaling = 1.0 / math.sqrt(head)
    take = per * steps
    for b in range(requests // per):
        part = queries[b * take : (b + 1) * take, :]
        stacked = jnp.concatenate([part[:, h * head : (h + 1) * head] for h in range(heads)], axis=0)
        limit = limit_of(b)
        keys, values, masks = [], [], []
        for c, cache_ref in enumerate(caches):
            count = cache_ref.shape[0] // requests
            block = cache_ref[b * per * count : (b + 1) * per * count, :]
            shape = (heads * take, per * count)
            request = lax.rem(lax.broadcasted_iota(jnp.int32, shape, 0), take) // steps
            column = lax.broadcasted_iota(jnp.int32, shape, 1)
            position = lax.rem(column, count) + c * count
            masks.append(jnp.logical_and(column // count == request, position < limit))
            keys.append(block[:, :head])
            values.append(block[:, head:])
        block = fresh_ref[b * take : (b + 1) * take, :]
        shape = (heads * take, take)
        row = lax.rem(lax.broadcasted_iota(jnp.int32, shape, 0), take)
        column = lax.broadcasted_iota(jnp.int32, shape, 1)
        masks.append(jnp.logical_and(row // steps == column // steps, column <= row))
        keys.append(block[:, :head])
        values.append(block[:, head:])
        mixed = attend_block(stacked, keys, values, masks, scaling).astype(jnp.bfloat16)
        put(
            b,
            jnp.concatenate([mixed[h * take : (h + 1) * take] for h in range(heads)], axis=1),
        )


def finish_kernel(
    steps, where_ref, own_ref, other_ref, beside_ref, across_ref, both_ref, holder_ref,
    up_ref, up_other_ref, low_ref, high_ref, fresh_ref, limits_ref, out_ref,
):
    rows = own_ref.shape[1]
    x, part = where_ref[1], where_ref[2]
    width = 128
    half = width // 2
    own = own_ref[0] + other_ref[0]
    beside, across, both = beside_ref[...], across_ref[...], both_ref[...]
    queries_here = part == 0
    columns = jnp.where(queries_here, own, across), jnp.where(queries_here, beside, both)
    ranks = jnp.where(queries_here, across, own), jnp.where(queries_here, both, beside)
    low_lanes = lax.broadcasted_iota(jnp.int32, (rows, width), 1) < half
    even = jnp.where(x == 0, columns[0], columns[1])
    odd = jnp.where(x == 0, columns[1], columns[0])

    def spaced(wide):
        out = []
        for j in range(4):
            pair = wide[:, (j // 2) * width : (j // 2 + 1) * width]
            out.append((pair, pltpu.roll(pair, half, 1)) if j % 2 == 0 else (pltpu.roll(pair, half, 1), pair))
        return out

    even, odd = spaced(even), spaced(odd)
    merged = [jnp.where(low_lanes, e[0], o[1]) for e, o in zip(even, odd)]
    groups = []
    for k in range(4):
        group = merged[3]
        for j in range(3):
            group = jnp.where(where_ref[4 + j] == 2 * k + x, merged[j], group)
        groups.append(group)
    base = jnp.concatenate(groups, axis=1)
    holder = holder_ref[...]
    spread = []
    for m in range(4):
        lane_owner = jnp.where(low_lanes, where_ref[4 + 2 * m], where_ref[5 + 2 * m])
        shrink = ranks[m // 2][:, (m % 2) * width : (m % 2 + 1) * width]
        spread.append(jnp.where(holder == lane_owner, shrink, 0.0).astype(jnp.bfloat16))
    spread = jnp.concatenate(spread, axis=1)
    mine, other = (
        jnp.dot(spread, ref[...], preferred_element_type=jnp.float32) for ref in (up_ref, up_other_ref)
    )
    first = where_ref[3] == 0
    adapted = jnp.concatenate([jnp.where(first, mine, other), jnp.where(first, other, mine)], axis=1)
    queries = (base + adapted).astype(jnp.bfloat16)
    requests = rows // steps
    out_ref[0] = queries.reshape(requests, steps, -1)
    head = fresh_ref.shape[1] // 2

    def put(b, mixed):
        out_ref[1, b * PER : (b + 1) * PER] = mixed.reshape(PER, steps, -1)

    attend(
        queries, (low_ref, high_ref), fresh_ref, lambda b: limits_ref[b : b + 1, :], put, steps, head, PER
    )


def finish(steps, where, *arrays):
    rows, up = arrays[0].shape[1], arrays[6]
    vmem = pl.BlockSpec(memory_space=pltpu.VMEM)
    return pl.pallas_call(
        functools.partial(finish_kernel, steps),
        out_shape=jax.ShapeDtypeStruct((2, rows // steps, steps, 2 * up.shape[1]), jnp.bfloat16),
        in_specs=[pl.BlockSpec(memory_space=pltpu.SMEM)] + [vmem] * len(arrays),
        out_specs=vmem,
        compiler_params=pltpu.CompilerParams(vmem_limit_bytes=8 << 20),
    )(where, *arrays)


def attend_kernel(steps, q_ref, low_ref, high_ref, fresh_ref, limits_ref, out_ref):
    head = fresh_ref.shape[1] // 2
    take = PER * steps

    def put(b, mixed):
        out_ref[b * take : (b + 1) * take, :] = mixed

    attend(
        q_ref[...], (low_ref, high_ref), fresh_ref, lambda b: limits_ref[b : b + 1, :], put, steps, head, PER
    )


def line_pairs(groups, moves):
    return [(a * 2 + x, b * 2 + x) for a, b in moves for x in range(2)]


def holders_of(request_adapter, adapter_owner):
    ids = jnp.arange(adapter_owner.shape[0], dtype=jnp.int32)
    lookup = request_adapter[:, None] == ids[None, :]
    return jnp.sum(jnp.where(lookup, adapter_owner[None, :], 0), axis=1)


def body(
    normed_hidden_states,
    query_matrix,
    factor_down,
    factor_up,
    kv_cache,
    incoming_key_value,
    kv_lengths,
    request_adapter,
    adapter_owner,
):
    groups = lax.axis_size("group")
    core = lax.axis_index("tensor")
    requests, steps, features = normed_hidden_states.shape
    rows = requests * steps

    down = factor_down[0].T
    down_other = lax.ppermute(factor_down, "tensor", SWAP)[0].T
    query_block = query_matrix.T
    width = query_matrix.shape[1] * groups
    out_shape = (requests, steps, width)

    if groups == 8 and lax.axis_size("parts") == 2 and query_matrix.shape[1] == 2 * down.shape[0]:
        place = lax.axis_index("group")
        z, x, part = place // 2, lax.rem(place, 2), lax.axis_index("parts")
        order = z ^ (z // 2)
        steps_back = [lax.rem(order + 4 - k, 4) for k in range(4)]
        places = [k ^ (k // 2) for k in steps_back]
        where = [z, x, part, core] + [p * 2 + x for p in places] + [p * 2 + 1 - x for p in places]
        where = jnp.stack(where).astype(jnp.int32)
        bar = lambda *a: lax.optimization_barrier(a)
        along = lambda a, moves: lax.ppermute(a, "group", line_pairs(groups, moves))
        across = lambda a: lax.ppermute(a, "parts", SWAP)
        beside = lambda a: lax.ppermute(a, "group", [(i, i ^ 1) for i in range(groups)])
        inside = lambda a: lax.ppermute(a, "tensor", SWAP)
        corner = [(p * groups + i, (1 - p) * groups + (i ^ 1)) for p in range(2) for i in range(groups)]
        ring = ((0, 1), (1, 3), (3, 2), (2, 0))

        half = rows // 2
        mine = rows_of(normed_hidden_states)
        up_beside = beside(factor_up[0])
        a0, b0 = block_of(where, query_block, down, down_other, factor_up[0], up_beside)
        a0, b0, mine = bar(a0, b0, mine)
        a1, b1 = along(a0, ring), along(b0, ring)
        x_beside, x_across = beside(mine), across(mine)
        a2 = along(a1, ring)
        b2 = along(b1, ring)
        a3 = along(a2, ring)
        low, high = beside(x_across[:half]), across(x_beside[half:])
        cache = kv_cache.reshape(-1, kv_cache.shape[2])
        prepared = ready(
            where, kv_lengths, request_adapter, adapter_owner, cache, inside(cache), incoming_key_value, steps
        )
        b2, x_beside, x_across, prepared = bar(b2, x_beside, x_across, prepared)
        b3 = along(b2, ring)
        weights = a0, b0, a1, b1, a2, b2, a3, b3
        t = products((mine, x_beside, x_across), weights)

        low, high, t, prepared = bar(low, high, t, prepared)
        kept, given, up = late_products(where, low, high, weights, t)
        got = inside(given)
        t_beside, t_across, t_both = add_halves(kept, got)
        t_beside, t_across = beside(t_beside), across(t_across)
        t_both = lax.ppermute(t_both, ("parts", "group"), corner)
        cache_low, cache_high, fresh, limits, holder_rows = prepared
        done = finish(
            steps, where, kept, got, t_beside, t_across, t_both, holder_rows, up, inside(up),
            cache_low, cache_high, fresh, limits,
        )
        return join(where, done, inside(done))

    mine_down = lax.dynamic_slice_in_dim(down, core * features, features, 1)
    other_down = lax.dynamic_slice_in_dim(down_other, core * features, features, 1)
    down_block = jnp.where(
        core == 0,
        jnp.concatenate([mine_down, other_down], 0),
        jnp.concatenate([other_down, mine_down], 0),
    )
    holder = holders_of(request_adapter, adapter_owner)
    holder_rows = jnp.repeat(holder, steps)[:, None]
    limits = jnp.repeat(kv_lengths, kv_cache.shape[1]).reshape(requests // PER, -1)
    own = normed_hidden_states.reshape(rows, features)
    other_cache = lax.ppermute(kv_cache, "tensor", SWAP)
    low = jnp.where(core == 0, kv_cache, other_cache).reshape(-1, kv_cache.shape[2])
    high = jnp.where(core == 0, other_cache, kv_cache).reshape(-1, kv_cache.shape[2])
    fresh = incoming_key_value.reshape(rows, -1)
    up = lax.all_gather(factor_up[0], "group", axis=0, tiled=True)
    up_other = lax.ppermute(up, "tensor", SWAP)
    up_full = jnp.where(
        core == 0, jnp.concatenate([up, up_other], 1), jnp.concatenate([up_other, up], 1)
    )

    place = lax.axis_index("group")
    ring = [(i, (i + 1) % groups) for i in range(groups)]

    def step(k, carry):
        q_part, d_part, base, shrink = carry
        at = lax.rem(place - k + groups, groups)
        base = lax.dynamic_update_slice_in_dim(base, nt_dot(own, q_part), at * q_part.shape[0], 1)
        shrink = shrink + jnp.where(holder_rows == at, nt_dot(own, d_part), 0.0)
        q_part, d_part = (lax.ppermute(w, "group", ring) for w in (q_part, d_part))
        return q_part, d_part, base, shrink

    start = (
        query_block,
        down_block,
        jnp.zeros((rows, width), jnp.float32),
        jnp.zeros((rows, down_block.shape[0]), jnp.float32),
    )
    _, _, base, shrink = lax.fori_loop(0, groups, step, start)
    base = base + lax.ppermute(base, "tensor", SWAP)
    shrink = (shrink + lax.ppermute(shrink, "tensor", SWAP)).astype(jnp.bfloat16)
    named = holder_rows == jnp.arange(groups, dtype=jnp.int32)[None, :]
    spread = jnp.where(named[:, :, None], shrink[:, None, :], 0).reshape(rows, -1)
    adapted = jnp.dot(spread, up_full, preferred_element_type=jnp.float32)
    queries = (base + adapted).astype(jnp.bfloat16)
    attended = pl.pallas_call(
        functools.partial(attend_kernel, steps),
        out_shape=jax.ShapeDtypeStruct(queries.shape, jnp.bfloat16),
        compiler_params=pltpu.CompilerParams(vmem_limit_bytes=24 << 20),
    )(queries, low, high, fresh, limits)
    return queries.reshape(out_shape), attended.reshape(out_shape)


def solution(mesh):
    placed = (
        P(("parts", "group"), None, "tensor"),
        P("tensor", "group"),
        P("group", None, "tensor"),
        P("group", None, "tensor"),
        P(("parts", "group"), "tensor", None),
        P(("parts", "group"), None, None),
        P(("parts", "group")),
        P(("parts", "group")),
        P("parts"),
    )
    return jax.shard_map(
        body,
        mesh=mesh,
        in_specs=placed,
        out_specs=(P(("parts", "group"), None, None), P(("parts", "group"), None, None)),
        check_vma=False,
    )
```

```python
import functools
import math

import jax
import jax.numpy as jnp
from jax import lax
from jax.experimental import pallas as pl
from jax.experimental.pallas import tpu as pltpu
from jax.sharding import PartitionSpec as P

SWAP = [(0, 1), (1, 0)]
FAR = -1e30
PER = 8


def nt_dot(a, b):
    return lax.dot_general(a, b, (((1,), (1,)), ((), ())), preferred_element_type=jnp.float32)


def copy_all(copies, sems):
    started = [pltpu.make_async_copy(source, target, sems.at[k]) for k, (source, target) in enumerate(copies)]
    for copy in started:
        copy.start()
    for copy in started:
        copy.wait()


def block_kernel(
    where_ref, query_ref, kept_ref, given_ref, up_ref, up_beside_ref, a_ref, b_ref, sems
):
    part, core = where_ref[2], where_ref[3]
    count, features = kept_ref.shape[0], query_ref.shape[1]
    columns = up_ref.shape[1]
    chunks = [ref.at[:, :features] for ref in (a_ref, b_ref)]
    ups = []
    for ref, source in ((a_ref, up_ref), (b_ref, up_beside_ref)):
        ups.append((source.at[:count], ref.at[:, features : features + columns]))
        ups.append((source.at[count:], ref.at[:, features + columns :]))

    @pl.when(part == 0)
    def _():
        copy_all([(query_ref.at[:count], chunks[0]), (query_ref.at[count:], chunks[1])] + ups, sems)

    @pl.when(jnp.logical_and(part != 0, core == 0))
    def _():
        low = slice(0, features)
        copy_all([(kept_ref.at[:, low], chunks[0]), (given_ref.at[:, low], chunks[1])] + ups, sems)

    @pl.when(jnp.logical_and(part != 0, core != 0))
    def _():
        high = slice(features, 2 * features)
        copy_all([(given_ref.at[:, high], chunks[0]), (kept_ref.at[:, high], chunks[1])] + ups, sems)


def block_of(where, query, kept, given, up, up_beside):
    count, features = kept.shape[0], query.shape[1]
    vmem = pl.BlockSpec(memory_space=pltpu.VMEM)
    shape = jax.ShapeDtypeStruct((count, features + 2 * up.shape[1]), query.dtype)
    return pl.pallas_call(
        block_kernel,
        out_shape=(shape, shape),
        in_specs=[pl.BlockSpec(memory_space=pltpu.SMEM)] + [pl.BlockSpec(memory_space=pl.ANY)] * 5,
        out_specs=(vmem, vmem),
        scratch_shapes=[pltpu.SemaphoreType.DMA((6,))],
        compiler_params=pltpu.CompilerParams(vmem_limit_bytes=2 << 20),
    )(where, query, kept, given, up, up_beside)


def rows_kernel(x_ref, out_ref):
    out_ref[...] = x_ref[...].reshape(out_ref.shape)


def rows_of(x):
    return pl.pallas_call(
        rows_kernel,
        out_shape=jax.ShapeDtypeStruct((x.shape[0] * x.shape[1], x.shape[2]), x.dtype),
        compiler_params=pltpu.CompilerParams(vmem_limit_bytes=4 << 20),
    )(x)


def ready_kernel(
    where_ref, lengths_ref, adapter_ref, owner_ref, mine_ref, other_ref, fresh_ref,
    low_ref, high_ref, new_ref, limits_ref, holder_ref, sems,
):
    core = where_ref[3]
    half = new_ref.shape[0]
    requests = lengths_ref.shape[0] // 2
    steps = half // requests
    many = low_ref.shape[0]
    for k, (low, high) in enumerate(((mine_ref, other_ref), (other_ref, mine_ref))):

        @pl.when(core == k)
        def _():
            rows = slice(k * many, (k + 1) * many)
            copy_all([(low.at[rows], low_ref), (high.at[rows], high_ref)], sems)
            new_ref[...] = fresh_ref[k * requests : (k + 1) * requests].reshape(new_ref.shape)

    first = core * requests
    per = limits_ref.shape[1] // (many // requests)
    column = lax.broadcasted_iota(jnp.int32, (1, limits_ref.shape[1]), 1) // (many // requests)
    for b in range(requests // per):
        limit = jnp.zeros(column.shape, jnp.int32)
        for r in range(per):
            limit = jnp.where(column == r, lengths_ref[first + b * per + r], limit)
        limits_ref[b : b + 1, :] = limit
    row = lax.broadcasted_iota(jnp.int32, holder_ref.shape, 0) // steps
    holder = jnp.zeros(holder_ref.shape, jnp.int32)
    for r in range(requests):
        holder = jnp.where(row == r, owner_ref[adapter_ref[first + r]], holder)
    holder_ref[...] = holder


def ready(where, lengths, adapter, owner, mine, other, fresh, steps):
    requests, count = lengths.shape[0] // 2, mine.shape[0] // lengths.shape[0]
    smem, vmem = (pl.BlockSpec(memory_space=m) for m in (pltpu.SMEM, pltpu.VMEM))
    anywhere = pl.BlockSpec(memory_space=pl.ANY)
    cache = jax.ShapeDtypeStruct((requests * count, mine.shape[1]), mine.dtype)
    return pl.pallas_call(
        ready_kernel,
        out_shape=(
            cache,
            cache,
            jax.ShapeDtypeStruct((requests * steps, fresh.shape[2]), fresh.dtype),
            jax.ShapeDtypeStruct((8, PER * count), jnp.int32),
            jax.ShapeDtypeStruct((requests * steps, 128), jnp.int32),
        ),
        in_specs=[smem] * 4 + [anywhere] * 2 + [vmem],
        out_specs=(vmem,) * 5,
        scratch_shapes=[pltpu.SemaphoreType.DMA((2,))],
        compiler_params=pltpu.CompilerParams(vmem_limit_bytes=4 << 20),
    )(where, lengths, adapter, owner, mine, other, fresh)


def products_kernel(sets, *refs):
    rows, weights, out_ref = refs[:sets], refs[sets:-1], refs[-1]
    features = rows[0].shape[1]
    columns = jnp.concatenate([w[:, :features] for w in weights], axis=0)
    out_ref[...] = nt_dot(jnp.concatenate([r[...] for r in rows], axis=0), columns)


def products(sets, weights):
    rows, columns = sum(r.shape[0] for r in sets), sum(w.shape[0] for w in weights)
    return pl.pallas_call(
        functools.partial(products_kernel, len(sets)),
        out_shape=jax.ShapeDtypeStruct((rows, columns), jnp.float32),
        cost_estimate=pl.CostEstimate(
            flops=2 * rows * columns * sets[0].shape[1],
            bytes_accessed=(rows + columns) * sets[0].shape[1] * 2,
            transcendentals=0,
        ),
        compiler_params=pltpu.CompilerParams(vmem_limit_bytes=12 << 20),
    )(*sets, *weights)


def late_kernel(where_ref, *refs):
    sets, (low_ref, high_ref) = refs[:3], refs[3:5]
    weights, (t_ref, kept_ref, given_ref, up_ref) = refs[5:-4], refs[-4:]
    half, features = low_ref.shape
    count, columns = weights[0].shape[0], up_ref.shape[1]
    for k, ref in enumerate(weights):
        at = (k % 2) * (len(weights) * count) + (k // 2) * (2 * count)
        for part in range(2):
            lanes = slice(features + part * columns, features + (part + 1) * columns)
            up_ref[at + part * count : at + (part + 1) * count] = ref[:, lanes]
    all_columns = jnp.concatenate([w[:, :features] for w in weights], axis=0)
    late = nt_dot(jnp.concatenate([low_ref[...], high_ref[...]], axis=0), all_columns)
    last = nt_dot(jnp.concatenate([r[...] for r in sets], axis=0), weights[-1][:, :features])
    first = where_ref[3] == 0
    for k in range(4):
        if k < 3:
            low, high = (
                jnp.concatenate([r[at * half : (at + 1) * half] for r in (t_ref, last)], axis=1)
                for at in (2 * k, 2 * k + 1)
            )
        else:
            low, high = late[:half], late[half:]
        kept_ref[k] = jnp.where(first, low, high)
        given_ref[k] = jnp.where(first, high, low)


def late_products(where, sets, low, high, weights, t):
    smem, vmem = (pl.BlockSpec(memory_space=m) for m in (pltpu.SMEM, pltpu.VMEM))
    count, lanes = weights[0].shape
    half, features = low.shape
    shape = jax.ShapeDtypeStruct((4, half, len(weights) * count), jnp.float32)
    up = ((2 * len(weights)) * count, (lanes - features) // 2)
    return pl.pallas_call(
        late_kernel,
        out_shape=(shape, shape, jax.ShapeDtypeStruct(up, low.dtype)),
        in_specs=[smem] + [vmem] * (len(sets) + len(weights) + 3),
        out_specs=(vmem,) * 3,
        compiler_params=pltpu.CompilerParams(vmem_limit_bytes=12 << 20),
    )(where, *sets, low, high, *weights, t)


def join_kernel(where_ref, mine_ref, other_ref, queries_ref, attended_ref, sems):
    core = where_ref[3]
    count = mine_ref.shape[1]
    mine, other = pl.ds(core * count, count), pl.ds((1 - core) * count, count)
    copy_all(
        [
            (mine_ref.at[0], queries_ref.at[mine]), (mine_ref.at[1], attended_ref.at[mine]),
            (other_ref.at[0], queries_ref.at[other]), (other_ref.at[1], attended_ref.at[other]),
        ],
        sems,
    )


def join(where, mine, other):
    anywhere = pl.BlockSpec(memory_space=pl.ANY)
    shape = jax.ShapeDtypeStruct((2 * mine.shape[1],) + mine.shape[2:], mine.dtype)
    return pl.pallas_call(
        join_kernel,
        out_shape=(shape, shape),
        in_specs=[pl.BlockSpec(memory_space=pltpu.SMEM), anywhere, anywhere],
        out_specs=(anywhere, anywhere),
        scratch_shapes=[pltpu.SemaphoreType.DMA((4,))],
        compiler_params=pltpu.CompilerParams(vmem_limit_bytes=2 << 20),
    )(where, mine, other)


def add_kernel(a_ref, b_ref, *outs):
    for k, out in enumerate(outs):
        out[...] = a_ref[k + 1] + b_ref[k + 1]


def add_halves(a, b):
    shape = jax.ShapeDtypeStruct(a.shape[1:], a.dtype)
    return pl.pallas_call(
        add_kernel,
        out_shape=(shape,) * (a.shape[0] - 1),
        compiler_params=pltpu.CompilerParams(vmem_limit_bytes=2 << 20),
    )(a, b)


def attend_block(queries, keys, values, masks, scaling):
    scores = [jnp.where(m, nt_dot(queries, k) * scaling, FAR) for k, m in zip(keys, masks)]
    highest = scores[0].max(axis=1, keepdims=True)
    for s in scores[1:]:
        highest = jnp.maximum(highest, s.max(axis=1, keepdims=True))
    weights = [jnp.where(m, jnp.exp(s - highest), 0.0) for s, m in zip(scores, masks)]
    totals = sum(w.sum(axis=1, keepdims=True) for w in weights)
    sums = sum(
        jnp.dot(w.astype(jnp.bfloat16), v, preferred_element_type=jnp.float32)
        for w, v in zip(weights, values)
    )
    return sums / totals


def attend(queries, caches, fresh_ref, limit_of, put, steps, head, per):
    rows = queries.shape[0]
    requests = rows // steps
    heads = queries.shape[1] // head
    scaling = 1.0 / math.sqrt(head)
    take = per * steps
    for b in range(requests // per):
        part = queries[b * take : (b + 1) * take, :]
        stacked = jnp.concatenate([part[:, h * head : (h + 1) * head] for h in range(heads)], axis=0)
        limit = limit_of(b)
        keys, values, masks = [], [], []
        for c, cache_ref in enumerate(caches):
            count = cache_ref.shape[0] // requests
            block = cache_ref[b * per * count : (b + 1) * per * count, :]
            shape = (heads * take, per * count)
            request = lax.rem(lax.broadcasted_iota(jnp.int32, shape, 0), take) // steps
            column = lax.broadcasted_iota(jnp.int32, shape, 1)
            position = lax.rem(column, count) + c * count
            masks.append(jnp.logical_and(column // count == request, position < limit))
            keys.append(block[:, :head])
            values.append(block[:, head:])
        block = fresh_ref[b * take : (b + 1) * take, :]
        shape = (heads * take, take)
        row = lax.rem(lax.broadcasted_iota(jnp.int32, shape, 0), take)
        column = lax.broadcasted_iota(jnp.int32, shape, 1)
        masks.append(jnp.logical_and(row // steps == column // steps, column <= row))
        keys.append(block[:, :head])
        values.append(block[:, head:])
        mixed = attend_block(stacked, keys, values, masks, scaling).astype(jnp.bfloat16)
        put(
            b,
            jnp.concatenate([mixed[h * take : (h + 1) * take] for h in range(heads)], axis=1),
        )


def finish_kernel(
    steps, where_ref, own_ref, other_ref, beside_ref, across_ref, both_ref, holder_ref,
    up_ref, up_other_ref, low_ref, high_ref, fresh_ref, limits_ref, out_ref,
):
    rows = own_ref.shape[1]
    x, part = where_ref[1], where_ref[2]
    width = 128
    half = width // 2
    own = own_ref[0] + other_ref[0]
    beside, across, both = beside_ref[...], across_ref[...], both_ref[...]
    queries_here = part == 0
    columns = jnp.where(queries_here, own, across), jnp.where(queries_here, beside, both)
    ranks = jnp.where(queries_here, across, own), jnp.where(queries_here, both, beside)
    low_lanes = lax.broadcasted_iota(jnp.int32, (rows, width), 1) < half
    even = jnp.where(x == 0, columns[0], columns[1])
    odd = jnp.where(x == 0, columns[1], columns[0])

    def spaced(wide):
        out = []
        for j in range(4):
            pair = wide[:, (j // 2) * width : (j // 2 + 1) * width]
            out.append((pair, pltpu.roll(pair, half, 1)) if j % 2 == 0 else (pltpu.roll(pair, half, 1), pair))
        return out

    even, odd = spaced(even), spaced(odd)
    merged = [jnp.where(low_lanes, e[0], o[1]) for e, o in zip(even, odd)]
    groups = []
    for k in range(4):
        group = merged[3]
        for j in range(3):
            group = jnp.where(where_ref[4 + j] == 2 * k + x, merged[j], group)
        groups.append(group)
    base = jnp.concatenate(groups, axis=1)
    holder = holder_ref[...]
    spread = []
    for m in range(4):
        lane_owner = jnp.where(low_lanes, where_ref[4 + 2 * m], where_ref[5 + 2 * m])
        shrink = ranks[m // 2][:, (m % 2) * width : (m % 2 + 1) * width]
        spread.append(jnp.where(holder == lane_owner, shrink, 0.0).astype(jnp.bfloat16))
    spread = jnp.concatenate(spread, axis=1)
    mine, other = (
        jnp.dot(spread, ref[...], preferred_element_type=jnp.float32) for ref in (up_ref, up_other_ref)
    )
    first = where_ref[3] == 0
    adapted = jnp.concatenate([jnp.where(first, mine, other), jnp.where(first, other, mine)], axis=1)
    queries = (base + adapted).astype(jnp.bfloat16)
    requests = rows // steps
    out_ref[0] = queries.reshape(requests, steps, -1)
    head = fresh_ref.shape[1] // 2

    def put(b, mixed):
        out_ref[1, b * PER : (b + 1) * PER] = mixed.reshape(PER, steps, -1)

    attend(
        queries, (low_ref, high_ref), fresh_ref, lambda b: limits_ref[b : b + 1, :], put, steps, head, PER
    )


def finish(steps, where, *arrays):
    rows, up = arrays[0].shape[1], arrays[6]
    vmem = pl.BlockSpec(memory_space=pltpu.VMEM)
    return pl.pallas_call(
        functools.partial(finish_kernel, steps),
        out_shape=jax.ShapeDtypeStruct((2, rows // steps, steps, 2 * up.shape[1]), jnp.bfloat16),
        in_specs=[pl.BlockSpec(memory_space=pltpu.SMEM)] + [vmem] * len(arrays),
        out_specs=vmem,
        compiler_params=pltpu.CompilerParams(vmem_limit_bytes=8 << 20),
    )(where, *arrays)


def attend_kernel(steps, q_ref, low_ref, high_ref, fresh_ref, limits_ref, out_ref):
    head = fresh_ref.shape[1] // 2
    take = PER * steps

    def put(b, mixed):
        out_ref[b * take : (b + 1) * take, :] = mixed

    attend(
        q_ref[...], (low_ref, high_ref), fresh_ref, lambda b: limits_ref[b : b + 1, :], put, steps, head, PER
    )


def line_pairs(groups, moves):
    return [(a * 2 + x, b * 2 + x) for a, b in moves for x in range(2)]


def holders_of(request_adapter, adapter_owner):
    ids = jnp.arange(adapter_owner.shape[0], dtype=jnp.int32)
    lookup = request_adapter[:, None] == ids[None, :]
    return jnp.sum(jnp.where(lookup, adapter_owner[None, :], 0), axis=1)


def body(
    normed_hidden_states,
    query_matrix,
    factor_down,
    factor_up,
    kv_cache,
    incoming_key_value,
    kv_lengths,
    request_adapter,
    adapter_owner,
):
    groups = lax.axis_size("group")
    core = lax.axis_index("tensor")
    requests, steps, features = normed_hidden_states.shape
    rows = requests * steps

    down = factor_down[0].T
    down_other = lax.ppermute(factor_down, "tensor", SWAP)[0].T
    query_block = query_matrix.T
    width = query_matrix.shape[1] * groups
    out_shape = (requests, steps, width)

    if groups == 8 and lax.axis_size("parts") == 2 and query_matrix.shape[1] == 2 * down.shape[0]:
        place = lax.axis_index("group")
        z, x, part = place // 2, lax.rem(place, 2), lax.axis_index("parts")
        order = z ^ (z // 2)
        steps_back = [lax.rem(order + 4 - k, 4) for k in range(4)]
        places = [k ^ (k // 2) for k in steps_back]
        where = [z, x, part, core] + [p * 2 + x for p in places] + [p * 2 + 1 - x for p in places]
        where = jnp.stack(where).astype(jnp.int32)
        bar = lambda *a: lax.optimization_barrier(a)
        along = lambda a, moves: lax.ppermute(a, "group", line_pairs(groups, moves))
        across = lambda a: lax.ppermute(a, "parts", SWAP)
        beside = lambda a: lax.ppermute(a, "group", [(i, i ^ 1) for i in range(groups)])
        inside = lambda a: lax.ppermute(a, "tensor", SWAP)
        corner = [(p * groups + i, (1 - p) * groups + (i ^ 1)) for p in range(2) for i in range(groups)]
        ring = ((0, 1), (1, 3), (3, 2), (2, 0))

        half = rows // 2
        mine = rows_of(normed_hidden_states)
        up_beside = beside(factor_up[0])
        a0, b0 = block_of(where, query_block, down, down_other, factor_up[0], up_beside)
        a0, b0, mine = bar(a0, b0, mine)
        a1, b1 = along(a0, ring), along(b0, ring)
        x_beside, x_across = beside(mine), across(mine)
        a2 = along(a1, ring)
        b2 = along(b1, ring)
        a3 = along(a2, ring)
        low, high = beside(x_across[:half]), across(x_beside[half:])
        cache = kv_cache.reshape(-1, kv_cache.shape[2])
        prepared = ready(
            where, kv_lengths, request_adapter, adapter_owner, cache, inside(cache), incoming_key_value, steps
        )
        b2, x_beside, x_across, prepared = bar(b2, x_beside, x_across, prepared)
        b3 = along(b2, ring)
        weights = a0, b0, a1, b1, a2, b2, a3, b3
        sets = mine, x_beside, x_across
        t = products(sets, weights[:-1])

        low, high, t, prepared = bar(low, high, t, prepared)
        kept, given, up = late_products(where, sets, low, high, weights, t)
        got = inside(given)
        t_beside, t_across, t_both = add_halves(kept, got)
        t_beside, t_across = beside(t_beside), across(t_across)
        t_both = lax.ppermute(t_both, ("parts", "group"), corner)
        cache_low, cache_high, fresh, limits, holder_rows = prepared
        done = finish(
            steps, where, kept, got, t_beside, t_across, t_both, holder_rows, up, inside(up),
            cache_low, cache_high, fresh, limits,
        )
        return join(where, done, inside(done))

    mine_down = lax.dynamic_slice_in_dim(down, core * features, features, 1)
    other_down = lax.dynamic_slice_in_dim(down_other, core * features, features, 1)
    down_block = jnp.where(
        core == 0,
        jnp.concatenate([mine_down, other_down], 0),
        jnp.concatenate([other_down, mine_down], 0),
    )
    holder = holders_of(request_adapter, adapter_owner)
    holder_rows = jnp.repeat(holder, steps)[:, None]
    limits = jnp.repeat(kv_lengths, kv_cache.shape[1]).reshape(requests // PER, -1)
    own = normed_hidden_states.reshape(rows, features)
    other_cache = lax.ppermute(kv_cache, "tensor", SWAP)
    low = jnp.where(core == 0, kv_cache, other_cache).reshape(-1, kv_cache.shape[2])
    high = jnp.where(core == 0, other_cache, kv_cache).reshape(-1, kv_cache.shape[2])
    fresh = incoming_key_value.reshape(rows, -1)
    up = lax.all_gather(factor_up[0], "group", axis=0, tiled=True)
    up_other = lax.ppermute(up, "tensor", SWAP)
    up_full = jnp.where(
        core == 0, jnp.concatenate([up, up_other], 1), jnp.concatenate([up_other, up], 1)
    )

    place = lax.axis_index("group")
    ring = [(i, (i + 1) % groups) for i in range(groups)]

    def step(k, carry):
        q_part, d_part, base, shrink = carry
        at = lax.rem(place - k + groups, groups)
        base = lax.dynamic_update_slice_in_dim(base, nt_dot(own, q_part), at * q_part.shape[0], 1)
        shrink = shrink + jnp.where(holder_rows == at, nt_dot(own, d_part), 0.0)
        q_part, d_part = (lax.ppermute(w, "group", ring) for w in (q_part, d_part))
        return q_part, d_part, base, shrink

    start = (
        query_block,
        down_block,
        jnp.zeros((rows, width), jnp.float32),
        jnp.zeros((rows, down_block.shape[0]), jnp.float32),
    )
    _, _, base, shrink = lax.fori_loop(0, groups, step, start)
    base = base + lax.ppermute(base, "tensor", SWAP)
    shrink = (shrink + lax.ppermute(shrink, "tensor", SWAP)).astype(jnp.bfloat16)
    named = holder_rows == jnp.arange(groups, dtype=jnp.int32)[None, :]
    spread = jnp.where(named[:, :, None], shrink[:, None, :], 0).reshape(rows, -1)
    adapted = jnp.dot(spread, up_full, preferred_element_type=jnp.float32)
    queries = (base + adapted).astype(jnp.bfloat16)
    attended = pl.pallas_call(
        functools.partial(attend_kernel, steps),
        out_shape=jax.ShapeDtypeStruct(queries.shape, jnp.bfloat16),
        compiler_params=pltpu.CompilerParams(vmem_limit_bytes=24 << 20),
    )(queries, low, high, fresh, limits)
    return queries.reshape(out_shape), attended.reshape(out_shape)


def solution(mesh):
    placed = (
        P(("parts", "group"), None, "tensor"),
        P("tensor", "group"),
        P("group", None, "tensor"),
        P("group", None, "tensor"),
        P(("parts", "group"), "tensor", None),
        P(("parts", "group"), None, None),
        P(("parts", "group")),
        P(("parts", "group")),
        P("parts"),
    )
    return jax.shard_map(
        body,
        mesh=mesh,
        in_specs=placed,
        out_specs=(P(("parts", "group"), None, None), P(("parts", "group"), None, None)),
        check_vma=False,
    )
```

```python
import functools
import math

import jax
import jax.numpy as jnp
from jax import lax
from jax.experimental import pallas as pl
from jax.experimental.pallas import tpu as pltpu
from jax.sharding import PartitionSpec as P

SWAP = [(0, 1), (1, 0)]
FAR = -1e30
PER = 16


def nt_dot(a, b):
    return lax.dot_general(a, b, (((1,), (1,)), ((), ())), preferred_element_type=jnp.float32)


def copy_all(copies, sems):
    started = [pltpu.make_async_copy(source, target, sems.at[k]) for k, (source, target) in enumerate(copies)]
    for copy in started:
        copy.start()
    for copy in started:
        copy.wait()


def block_kernel(
    where_ref, query_ref, kept_ref, given_ref, up_ref, up_beside_ref, a_ref, b_ref, sems
):
    part, core = where_ref[2], where_ref[3]
    count, features = kept_ref.shape[0], query_ref.shape[1]
    columns = up_ref.shape[1]
    chunks = [ref.at[:, :features] for ref in (a_ref, b_ref)]
    ups = []
    for ref, source in ((a_ref, up_ref), (b_ref, up_beside_ref)):
        ups.append((source.at[:count], ref.at[:, features : features + columns]))
        ups.append((source.at[count:], ref.at[:, features + columns :]))

    @pl.when(part == 0)
    def _():
        copy_all([(query_ref.at[:count], chunks[0]), (query_ref.at[count:], chunks[1])] + ups, sems)

    @pl.when(jnp.logical_and(part != 0, core == 0))
    def _():
        low = slice(0, features)
        copy_all([(kept_ref.at[:, low], chunks[0]), (given_ref.at[:, low], chunks[1])] + ups, sems)

    @pl.when(jnp.logical_and(part != 0, core != 0))
    def _():
        high = slice(features, 2 * features)
        copy_all([(given_ref.at[:, high], chunks[0]), (kept_ref.at[:, high], chunks[1])] + ups, sems)


def block_of(where, query, kept, given, up, up_beside):
    count, features = kept.shape[0], query.shape[1]
    vmem = pl.BlockSpec(memory_space=pltpu.VMEM)
    shape = jax.ShapeDtypeStruct((count, features + 2 * up.shape[1]), query.dtype)
    return pl.pallas_call(
        block_kernel,
        out_shape=(shape, shape),
        in_specs=[pl.BlockSpec(memory_space=pltpu.SMEM)] + [pl.BlockSpec(memory_space=pl.ANY)] * 5,
        out_specs=(vmem, vmem),
        scratch_shapes=[pltpu.SemaphoreType.DMA((6,))],
        compiler_params=pltpu.CompilerParams(vmem_limit_bytes=2 << 20),
    )(where, query, kept, given, up, up_beside)


def rows_kernel(x_ref, out_ref):
    out_ref[...] = x_ref[...].reshape(out_ref.shape)


def rows_of(x):
    return pl.pallas_call(
        rows_kernel,
        out_shape=jax.ShapeDtypeStruct((x.shape[0] * x.shape[1], x.shape[2]), x.dtype),
        compiler_params=pltpu.CompilerParams(vmem_limit_bytes=4 << 20),
    )(x)


def ready_kernel(
    where_ref, lengths_ref, adapter_ref, owner_ref, mine_ref, other_ref, fresh_ref,
    low_ref, high_ref, new_ref, limits_ref, holder_ref, sems,
):
    core = where_ref[3]
    half = new_ref.shape[0]
    requests = lengths_ref.shape[0] // 2
    steps = half // requests
    many = low_ref.shape[0]
    for k, (low, high) in enumerate(((mine_ref, other_ref), (other_ref, mine_ref))):

        @pl.when(core == k)
        def _():
            rows = slice(k * many, (k + 1) * many)
            copy_all([(low.at[rows], low_ref), (high.at[rows], high_ref)], sems)
            new_ref[...] = fresh_ref[k * requests : (k + 1) * requests].reshape(new_ref.shape)

    first = core * requests
    per = limits_ref.shape[1] // (many // requests)
    column = lax.broadcasted_iota(jnp.int32, (1, limits_ref.shape[1]), 1) // (many // requests)
    for b in range(requests // per):
        limit = jnp.zeros(column.shape, jnp.int32)
        for r in range(per):
            limit = jnp.where(column == r, lengths_ref[first + b * per + r], limit)
        limits_ref[b : b + 1, :] = limit
    row = lax.broadcasted_iota(jnp.int32, holder_ref.shape, 0) // steps
    holder = jnp.zeros(holder_ref.shape, jnp.int32)
    for r in range(requests):
        holder = jnp.where(row == r, owner_ref[adapter_ref[first + r]], holder)
    holder_ref[...] = holder


def ready(where, lengths, adapter, owner, mine, other, fresh, steps):
    requests, count = lengths.shape[0] // 2, mine.shape[0] // lengths.shape[0]
    smem, vmem = (pl.BlockSpec(memory_space=m) for m in (pltpu.SMEM, pltpu.VMEM))
    anywhere = pl.BlockSpec(memory_space=pl.ANY)
    cache = jax.ShapeDtypeStruct((requests * count, mine.shape[1]), mine.dtype)
    return pl.pallas_call(
        ready_kernel,
        out_shape=(
            cache,
            cache,
            jax.ShapeDtypeStruct((requests * steps, fresh.shape[2]), fresh.dtype),
            jax.ShapeDtypeStruct((8, PER * count), jnp.int32),
            jax.ShapeDtypeStruct((requests * steps, 128), jnp.int32),
        ),
        in_specs=[smem] * 4 + [anywhere] * 2 + [vmem],
        out_specs=(vmem,) * 5,
        scratch_shapes=[pltpu.SemaphoreType.DMA((2,))],
        compiler_params=pltpu.CompilerParams(vmem_limit_bytes=4 << 20),
    )(where, lengths, adapter, owner, mine, other, fresh)


def products_kernel(sets, *refs):
    rows, weights, out_ref = refs[:sets], refs[sets:-1], refs[-1]
    features = rows[0].shape[1]
    columns = jnp.concatenate([w[:, :features] for w in weights], axis=0)
    out_ref[...] = nt_dot(jnp.concatenate([r[...] for r in rows], axis=0), columns)


def products(sets, weights):
    rows, columns = sum(r.shape[0] for r in sets), sum(w.shape[0] for w in weights)
    return pl.pallas_call(
        functools.partial(products_kernel, len(sets)),
        out_shape=jax.ShapeDtypeStruct((rows, columns), jnp.float32),
        cost_estimate=pl.CostEstimate(
            flops=2 * rows * columns * sets[0].shape[1],
            bytes_accessed=(rows + columns) * sets[0].shape[1] * 2,
            transcendentals=0,
        ),
        compiler_params=pltpu.CompilerParams(vmem_limit_bytes=12 << 20),
    )(*sets, *weights)


def late_kernel(where_ref, *refs):
    sets, weights = refs[:5], refs[5:-5]
    t_ref, corner_ref, kept_ref, given_ref, up_ref = refs[-5:]
    half, features = sets[-1].shape
    count, columns = weights[0].shape[0], up_ref.shape[1]
    for k, ref in enumerate(weights):
        at = (k % 2) * (len(weights) * count) + (k // 2) * (2 * count)
        for part in range(2):
            lanes = slice(features + part * columns, features + (part + 1) * columns)
            up_ref[at + part * count : at + (part + 1) * count] = ref[:, lanes]
    last = nt_dot(jnp.concatenate([r[...] for r in sets], axis=0), weights[-1][:, :features])
    first = where_ref[3] == 0
    for k in range(4):
        ref, base = (t_ref, 2 * k * half) if k < 3 else (corner_ref, 0)
        low, high = (
            jnp.concatenate(
                [ref[base + p * half : base + (p + 1) * half], last[(2 * k + p) * half : (2 * k + p + 1) * half]],
                axis=1,
            )
            for p in range(2)
        )
        kept_ref[k] = jnp.where(first, low, high)
        given_ref[k] = jnp.where(first, high, low)


def late_products(where, sets, weights, t, corner):
    smem, vmem = (pl.BlockSpec(memory_space=m) for m in (pltpu.SMEM, pltpu.VMEM))
    count, lanes = weights[0].shape
    half, features = sets[-1].shape
    shape = jax.ShapeDtypeStruct((4, half, len(weights) * count), jnp.float32)
    up = ((2 * len(weights)) * count, (lanes - features) // 2)
    return pl.pallas_call(
        late_kernel,
        out_shape=(shape, shape, jax.ShapeDtypeStruct(up, sets[0].dtype)),
        in_specs=[smem] + [vmem] * (len(sets) + len(weights) + 2),
        out_specs=(vmem,) * 3,
        compiler_params=pltpu.CompilerParams(vmem_limit_bytes=12 << 20),
    )(where, *sets, *weights, t, corner)


def join_kernel(where_ref, mine_ref, other_ref, queries_ref, attended_ref, sems):
    core = where_ref[3]
    count = mine_ref.shape[1]
    mine, other = pl.ds(core * count, count), pl.ds((1 - core) * count, count)
    copy_all(
        [
            (mine_ref.at[0], queries_ref.at[mine]), (mine_ref.at[1], attended_ref.at[mine]),
            (other_ref.at[0], queries_ref.at[other]), (other_ref.at[1], attended_ref.at[other]),
        ],
        sems,
    )


def join(where, mine, other):
    anywhere = pl.BlockSpec(memory_space=pl.ANY)
    shape = jax.ShapeDtypeStruct((2 * mine.shape[1],) + mine.shape[2:], mine.dtype)
    return pl.pallas_call(
        join_kernel,
        out_shape=(shape, shape),
        in_specs=[pl.BlockSpec(memory_space=pltpu.SMEM), anywhere, anywhere],
        out_specs=(anywhere, anywhere),
        scratch_shapes=[pltpu.SemaphoreType.DMA((4,))],
        compiler_params=pltpu.CompilerParams(vmem_limit_bytes=2 << 20),
    )(where, mine, other)


def add_kernel(a_ref, b_ref, *outs):
    for k, out in enumerate(outs):
        out[...] = a_ref[k + 1] + b_ref[k + 1]


def add_halves(a, b):
    shape = jax.ShapeDtypeStruct(a.shape[1:], a.dtype)
    return pl.pallas_call(
        add_kernel,
        out_shape=(shape,) * (a.shape[0] - 1),
        compiler_params=pltpu.CompilerParams(vmem_limit_bytes=2 << 20),
    )(a, b)


def attend_block(queries, keys, values, mask, scaling):
    scores = jnp.where(mask, nt_dot(queries, keys) * scaling, FAR)
    highest = scores.max(axis=1, keepdims=True)
    weights = jnp.where(mask, jnp.exp(scores - highest), 0.0)
    totals = weights.sum(axis=1, keepdims=True)
    sums = jnp.dot(weights.astype(jnp.bfloat16), values, preferred_element_type=jnp.float32)
    return sums / totals


def attend(queries, caches, fresh_ref, limit_of, put, steps, head, per):
    rows = queries.shape[0]
    requests = rows // steps
    heads = queries.shape[1] // head
    scaling = 1.0 / math.sqrt(head)
    take = per * steps
    for b in range(requests // per):
        part = queries[b * take : (b + 1) * take, :]
        stacked = jnp.concatenate([part[:, h * head : (h + 1) * head] for h in range(heads)], axis=0)
        limit = limit_of(b)
        keys, values, masks = [], [], []
        for c, cache_ref in enumerate(caches):
            count = cache_ref.shape[0] // requests
            block = cache_ref[b * per * count : (b + 1) * per * count, :]
            shape = (heads * take, per * count)
            request = lax.rem(lax.broadcasted_iota(jnp.int32, shape, 0), take) // steps
            column = lax.broadcasted_iota(jnp.int32, shape, 1)
            position = lax.rem(column, count) + c * count
            masks.append(jnp.logical_and(column // count == request, position < limit))
            keys.append(block[:, :head])
            values.append(block[:, head:])
        block = fresh_ref[b * take : (b + 1) * take, :]
        shape = (heads * take, take)
        row = lax.rem(lax.broadcasted_iota(jnp.int32, shape, 0), take)
        column = lax.broadcasted_iota(jnp.int32, shape, 1)
        masks.append(jnp.logical_and(row // steps == column // steps, column <= row))
        keys.append(block[:, :head])
        values.append(block[:, head:])
        mixed = attend_block(
            stacked, *(jnp.concatenate(a, axis=0) for a in (keys, values)),
            jnp.concatenate(masks, axis=1), scaling,
        ).astype(jnp.bfloat16)
        put(
            b,
            jnp.concatenate([mixed[h * take : (h + 1) * take] for h in range(heads)], axis=1),
        )


def finish_kernel(
    steps, where_ref, own_ref, other_ref, beside_ref, across_ref, both_ref, holder_ref,
    up_ref, up_other_ref, low_ref, high_ref, fresh_ref, limits_ref, out_ref,
):
    rows = own_ref.shape[1]
    x, part = where_ref[1], where_ref[2]
    width = 128
    half = width // 2
    own = own_ref[0] + other_ref[0]
    beside, across, both = beside_ref[...], across_ref[...], both_ref[...]
    queries_here = part == 0
    columns = jnp.where(queries_here, own, across), jnp.where(queries_here, beside, both)
    ranks = jnp.where(queries_here, across, own), jnp.where(queries_here, both, beside)
    low_lanes = lax.broadcasted_iota(jnp.int32, (rows, width), 1) < half
    even = jnp.where(x == 0, columns[0], columns[1])
    odd = jnp.where(x == 0, columns[1], columns[0])

    def spaced(wide):
        out = []
        for j in range(4):
            pair = wide[:, (j // 2) * width : (j // 2 + 1) * width]
            out.append((pair, pltpu.roll(pair, half, 1)) if j % 2 == 0 else (pltpu.roll(pair, half, 1), pair))
        return out

    even, odd = spaced(even), spaced(odd)
    merged = [jnp.where(low_lanes, e[0], o[1]) for e, o in zip(even, odd)]
    groups = []
    for k in range(4):
        group = merged[3]
        for j in range(3):
            group = jnp.where(where_ref[4 + j] == 2 * k + x, merged[j], group)
        groups.append(group)
    base = jnp.concatenate(groups, axis=1)
    holder = holder_ref[...]
    spread = []
    for m in range(4):
        lane_owner = jnp.where(low_lanes, where_ref[4 + 2 * m], where_ref[5 + 2 * m])
        shrink = ranks[m // 2][:, (m % 2) * width : (m % 2 + 1) * width]
        spread.append(jnp.where(holder == lane_owner, shrink, 0.0).astype(jnp.bfloat16))
    spread = jnp.concatenate(spread, axis=1)
    mine, other = (
        jnp.dot(spread, ref[...], preferred_element_type=jnp.float32) for ref in (up_ref, up_other_ref)
    )
    first = where_ref[3] == 0
    adapted = jnp.concatenate([jnp.where(first, mine, other), jnp.where(first, other, mine)], axis=1)
    queries = (base + adapted).astype(jnp.bfloat16)
    requests = rows // steps
    out_ref[0] = queries.reshape(requests, steps, -1)
    head = fresh_ref.shape[1] // 2

    def put(b, mixed):
        out_ref[1, b * PER : (b + 1) * PER] = mixed.reshape(PER, steps, -1)

    attend(
        queries, (low_ref, high_ref), fresh_ref, lambda b: limits_ref[b : b + 1, :], put, steps, head, PER
    )


def finish(steps, where, *arrays):
    rows, up = arrays[0].shape[1], arrays[6]
    vmem = pl.BlockSpec(memory_space=pltpu.VMEM)
    return pl.pallas_call(
        functools.partial(finish_kernel, steps),
        out_shape=jax.ShapeDtypeStruct((2, rows // steps, steps, 2 * up.shape[1]), jnp.bfloat16),
        in_specs=[pl.BlockSpec(memory_space=pltpu.SMEM)] + [vmem] * len(arrays),
        out_specs=vmem,
        compiler_params=pltpu.CompilerParams(vmem_limit_bytes=8 << 20),
    )(where, *arrays)


def attend_kernel(steps, q_ref, low_ref, high_ref, fresh_ref, limits_ref, out_ref):
    head = fresh_ref.shape[1] // 2
    take = PER * steps

    def put(b, mixed):
        out_ref[b * take : (b + 1) * take, :] = mixed

    attend(
        q_ref[...], (low_ref, high_ref), fresh_ref, lambda b: limits_ref[b : b + 1, :], put, steps, head, PER
    )


def line_pairs(groups, moves):
    return [(a * 2 + x, b * 2 + x) for a, b in moves for x in range(2)]


def holders_of(request_adapter, adapter_owner):
    ids = jnp.arange(adapter_owner.shape[0], dtype=jnp.int32)
    lookup = request_adapter[:, None] == ids[None, :]
    return jnp.sum(jnp.where(lookup, adapter_owner[None, :], 0), axis=1)


def body(
    normed_hidden_states,
    query_matrix,
    factor_down,
    factor_up,
    kv_cache,
    incoming_key_value,
    kv_lengths,
    request_adapter,
    adapter_owner,
):
    groups = lax.axis_size("group")
    core = lax.axis_index("tensor")
    requests, steps, features = normed_hidden_states.shape
    rows = requests * steps

    down = factor_down[0].T
    down_other = lax.ppermute(factor_down, "tensor", SWAP)[0].T
    query_block = query_matrix.T
    width = query_matrix.shape[1] * groups
    out_shape = (requests, steps, width)

    if groups == 8 and lax.axis_size("parts") == 2 and query_matrix.shape[1] == 2 * down.shape[0]:
        place = lax.axis_index("group")
        z, x, part = place // 2, lax.rem(place, 2), lax.axis_index("parts")
        order = z ^ (z // 2)
        steps_back = [lax.rem(order + 4 - k, 4) for k in range(4)]
        places = [k ^ (k // 2) for k in steps_back]
        where = [z, x, part, core] + [p * 2 + x for p in places] + [p * 2 + 1 - x for p in places]
        where = jnp.stack(where).astype(jnp.int32)
        bar = lambda *a: lax.optimization_barrier(a)
        along = lambda a, moves: lax.ppermute(a, "group", line_pairs(groups, moves))
        across = lambda a: lax.ppermute(a, "parts", SWAP)
        beside = lambda a: lax.ppermute(a, "group", [(i, i ^ 1) for i in range(groups)])
        inside = lambda a: lax.ppermute(a, "tensor", SWAP)
        corner = [(p * groups + i, (1 - p) * groups + (i ^ 1)) for p in range(2) for i in range(groups)]
        ring = ((0, 1), (1, 3), (3, 2), (2, 0))

        half = rows // 2
        mine = rows_of(normed_hidden_states)
        up_beside = beside(factor_up[0])
        a0, b0 = block_of(where, query_block, down, down_other, factor_up[0], up_beside)
        a0, b0, mine = bar(a0, b0, mine)
        a1, b1 = along(a0, ring), along(b0, ring)
        x_beside, x_across = beside(mine), across(mine)
        a2 = along(a1, ring)
        b2 = along(b1, ring)
        a3 = along(a2, ring)
        low, high = beside(x_across[:half]), across(x_beside[half:])
        cache = kv_cache.reshape(-1, kv_cache.shape[2])
        prepared = ready(
            where, kv_lengths, request_adapter, adapter_owner, cache, inside(cache), incoming_key_value, steps
        )
        b2, x_beside, x_across, prepared = bar(b2, x_beside, x_across, prepared)
        b3 = along(b2, ring)
        weights = a0, b0, a1, b1, a2, b2, a3, b3
        sets = mine, x_beside, x_across
        t, corner_t = products(sets, weights[:-1]), products((low, high), weights[:-1])

        t, corner_t, prepared = bar(t, corner_t, prepared)
        kept, given, up = late_products(where, sets + (low, high), weights, t, corner_t)
        got = inside(given)
        t_beside, t_across, t_both = add_halves(kept, got)
        t_beside, t_across = beside(t_beside), across(t_across)
        t_both = lax.ppermute(t_both, ("parts", "group"), corner)
        cache_low, cache_high, fresh, limits, holder_rows = prepared
        done = finish(
            steps, where, kept, got, t_beside, t_across, t_both, holder_rows, up, inside(up),
            cache_low, cache_high, fresh, limits,
        )
        return join(where, done, inside(done))

    mine_down = lax.dynamic_slice_in_dim(down, core * features, features, 1)
    other_down = lax.dynamic_slice_in_dim(down_other, core * features, features, 1)
    down_block = jnp.where(
        core == 0,
        jnp.concatenate([mine_down, other_down], 0),
        jnp.concatenate([other_down, mine_down], 0),
    )
    holder = holders_of(request_adapter, adapter_owner)
    holder_rows = jnp.repeat(holder, steps)[:, None]
    limits = jnp.repeat(kv_lengths, kv_cache.shape[1]).reshape(requests // PER, -1)
    own = normed_hidden_states.reshape(rows, features)
    other_cache = lax.ppermute(kv_cache, "tensor", SWAP)
    low = jnp.where(core == 0, kv_cache, other_cache).reshape(-1, kv_cache.shape[2])
    high = jnp.where(core == 0, other_cache, kv_cache).reshape(-1, kv_cache.shape[2])
    fresh = incoming_key_value.reshape(rows, -1)
    up = lax.all_gather(factor_up[0], "group", axis=0, tiled=True)
    up_other = lax.ppermute(up, "tensor", SWAP)
    up_full = jnp.where(
        core == 0, jnp.concatenate([up, up_other], 1), jnp.concatenate([up_other, up], 1)
    )

    place = lax.axis_index("group")
    ring = [(i, (i + 1) % groups) for i in range(groups)]

    def step(k, carry):
        q_part, d_part, base, shrink = carry
        at = lax.rem(place - k + groups, groups)
        base = lax.dynamic_update_slice_in_dim(base, nt_dot(own, q_part), at * q_part.shape[0], 1)
        shrink = shrink + jnp.where(holder_rows == at, nt_dot(own, d_part), 0.0)
        q_part, d_part = (lax.ppermute(w, "group", ring) for w in (q_part, d_part))
        return q_part, d_part, base, shrink

    start = (
        query_block,
        down_block,
        jnp.zeros((rows, width), jnp.float32),
        jnp.zeros((rows, down_block.shape[0]), jnp.float32),
    )
    _, _, base, shrink = lax.fori_loop(0, groups, step, start)
    base = base + lax.ppermute(base, "tensor", SWAP)
    shrink = (shrink + lax.ppermute(shrink, "tensor", SWAP)).astype(jnp.bfloat16)
    named = holder_rows == jnp.arange(groups, dtype=jnp.int32)[None, :]
    spread = jnp.where(named[:, :, None], shrink[:, None, :], 0).reshape(rows, -1)
    adapted = jnp.dot(spread, up_full, preferred_element_type=jnp.float32)
    queries = (base + adapted).astype(jnp.bfloat16)
    attended = pl.pallas_call(
        functools.partial(attend_kernel, steps),
        out_shape=jax.ShapeDtypeStruct(queries.shape, jnp.bfloat16),
        compiler_params=pltpu.CompilerParams(vmem_limit_bytes=24 << 20),
    )(queries, low, high, fresh, limits)
    return queries.reshape(out_shape), attended.reshape(out_shape)


def solution(mesh):
    placed = (
        P(("parts", "group"), None, "tensor"),
        P("tensor", "group"),
        P("group", None, "tensor"),
        P("group", None, "tensor"),
        P(("parts", "group"), "tensor", None),
        P(("parts", "group"), None, None),
        P(("parts", "group")),
        P(("parts", "group")),
        P("parts"),
    )
    return jax.shard_map(
        body,
        mesh=mesh,
        in_specs=placed,
        out_specs=(P(("parts", "group"), None, None), P(("parts", "group"), None, None)),
        check_vma=False,
    )
```

```python
import functools
import math

import jax
import jax.numpy as jnp
from jax import lax
from jax.experimental import pallas as pl
from jax.experimental.pallas import tpu as pltpu
from jax.sharding import PartitionSpec as P

SWAP = [(0, 1), (1, 0)]
FAR = -1e30
PER = 16


def nt_dot(a, b):
    return lax.dot_general(a, b, (((1,), (1,)), ((), ())), preferred_element_type=jnp.float32)


def copy_all(copies, sems):
    started = [pltpu.make_async_copy(source, target, sems.at[k]) for k, (source, target) in enumerate(copies)]
    for copy in started:
        copy.start()
    for copy in started:
        copy.wait()


def block_kernel(
    where_ref, query_ref, kept_ref, given_ref, up_ref, up_beside_ref, a_ref, b_ref, sems
):
    part, core = where_ref[2], where_ref[3]
    count, features = kept_ref.shape[0], query_ref.shape[1]
    columns = up_ref.shape[1]
    chunks = [ref.at[:, :features] for ref in (a_ref, b_ref)]
    ups = []
    for ref, source in ((a_ref, up_ref), (b_ref, up_beside_ref)):
        ups.append((source.at[:count], ref.at[:, features : features + columns]))
        ups.append((source.at[count:], ref.at[:, features + columns :]))

    @pl.when(part == 0)
    def _():
        copy_all([(query_ref.at[:count], chunks[0]), (query_ref.at[count:], chunks[1])] + ups, sems)

    @pl.when(jnp.logical_and(part != 0, core == 0))
    def _():
        low = slice(0, features)
        copy_all([(kept_ref.at[:, low], chunks[0]), (given_ref.at[:, low], chunks[1])] + ups, sems)

    @pl.when(jnp.logical_and(part != 0, core != 0))
    def _():
        high = slice(features, 2 * features)
        copy_all([(given_ref.at[:, high], chunks[0]), (kept_ref.at[:, high], chunks[1])] + ups, sems)


def block_of(where, query, kept, given, up, up_beside):
    count, features = kept.shape[0], query.shape[1]
    vmem = pl.BlockSpec(memory_space=pltpu.VMEM)
    shape = jax.ShapeDtypeStruct((count, features + 2 * up.shape[1]), query.dtype)
    return pl.pallas_call(
        block_kernel,
        out_shape=(shape, shape),
        in_specs=[pl.BlockSpec(memory_space=pltpu.SMEM)] + [pl.BlockSpec(memory_space=pl.ANY)] * 5,
        out_specs=(vmem, vmem),
        scratch_shapes=[pltpu.SemaphoreType.DMA((6,))],
        compiler_params=pltpu.CompilerParams(vmem_limit_bytes=2 << 20),
    )(where, query, kept, given, up, up_beside)


def rows_kernel(x_ref, out_ref):
    out_ref[...] = x_ref[...].reshape(out_ref.shape)


def rows_of(x):
    return pl.pallas_call(
        rows_kernel,
        out_shape=jax.ShapeDtypeStruct((x.shape[0] * x.shape[1], x.shape[2]), x.dtype),
        compiler_params=pltpu.CompilerParams(vmem_limit_bytes=4 << 20),
    )(x)


def ready_kernel(
    where_ref, lengths_ref, adapter_ref, owner_ref, mine_ref, other_ref, fresh_ref,
    low_ref, high_ref, new_ref, limits_ref, holder_ref, sems,
):
    core = where_ref[3]
    half = new_ref.shape[0]
    requests = lengths_ref.shape[0] // 2
    steps = half // requests
    many = low_ref.shape[0]
    for k, (low, high) in enumerate(((mine_ref, other_ref), (other_ref, mine_ref))):

        @pl.when(core == k)
        def _():
            rows = slice(k * many, (k + 1) * many)
            copy_all([(low.at[rows], low_ref), (high.at[rows], high_ref)], sems)
            new_ref[...] = fresh_ref[k * requests : (k + 1) * requests].reshape(new_ref.shape)

    first = core * requests
    per = limits_ref.shape[1] // (many // requests)
    column = lax.broadcasted_iota(jnp.int32, (1, limits_ref.shape[1]), 1) // (many // requests)
    for b in range(requests // per):
        limit = jnp.zeros(column.shape, jnp.int32)
        for r in range(per):
            limit = jnp.where(column == r, lengths_ref[first + b * per + r], limit)
        limits_ref[b : b + 1, :] = limit
    row = lax.broadcasted_iota(jnp.int32, holder_ref.shape, 0) // steps
    holder = jnp.zeros(holder_ref.shape, jnp.int32)
    for r in range(requests):
        holder = jnp.where(row == r, owner_ref[adapter_ref[first + r]], holder)
    holder_ref[...] = holder


def ready(where, lengths, adapter, owner, mine, other, fresh, steps):
    requests, count = lengths.shape[0] // 2, mine.shape[0] // lengths.shape[0]
    smem, vmem = (pl.BlockSpec(memory_space=m) for m in (pltpu.SMEM, pltpu.VMEM))
    anywhere = pl.BlockSpec(memory_space=pl.ANY)
    cache = jax.ShapeDtypeStruct((requests * count, mine.shape[1]), mine.dtype)
    return pl.pallas_call(
        ready_kernel,
        out_shape=(
            cache,
            cache,
            jax.ShapeDtypeStruct((requests * steps, fresh.shape[2]), fresh.dtype),
            jax.ShapeDtypeStruct((8, PER * count), jnp.int32),
            jax.ShapeDtypeStruct((requests * steps, 128), jnp.int32),
        ),
        in_specs=[smem] * 4 + [anywhere] * 2 + [vmem],
        out_specs=(vmem,) * 5,
        scratch_shapes=[pltpu.SemaphoreType.DMA((2,))],
        compiler_params=pltpu.CompilerParams(vmem_limit_bytes=4 << 20),
    )(where, lengths, adapter, owner, mine, other, fresh)


def products_kernel(sets, *refs):
    rows, weights, out_ref = refs[:sets], refs[sets:-1], refs[-1]
    features = rows[0].shape[1]
    columns = jnp.concatenate([w[:, :features] for w in weights], axis=0)
    out_ref[...] = nt_dot(jnp.concatenate([r[...] for r in rows], axis=0), columns)


def products(sets, weights):
    rows, columns = sum(r.shape[0] for r in sets), sum(w.shape[0] for w in weights)
    return pl.pallas_call(
        functools.partial(products_kernel, len(sets)),
        out_shape=jax.ShapeDtypeStruct((rows, columns), jnp.float32),
        cost_estimate=pl.CostEstimate(
            flops=2 * rows * columns * sets[0].shape[1],
            bytes_accessed=(rows + columns) * sets[0].shape[1] * 2,
            transcendentals=0,
        ),
        compiler_params=pltpu.CompilerParams(vmem_limit_bytes=12 << 20),
    )(*sets, *weights)


def late_kernel(where_ref, *refs):
    sets, weights = refs[:5], refs[5:-5]
    t_ref, corner_ref, kept_ref, given_ref, up_ref = refs[-5:]
    half, features = sets[-1].shape
    count, columns = weights[0].shape[0], up_ref.shape[1]
    for k, ref in enumerate(weights):
        at = (k % 2) * (len(weights) * count) + (k // 2) * (2 * count)
        for part in range(2):
            lanes = slice(features + part * columns, features + (part + 1) * columns)
            up_ref[at + part * count : at + (part + 1) * count] = ref[:, lanes]
    last = nt_dot(jnp.concatenate([r[...] for r in sets], axis=0), weights[-1][:, :features])
    first = where_ref[3] == 0
    for k in range(4):
        ref, base = (t_ref, 2 * k * half) if k < 3 else (corner_ref, 0)
        low, high = (
            jnp.concatenate(
                [ref[base + p * half : base + (p + 1) * half], last[(2 * k + p) * half : (2 * k + p + 1) * half]],
                axis=1,
            )
            for p in range(2)
        )
        kept_ref[k] = jnp.where(first, low, high)
        given_ref[k] = jnp.where(first, high, low)


def late_products(where, sets, weights, t, corner):
    smem, vmem = (pl.BlockSpec(memory_space=m) for m in (pltpu.SMEM, pltpu.VMEM))
    count, lanes = weights[0].shape
    half, features = sets[-1].shape
    shape = jax.ShapeDtypeStruct((4, half, len(weights) * count), jnp.float32)
    up = ((2 * len(weights)) * count, (lanes - features) // 2)
    return pl.pallas_call(
        late_kernel,
        out_shape=(shape, shape, jax.ShapeDtypeStruct(up, sets[0].dtype)),
        in_specs=[smem] + [vmem] * (len(sets) + len(weights) + 2),
        out_specs=(vmem,) * 3,
        compiler_params=pltpu.CompilerParams(vmem_limit_bytes=12 << 20),
    )(where, *sets, *weights, t, corner)


def join_kernel(where_ref, mine_ref, other_ref, queries_ref, attended_ref, sems):
    core = where_ref[3]
    count = mine_ref.shape[1]
    mine, other = pl.ds(core * count, count), pl.ds((1 - core) * count, count)
    copy_all(
        [
            (mine_ref.at[0], queries_ref.at[mine]), (mine_ref.at[1], attended_ref.at[mine]),
            (other_ref.at[0], queries_ref.at[other]), (other_ref.at[1], attended_ref.at[other]),
        ],
        sems,
    )


def join(where, mine, other):
    anywhere = pl.BlockSpec(memory_space=pl.ANY)
    shape = jax.ShapeDtypeStruct((2 * mine.shape[1],) + mine.shape[2:], mine.dtype)
    return pl.pallas_call(
        join_kernel,
        out_shape=(shape, shape),
        in_specs=[pl.BlockSpec(memory_space=pltpu.SMEM), anywhere, anywhere],
        out_specs=(anywhere, anywhere),
        scratch_shapes=[pltpu.SemaphoreType.DMA((4,))],
        compiler_params=pltpu.CompilerParams(vmem_limit_bytes=2 << 20),
    )(where, mine, other)


def add_kernel(a_ref, b_ref, *outs):
    for k, out in enumerate(outs):
        out[...] = a_ref[k + 1] + b_ref[k + 1]


def add_halves(a, b):
    shape = jax.ShapeDtypeStruct(a.shape[1:], a.dtype)
    return pl.pallas_call(
        add_kernel,
        out_shape=(shape,) * (a.shape[0] - 1),
        compiler_params=pltpu.CompilerParams(vmem_limit_bytes=2 << 20),
    )(a, b)


def attend_block(queries, keys, values, mask, scaling):
    scores = jnp.where(mask, nt_dot(queries, keys) * scaling, FAR)
    highest = scores.max(axis=1, keepdims=True)
    weights = jnp.where(mask, jnp.exp(scores - highest), 0.0)
    totals = weights.sum(axis=1, keepdims=True)
    sums = jnp.dot(weights.astype(jnp.bfloat16), values, preferred_element_type=jnp.float32)
    return sums / totals


def attend(queries, caches, fresh_ref, limit_of, put, steps, head, per):
    rows = queries.shape[0]
    requests = rows // steps
    heads = queries.shape[1] // head
    scaling = 1.0 / math.sqrt(head)
    take = per * steps
    for b in range(requests // per):
        part = queries[b * take : (b + 1) * take, :]
        stacked = jnp.concatenate([part[:, h * head : (h + 1) * head] for h in range(heads)], axis=0)
        limit = limit_of(b)
        keys, values, masks = [], [], []
        for c, cache_ref in enumerate(caches):
            count = cache_ref.shape[0] // requests
            block = cache_ref[b * per * count : (b + 1) * per * count, :]
            shape = (heads * take, per * count)
            request = lax.rem(lax.broadcasted_iota(jnp.int32, shape, 0), take) // steps
            column = lax.broadcasted_iota(jnp.int32, shape, 1)
            position = lax.rem(column, count) + c * count
            masks.append(jnp.logical_and(column // count == request, position < limit))
            keys.append(block[:, :head])
            values.append(block[:, head:])
        block = fresh_ref[b * take : (b + 1) * take, :]
        shape = (heads * take, take)
        row = lax.rem(lax.broadcasted_iota(jnp.int32, shape, 0), take)
        column = lax.broadcasted_iota(jnp.int32, shape, 1)
        masks.append(jnp.logical_and(row // steps == column // steps, column <= row))
        keys.append(block[:, :head])
        values.append(block[:, head:])
        mixed = attend_block(
            stacked, *(jnp.concatenate(a, axis=0) for a in (keys, values)),
            jnp.concatenate(masks, axis=1), scaling,
        ).astype(jnp.bfloat16)
        put(
            b,
            jnp.concatenate([mixed[h * take : (h + 1) * take] for h in range(heads)], axis=1),
        )


def finish_kernel(
    steps, where_ref, own_ref, other_ref, beside_ref, across_ref, both_ref, holder_ref,
    up_ref, up_other_ref, low_ref, high_ref, fresh_ref, limits_ref, out_ref,
):
    rows = own_ref.shape[1]
    x, part = where_ref[1], where_ref[2]
    width = 128
    half = width // 2
    own = own_ref[0] + other_ref[0]
    beside, across, both = beside_ref[...], across_ref[...], both_ref[...]
    queries_here = part == 0
    columns = jnp.where(queries_here, own, across), jnp.where(queries_here, beside, both)
    ranks = jnp.where(queries_here, across, own), jnp.where(queries_here, both, beside)
    low_lanes = lax.broadcasted_iota(jnp.int32, (rows, width), 1) < half
    even = jnp.where(x == 0, columns[0], columns[1])
    odd = jnp.where(x == 0, columns[1], columns[0])

    def spaced(wide):
        out = []
        for j in range(4):
            pair = wide[:, (j // 2) * width : (j // 2 + 1) * width]
            out.append((pair, pltpu.roll(pair, half, 1)) if j % 2 == 0 else (pltpu.roll(pair, half, 1), pair))
        return out

    even, odd = spaced(even), spaced(odd)
    merged = [jnp.where(low_lanes, e[0], o[1]) for e, o in zip(even, odd)]
    groups = []
    for k in range(4):
        group = merged[3]
        for j in range(3):
            group = jnp.where(where_ref[4 + j] == 2 * k + x, merged[j], group)
        groups.append(group)
    base = jnp.concatenate(groups, axis=1)
    holder = holder_ref[...]
    spread = []
    for m in range(4):
        lane_owner = jnp.where(low_lanes, where_ref[4 + 2 * m], where_ref[5 + 2 * m])
        shrink = ranks[m // 2][:, (m % 2) * width : (m % 2 + 1) * width]
        spread.append(jnp.where(holder == lane_owner, shrink, 0.0).astype(jnp.bfloat16))
    spread = jnp.concatenate(spread, axis=1)
    mine, other = (
        jnp.dot(spread, ref[...], preferred_element_type=jnp.float32) for ref in (up_ref, up_other_ref)
    )
    first = where_ref[3] == 0
    adapted = jnp.concatenate([jnp.where(first, mine, other), jnp.where(first, other, mine)], axis=1)
    queries = (base + adapted).astype(jnp.bfloat16)
    requests = rows // steps
    out_ref[0] = queries.reshape(requests, steps, -1)
    head = fresh_ref.shape[1] // 2

    def put(b, mixed):
        out_ref[1, b * PER : (b + 1) * PER] = mixed.reshape(PER, steps, -1)

    attend(
        queries, (low_ref, high_ref), fresh_ref, lambda b: limits_ref[b : b + 1, :], put, steps, head, PER
    )


def finish(steps, where, *arrays):
    rows, up = arrays[0].shape[1], arrays[6]
    vmem = pl.BlockSpec(memory_space=pltpu.VMEM)
    return pl.pallas_call(
        functools.partial(finish_kernel, steps),
        out_shape=jax.ShapeDtypeStruct((2, rows // steps, steps, 2 * up.shape[1]), jnp.bfloat16),
        in_specs=[pl.BlockSpec(memory_space=pltpu.SMEM)] + [vmem] * len(arrays),
        out_specs=vmem,
        compiler_params=pltpu.CompilerParams(vmem_limit_bytes=8 << 20),
    )(where, *arrays)


def attend_kernel(steps, q_ref, low_ref, high_ref, fresh_ref, limits_ref, out_ref):
    head = fresh_ref.shape[1] // 2
    take = PER * steps

    def put(b, mixed):
        out_ref[b * take : (b + 1) * take, :] = mixed

    attend(
        q_ref[...], (low_ref, high_ref), fresh_ref, lambda b: limits_ref[b : b + 1, :], put, steps, head, PER
    )


def line_pairs(groups, moves):
    return [(a * 2 + x, b * 2 + x) for a, b in moves for x in range(2)]


def holders_of(request_adapter, adapter_owner):
    ids = jnp.arange(adapter_owner.shape[0], dtype=jnp.int32)
    lookup = request_adapter[:, None] == ids[None, :]
    return jnp.sum(jnp.where(lookup, adapter_owner[None, :], 0), axis=1)


def body(
    normed_hidden_states,
    query_matrix,
    factor_down,
    factor_up,
    kv_cache,
    incoming_key_value,
    kv_lengths,
    request_adapter,
    adapter_owner,
):
    groups = lax.axis_size("group")
    core = lax.axis_index("tensor")
    requests, steps, features = normed_hidden_states.shape
    rows = requests * steps

    down = factor_down[0].T
    down_other = lax.ppermute(factor_down, "tensor", SWAP)[0].T
    query_block = query_matrix.T
    width = query_matrix.shape[1] * groups
    out_shape = (requests, steps, width)

    if groups == 8 and lax.axis_size("parts") == 2 and query_matrix.shape[1] == 2 * down.shape[0]:
        place = lax.axis_index("group")
        z, x, part = place // 2, lax.rem(place, 2), lax.axis_index("parts")
        order = z ^ (z // 2)
        steps_back = [lax.rem(order + k, 4) for k in range(4)]
        places = [k ^ (k // 2) for k in steps_back]
        where = [z, x, part, core] + [p * 2 + x for p in places] + [p * 2 + 1 - x for p in places]
        where = jnp.stack(where).astype(jnp.int32)
        bar = lambda *a: lax.optimization_barrier(a)
        along = lambda a, moves: lax.ppermute(a, "group", line_pairs(groups, moves))
        across = lambda a: lax.ppermute(a, "parts", SWAP)
        beside = lambda a: lax.ppermute(a, "group", [(i, i ^ 1) for i in range(groups)])
        inside = lambda a: lax.ppermute(a, "tensor", SWAP)
        corner = [(p * groups + i, (1 - p) * groups + (i ^ 1)) for p in range(2) for i in range(groups)]
        ring = ((1, 0), (3, 1), (2, 3), (0, 2))

        half = rows // 2
        mine = rows_of(normed_hidden_states)
        up_beside = beside(factor_up[0])
        a0, b0 = block_of(where, query_block, down, down_other, factor_up[0], up_beside)
        a0, b0, mine = bar(a0, b0, mine)
        a1, b1 = along(a0, ring), along(b0, ring)
        x_beside, x_across = beside(mine), across(mine)
        a2 = along(a1, ring)
        b2 = along(b1, ring)
        a3 = along(a2, ring)
        low, high = beside(x_across[:half]), across(x_beside[half:])
        cache = kv_cache.reshape(-1, kv_cache.shape[2])
        prepared = ready(
            where, kv_lengths, request_adapter, adapter_owner, cache, inside(cache), incoming_key_value, steps
        )
        b2, x_across, prepared = bar(b2, x_across, prepared)
        b3 = along(b2, ring)
        weights = a0, b0, a1, b1, a2, b2, a3, b3
        sets = mine, x_beside, x_across
        t, corner_t = products(sets, weights[:-1]), products((low, high), weights[:-1])

        t, corner_t, prepared = bar(t, corner_t, prepared)
        kept, given, up = late_products(where, sets + (low, high), weights, t, corner_t)
        got = inside(given)
        t_beside, t_across, t_both = add_halves(kept, got)
        t_beside, t_across = beside(t_beside), across(t_across)
        t_both = lax.ppermute(t_both, ("parts", "group"), corner)
        cache_low, cache_high, fresh, limits, holder_rows = prepared
        done = finish(
            steps, where, kept, got, t_beside, t_across, t_both, holder_rows, up, inside(up),
            cache_low, cache_high, fresh, limits,
        )
        return join(where, done, inside(done))

    mine_down = lax.dynamic_slice_in_dim(down, core * features, features, 1)
    other_down = lax.dynamic_slice_in_dim(down_other, core * features, features, 1)
    down_block = jnp.where(
        core == 0,
        jnp.concatenate([mine_down, other_down], 0),
        jnp.concatenate([other_down, mine_down], 0),
    )
    holder = holders_of(request_adapter, adapter_owner)
    holder_rows = jnp.repeat(holder, steps)[:, None]
    limits = jnp.repeat(kv_lengths, kv_cache.shape[1]).reshape(requests // PER, -1)
    own = normed_hidden_states.reshape(rows, features)
    other_cache = lax.ppermute(kv_cache, "tensor", SWAP)
    low = jnp.where(core == 0, kv_cache, other_cache).reshape(-1, kv_cache.shape[2])
    high = jnp.where(core == 0, other_cache, kv_cache).reshape(-1, kv_cache.shape[2])
    fresh = incoming_key_value.reshape(rows, -1)
    up = lax.all_gather(factor_up[0], "group", axis=0, tiled=True)
    up_other = lax.ppermute(up, "tensor", SWAP)
    up_full = jnp.where(
        core == 0, jnp.concatenate([up, up_other], 1), jnp.concatenate([up_other, up], 1)
    )

    place = lax.axis_index("group")
    ring = [(i, (i + 1) % groups) for i in range(groups)]

    def step(k, carry):
        q_part, d_part, base, shrink = carry
        at = lax.rem(place - k + groups, groups)
        base = lax.dynamic_update_slice_in_dim(base, nt_dot(own, q_part), at * q_part.shape[0], 1)
        shrink = shrink + jnp.where(holder_rows == at, nt_dot(own, d_part), 0.0)
        q_part, d_part = (lax.ppermute(w, "group", ring) for w in (q_part, d_part))
        return q_part, d_part, base, shrink

    start = (
        query_block,
        down_block,
        jnp.zeros((rows, width), jnp.float32),
        jnp.zeros((rows, down_block.shape[0]), jnp.float32),
    )
    _, _, base, shrink = lax.fori_loop(0, groups, step, start)
    base = base + lax.ppermute(base, "tensor", SWAP)
    shrink = (shrink + lax.ppermute(shrink, "tensor", SWAP)).astype(jnp.bfloat16)
    named = holder_rows == jnp.arange(groups, dtype=jnp.int32)[None, :]
    spread = jnp.where(named[:, :, None], shrink[:, None, :], 0).reshape(rows, -1)
    adapted = jnp.dot(spread, up_full, preferred_element_type=jnp.float32)
    queries = (base + adapted).astype(jnp.bfloat16)
    attended = pl.pallas_call(
        functools.partial(attend_kernel, steps),
        out_shape=jax.ShapeDtypeStruct(queries.shape, jnp.bfloat16),
        compiler_params=pltpu.CompilerParams(vmem_limit_bytes=24 << 20),
    )(queries, low, high, fresh, limits)
    return queries.reshape(out_shape), attended.reshape(out_shape)


def solution(mesh):
    placed = (
        P(("parts", "group"), None, "tensor"),
        P("tensor", "group"),
        P("group", None, "tensor"),
        P("group", None, "tensor"),
        P(("parts", "group"), "tensor", None),
        P(("parts", "group"), None, None),
        P(("parts", "group")),
        P(("parts", "group")),
        P("parts"),
    )
    return jax.shard_map(
        body,
        mesh=mesh,
        in_specs=placed,
        out_specs=(P(("parts", "group"), None, None), P(("parts", "group"), None, None)),
        check_vma=False,
    )
```

```python
import functools
import math

import jax
import jax.numpy as jnp
from jax import lax
from jax.experimental import pallas as pl
from jax.experimental.pallas import tpu as pltpu
from jax.sharding import PartitionSpec as P

SWAP = [(0, 1), (1, 0)]
FAR = -1e30
PER = 16


def nt_dot(a, b):
    return lax.dot_general(a, b, (((1,), (1,)), ((), ())), preferred_element_type=jnp.float32)


def copy_all(copies, sems):
    started = [pltpu.make_async_copy(source, target, sems.at[k]) for k, (source, target) in enumerate(copies)]
    for copy in started:
        copy.start()
    for copy in started:
        copy.wait()


def block_kernel(
    where_ref, query_ref, kept_ref, given_ref, up_ref, up_beside_ref, a_ref, b_ref, sems
):
    part, core = where_ref[2], where_ref[3]
    count, width = kept_ref.shape[0], query_ref.shape[1] // 2
    chunks = [ref.at[:, :width] for ref in (a_ref, b_ref)]
    ups = [(up_ref, a_ref.at[:, width:]), (up_beside_ref, b_ref.at[:, width:])]

    @pl.when(part == 0)
    def _():
        copy_all([(query_ref.at[:, k * width : (k + 1) * width], chunks[k]) for k in range(2)] + ups, sems)

    for own in range(2):

        @pl.when(jnp.logical_and(part != 0, core == own))
        def _():
            copies = []
            for k in range(2):
                features = slice((2 * own + k) * width, (2 * own + k + 1) * width)
                for owner in range(2):
                    source = kept_ref if owner == own else given_ref
                    target = (a_ref, b_ref)[k].at[owner * count : (owner + 1) * count, :width]
                    copies.append((source.at[:, features], target))
            copy_all(copies + ups, sems)


def block_of(where, query, kept, given, up, up_beside):
    vmem = pl.BlockSpec(memory_space=pltpu.VMEM)
    shape = jax.ShapeDtypeStruct((query.shape[0], query.shape[1] // 2 + up.shape[1]), query.dtype)
    return pl.pallas_call(
        block_kernel,
        out_shape=(shape, shape),
        in_specs=[pl.BlockSpec(memory_space=pltpu.SMEM)] + [pl.BlockSpec(memory_space=pl.ANY)] * 5,
        out_specs=(vmem, vmem),
        scratch_shapes=[pltpu.SemaphoreType.DMA((6,))],
        compiler_params=pltpu.CompilerParams(vmem_limit_bytes=2 << 20),
    )(where, query, kept, given, up, up_beside)


def rows_kernel(x_ref, out_ref):
    out_ref[...] = x_ref[...].reshape(out_ref.shape)


def rows_of(x):
    return pl.pallas_call(
        rows_kernel,
        out_shape=jax.ShapeDtypeStruct((x.shape[0] * x.shape[1], x.shape[2]), x.dtype),
        compiler_params=pltpu.CompilerParams(vmem_limit_bytes=4 << 20),
    )(x)


def ready_kernel(
    where_ref, lengths_ref, adapter_ref, owner_ref, mine_ref, other_ref, fresh_ref,
    low_ref, high_ref, new_ref, limits_ref, holder_ref, sems,
):
    core = where_ref[3]
    half = new_ref.shape[0]
    requests = lengths_ref.shape[0] // 2
    steps = half // requests
    many = low_ref.shape[0]
    for k, (low, high) in enumerate(((mine_ref, other_ref), (other_ref, mine_ref))):

        @pl.when(core == k)
        def _():
            rows = slice(k * many, (k + 1) * many)
            copy_all([(low.at[rows], low_ref), (high.at[rows], high_ref)], sems)
            new_ref[...] = fresh_ref[k * requests : (k + 1) * requests].reshape(new_ref.shape)

    first = core * requests
    per = limits_ref.shape[1] // (many // requests)
    column = lax.broadcasted_iota(jnp.int32, (1, limits_ref.shape[1]), 1) // (many // requests)
    for b in range(requests // per):
        limit = jnp.zeros(column.shape, jnp.int32)
        for r in range(per):
            limit = jnp.where(column == r, lengths_ref[first + b * per + r], limit)
        limits_ref[b : b + 1, :] = limit
    row = lax.broadcasted_iota(jnp.int32, holder_ref.shape, 0) // steps
    holder = jnp.zeros(holder_ref.shape, jnp.int32)
    for r in range(requests):
        holder = jnp.where(row == r, owner_ref[adapter_ref[first + r]], holder)
    holder_ref[...] = holder


def ready(where, lengths, adapter, owner, mine, other, fresh, steps):
    requests, count = lengths.shape[0] // 2, mine.shape[0] // lengths.shape[0]
    smem, vmem = (pl.BlockSpec(memory_space=m) for m in (pltpu.SMEM, pltpu.VMEM))
    anywhere = pl.BlockSpec(memory_space=pl.ANY)
    cache = jax.ShapeDtypeStruct((requests * count, mine.shape[1]), mine.dtype)
    return pl.pallas_call(
        ready_kernel,
        out_shape=(
            cache,
            cache,
            jax.ShapeDtypeStruct((requests * steps, fresh.shape[2]), fresh.dtype),
            jax.ShapeDtypeStruct((8, PER * count), jnp.int32),
            jax.ShapeDtypeStruct((requests * steps, 128), jnp.int32),
        ),
        in_specs=[smem] * 4 + [anywhere] * 2 + [vmem],
        out_specs=(vmem,) * 5,
        scratch_shapes=[pltpu.SemaphoreType.DMA((2,))],
        compiler_params=pltpu.CompilerParams(vmem_limit_bytes=4 << 20),
    )(where, lengths, adapter, owner, mine, other, fresh)


def products_kernel(sets, *refs):
    rows, weights, out_ref = refs[:sets], refs[sets:-1], refs[-1]
    width = rows[0].shape[1] // 2
    firsts, seconds = (
        jnp.concatenate([w[:, :width] for w in weights[k::2]], axis=0) for k in range(2)
    )
    known = seconds.shape[0]
    total = nt_dot(jnp.concatenate([r[:, :width] for r in rows], axis=0), firsts)
    more = nt_dot(jnp.concatenate([r[:, width:] for r in rows], axis=0), seconds)
    out_ref[:, :known] = total[:, :known] + more
    out_ref[:, known:] = total[:, known:]


def products(sets, weights):
    rows, columns = sum(r.shape[0] for r in sets), (len(weights) + 1) // 2 * weights[0].shape[0]
    return pl.pallas_call(
        functools.partial(products_kernel, len(sets)),
        out_shape=jax.ShapeDtypeStruct((rows, columns), jnp.float32),
        cost_estimate=pl.CostEstimate(
            flops=2 * rows * columns * sets[0].shape[1],
            bytes_accessed=(rows + columns) * sets[0].shape[1] * 2,
            transcendentals=0,
        ),
        compiler_params=pltpu.CompilerParams(vmem_limit_bytes=12 << 20),
    )(*sets, *weights)


def late_kernel(where_ref, *refs):
    sets, weights = refs[:5], refs[5:-5]
    t_ref, corner_ref, kept_ref, given_ref, up_ref = refs[-5:]
    half, width = sets[-1].shape[0], sets[-1].shape[1] // 2
    count = weights[0].shape[0]
    for k, ref in enumerate(weights):
        at = (k % 2) * (len(weights) // 2 * count) + (k // 2) * count
        up_ref[at : at + count] = ref[:, width:]
    last = nt_dot(jnp.concatenate([r[:, width:] for r in sets], axis=0), weights[-1][:, :width])
    first = where_ref[3] == 0
    known = t_ref.shape[1] - count
    for k in range(4):
        ref, base = (t_ref, 2 * k * half) if k < 3 else (corner_ref, 0)
        low, high = (
            jnp.concatenate(
                [
                    ref[base + p * half : base + (p + 1) * half, :known],
                    ref[base + p * half : base + (p + 1) * half, known:]
                    + last[(2 * k + p) * half : (2 * k + p + 1) * half],
                ],
                axis=1,
            )
            for p in range(2)
        )
        kept_ref[k] = jnp.where(first, low, high)
        given_ref[k] = jnp.where(first, high, low)


def late_products(where, sets, weights, t, corner):
    smem, vmem = (pl.BlockSpec(memory_space=m) for m in (pltpu.SMEM, pltpu.VMEM))
    count, lanes = weights[0].shape
    half, features = sets[-1].shape
    shape = jax.ShapeDtypeStruct((4, half, len(weights) // 2 * count), jnp.float32)
    up = (len(weights) * count, lanes - features // 2)
    return pl.pallas_call(
        late_kernel,
        out_shape=(shape, shape, jax.ShapeDtypeStruct(up, sets[0].dtype)),
        in_specs=[smem] + [vmem] * (len(sets) + len(weights) + 2),
        out_specs=(vmem,) * 3,
        compiler_params=pltpu.CompilerParams(vmem_limit_bytes=12 << 20),
    )(where, *sets, *weights, t, corner)


def join_kernel(where_ref, mine_ref, other_ref, queries_ref, attended_ref, sems):
    core = where_ref[3]
    count = mine_ref.shape[1]
    mine, other = pl.ds(core * count, count), pl.ds((1 - core) * count, count)
    copy_all(
        [
            (mine_ref.at[0], queries_ref.at[mine]), (mine_ref.at[1], attended_ref.at[mine]),
            (other_ref.at[0], queries_ref.at[other]), (other_ref.at[1], attended_ref.at[other]),
        ],
        sems,
    )


def join(where, mine, other):
    anywhere = pl.BlockSpec(memory_space=pl.ANY)
    shape = jax.ShapeDtypeStruct((2 * mine.shape[1],) + mine.shape[2:], mine.dtype)
    return pl.pallas_call(
        join_kernel,
        out_shape=(shape, shape),
        in_specs=[pl.BlockSpec(memory_space=pltpu.SMEM), anywhere, anywhere],
        out_specs=(anywhere, anywhere),
        scratch_shapes=[pltpu.SemaphoreType.DMA((4,))],
        compiler_params=pltpu.CompilerParams(vmem_limit_bytes=2 << 20),
    )(where, mine, other)


def add_kernel(a_ref, b_ref, *outs):
    for k, out in enumerate(outs):
        out[...] = a_ref[k + 1] + b_ref[k + 1]


def add_halves(a, b):
    shape = jax.ShapeDtypeStruct(a.shape[1:], a.dtype)
    return pl.pallas_call(
        add_kernel,
        out_shape=(shape,) * (a.shape[0] - 1),
        compiler_params=pltpu.CompilerParams(vmem_limit_bytes=2 << 20),
    )(a, b)


def attend_block(queries, keys, values, mask, scaling):
    scores = jnp.where(mask, nt_dot(queries, keys) * scaling, FAR)
    highest = scores.max(axis=1, keepdims=True)
    weights = jnp.where(mask, jnp.exp(scores - highest), 0.0)
    totals = weights.sum(axis=1, keepdims=True)
    sums = jnp.dot(weights.astype(jnp.bfloat16), values, preferred_element_type=jnp.float32)
    return sums / totals


def attend(queries, caches, fresh_ref, limit_of, put, steps, head, per):
    rows = queries.shape[0]
    requests = rows // steps
    heads = queries.shape[1] // head
    scaling = 1.0 / math.sqrt(head)
    take = per * steps
    for b in range(requests // per):
        part = queries[b * take : (b + 1) * take, :]
        stacked = jnp.concatenate([part[:, h * head : (h + 1) * head] for h in range(heads)], axis=0)
        limit = limit_of(b)
        keys, values, masks = [], [], []
        for c, cache_ref in enumerate(caches):
            count = cache_ref.shape[0] // requests
            block = cache_ref[b * per * count : (b + 1) * per * count, :]
            shape = (heads * take, per * count)
            request = lax.rem(lax.broadcasted_iota(jnp.int32, shape, 0), take) // steps
            column = lax.broadcasted_iota(jnp.int32, shape, 1)
            position = lax.rem(column, count) + c * count
            masks.append(jnp.logical_and(column // count == request, position < limit))
            keys.append(block[:, :head])
            values.append(block[:, head:])
        block = fresh_ref[b * take : (b + 1) * take, :]
        shape = (heads * take, take)
        row = lax.rem(lax.broadcasted_iota(jnp.int32, shape, 0), take)
        column = lax.broadcasted_iota(jnp.int32, shape, 1)
        masks.append(jnp.logical_and(row // steps == column // steps, column <= row))
        keys.append(block[:, :head])
        values.append(block[:, head:])
        mixed = attend_block(
            stacked, *(jnp.concatenate(a, axis=0) for a in (keys, values)),
            jnp.concatenate(masks, axis=1), scaling,
        ).astype(jnp.bfloat16)
        put(
            b,
            jnp.concatenate([mixed[h * take : (h + 1) * take] for h in range(heads)], axis=1),
        )


def finish_kernel(
    steps, where_ref, own_ref, other_ref, beside_ref, across_ref, both_ref, holder_ref,
    up_ref, up_other_ref, low_ref, high_ref, fresh_ref, limits_ref, out_ref,
):
    rows = own_ref.shape[1]
    x, part = where_ref[1], where_ref[2]
    width = 128
    half = width // 2
    own = own_ref[0] + other_ref[0]
    beside, across, both = beside_ref[...], across_ref[...], both_ref[...]
    queries_here = part == 0
    columns = jnp.where(queries_here, own, across), jnp.where(queries_here, beside, both)
    ranks = jnp.where(queries_here, across, own), jnp.where(queries_here, both, beside)
    low_lanes = lax.broadcasted_iota(jnp.int32, (rows, width), 1) < half
    even = jnp.where(x == 0, columns[0], columns[1])
    odd = jnp.where(x == 0, columns[1], columns[0])

    def spaced(wide):
        out = []
        for j in range(4):
            pair = wide[:, (j // 2) * width : (j // 2 + 1) * width]
            out.append((pair, pltpu.roll(pair, half, 1)) if j % 2 == 0 else (pltpu.roll(pair, half, 1), pair))
        return out

    even, odd = spaced(even), spaced(odd)
    merged = [jnp.where(low_lanes, e[0], o[1]) for e, o in zip(even, odd)]
    groups = []
    for k in range(4):
        group = merged[3]
        for j in range(3):
            group = jnp.where(where_ref[4 + j] == 2 * k + x, merged[j], group)
        groups.append(group)
    base = jnp.concatenate(groups, axis=1)
    holder = holder_ref[...]
    spread = []
    for m in range(4):
        lane_owner = jnp.where(low_lanes, where_ref[4 + 2 * m], where_ref[5 + 2 * m])
        shrink = ranks[m // 2][:, (m % 2) * width : (m % 2 + 1) * width]
        spread.append(jnp.where(holder == lane_owner, shrink, 0.0).astype(jnp.bfloat16))
    spread = jnp.concatenate(spread, axis=1)
    mine, other = (
        jnp.dot(spread, ref[...], preferred_element_type=jnp.float32) for ref in (up_ref, up_other_ref)
    )
    first = where_ref[3] == 0
    adapted = jnp.concatenate([jnp.where(first, mine, other), jnp.where(first, other, mine)], axis=1)
    queries = (base + adapted).astype(jnp.bfloat16)
    requests = rows // steps
    out_ref[0] = queries.reshape(requests, steps, -1)
    head = fresh_ref.shape[1] // 2

    def put(b, mixed):
        out_ref[1, b * PER : (b + 1) * PER] = mixed.reshape(PER, steps, -1)

    attend(
        queries, (low_ref, high_ref), fresh_ref, lambda b: limits_ref[b : b + 1, :], put, steps, head, PER
    )


def finish(steps, where, *arrays):
    rows, up = arrays[0].shape[1], arrays[6]
    vmem = pl.BlockSpec(memory_space=pltpu.VMEM)
    return pl.pallas_call(
        functools.partial(finish_kernel, steps),
        out_shape=jax.ShapeDtypeStruct((2, rows // steps, steps, 2 * up.shape[1]), jnp.bfloat16),
        in_specs=[pl.BlockSpec(memory_space=pltpu.SMEM)] + [vmem] * len(arrays),
        out_specs=vmem,
        compiler_params=pltpu.CompilerParams(vmem_limit_bytes=8 << 20),
    )(where, *arrays)


def attend_kernel(steps, q_ref, low_ref, high_ref, fresh_ref, limits_ref, out_ref):
    head = fresh_ref.shape[1] // 2
    take = PER * steps

    def put(b, mixed):
        out_ref[b * take : (b + 1) * take, :] = mixed

    attend(
        q_ref[...], (low_ref, high_ref), fresh_ref, lambda b: limits_ref[b : b + 1, :], put, steps, head, PER
    )


def line_pairs(groups, moves):
    return [(a * 2 + x, b * 2 + x) for a, b in moves for x in range(2)]


def holders_of(request_adapter, adapter_owner):
    ids = jnp.arange(adapter_owner.shape[0], dtype=jnp.int32)
    lookup = request_adapter[:, None] == ids[None, :]
    return jnp.sum(jnp.where(lookup, adapter_owner[None, :], 0), axis=1)


def body(
    normed_hidden_states,
    query_matrix,
    factor_down,
    factor_up,
    kv_cache,
    incoming_key_value,
    kv_lengths,
    request_adapter,
    adapter_owner,
):
    groups = lax.axis_size("group")
    core = lax.axis_index("tensor")
    requests, steps, features = normed_hidden_states.shape
    rows = requests * steps

    down = factor_down[0].T
    down_other = lax.ppermute(factor_down, "tensor", SWAP)[0].T
    query_block = query_matrix.T
    width = query_matrix.shape[1] * groups
    out_shape = (requests, steps, width)

    if groups == 8 and lax.axis_size("parts") == 2 and query_matrix.shape[1] == 2 * down.shape[0]:
        place = lax.axis_index("group")
        z, x, part = place // 2, lax.rem(place, 2), lax.axis_index("parts")
        order = z ^ (z // 2)
        steps_back = [lax.rem(order + k, 4) for k in range(4)]
        places = [k ^ (k // 2) for k in steps_back]
        where = [z, x, part, core] + [p * 2 + x for p in places] + [p * 2 + 1 - x for p in places]
        where = jnp.stack(where).astype(jnp.int32)
        bar = lambda *a: lax.optimization_barrier(a)
        along = lambda a, moves: lax.ppermute(a, "group", line_pairs(groups, moves))
        across = lambda a: lax.ppermute(a, "parts", SWAP)
        beside = lambda a: lax.ppermute(a, "group", [(i, i ^ 1) for i in range(groups)])
        inside = lambda a: lax.ppermute(a, "tensor", SWAP)
        corner = [(p * groups + i, (1 - p) * groups + (i ^ 1)) for p in range(2) for i in range(groups)]
        ring = ((1, 0), (3, 1), (2, 3), (0, 2))

        half = rows // 2
        mine = rows_of(normed_hidden_states)
        up_beside = beside(factor_up[0])
        a0, b0 = block_of(where, query_block, down, down_other, factor_up[0], up_beside)
        a0, b0, mine = bar(a0, b0, mine)
        a1, b1 = along(a0, ring), along(b0, ring)
        x_beside, x_across = beside(mine), across(mine)
        a2 = along(a1, ring)
        b2 = along(b1, ring)
        a3 = along(a2, ring)
        low, high = beside(x_across[:half]), across(x_beside[half:])
        cache = kv_cache.reshape(-1, kv_cache.shape[2])
        prepared = ready(
            where, kv_lengths, request_adapter, adapter_owner, cache, inside(cache), incoming_key_value, steps
        )
        b2, x_across, prepared = bar(b2, x_across, prepared)
        b3 = along(b2, ring)
        weights = a0, b0, a1, b1, a2, b2, a3, b3
        sets = mine, x_beside, x_across
        t, corner_t = products(sets, weights[:-1]), products((low, high), weights[:-1])

        t, corner_t, prepared = bar(t, corner_t, prepared)
        kept, given, up = late_products(where, sets + (low, high), weights, t, corner_t)
        got = inside(given)
        t_beside, t_across, t_both = add_halves(kept, got)
        t_beside, t_across = beside(t_beside), across(t_across)
        t_both = lax.ppermute(t_both, ("parts", "group"), corner)
        cache_low, cache_high, fresh, limits, holder_rows = prepared
        done = finish(
            steps, where, kept, got, t_beside, t_across, t_both, holder_rows, up, inside(up),
            cache_low, cache_high, fresh, limits,
        )
        return join(where, done, inside(done))

    mine_down = lax.dynamic_slice_in_dim(down, core * features, features, 1)
    other_down = lax.dynamic_slice_in_dim(down_other, core * features, features, 1)
    down_block = jnp.where(
        core == 0,
        jnp.concatenate([mine_down, other_down], 0),
        jnp.concatenate([other_down, mine_down], 0),
    )
    holder = holders_of(request_adapter, adapter_owner)
    holder_rows = jnp.repeat(holder, steps)[:, None]
    limits = jnp.repeat(kv_lengths, kv_cache.shape[1]).reshape(requests // PER, -1)
    own = normed_hidden_states.reshape(rows, features)
    other_cache = lax.ppermute(kv_cache, "tensor", SWAP)
    low = jnp.where(core == 0, kv_cache, other_cache).reshape(-1, kv_cache.shape[2])
    high = jnp.where(core == 0, other_cache, kv_cache).reshape(-1, kv_cache.shape[2])
    fresh = incoming_key_value.reshape(rows, -1)
    up = lax.all_gather(factor_up[0], "group", axis=0, tiled=True)
    up_other = lax.ppermute(up, "tensor", SWAP)
    up_full = jnp.where(
        core == 0, jnp.concatenate([up, up_other], 1), jnp.concatenate([up_other, up], 1)
    )

    place = lax.axis_index("group")
    ring = [(i, (i + 1) % groups) for i in range(groups)]

    def step(k, carry):
        q_part, d_part, base, shrink = carry
        at = lax.rem(place - k + groups, groups)
        base = lax.dynamic_update_slice_in_dim(base, nt_dot(own, q_part), at * q_part.shape[0], 1)
        shrink = shrink + jnp.where(holder_rows == at, nt_dot(own, d_part), 0.0)
        q_part, d_part = (lax.ppermute(w, "group", ring) for w in (q_part, d_part))
        return q_part, d_part, base, shrink

    start = (
        query_block,
        down_block,
        jnp.zeros((rows, width), jnp.float32),
        jnp.zeros((rows, down_block.shape[0]), jnp.float32),
    )
    _, _, base, shrink = lax.fori_loop(0, groups, step, start)
    base = base + lax.ppermute(base, "tensor", SWAP)
    shrink = (shrink + lax.ppermute(shrink, "tensor", SWAP)).astype(jnp.bfloat16)
    named = holder_rows == jnp.arange(groups, dtype=jnp.int32)[None, :]
    spread = jnp.where(named[:, :, None], shrink[:, None, :], 0).reshape(rows, -1)
    adapted = jnp.dot(spread, up_full, preferred_element_type=jnp.float32)
    queries = (base + adapted).astype(jnp.bfloat16)
    attended = pl.pallas_call(
        functools.partial(attend_kernel, steps),
        out_shape=jax.ShapeDtypeStruct(queries.shape, jnp.bfloat16),
        compiler_params=pltpu.CompilerParams(vmem_limit_bytes=24 << 20),
    )(queries, low, high, fresh, limits)
    return queries.reshape(out_shape), attended.reshape(out_shape)


def solution(mesh):
    placed = (
        P(("parts", "group"), None, "tensor"),
        P("tensor", "group"),
        P("group", None, "tensor"),
        P("group", None, "tensor"),
        P(("parts", "group"), "tensor", None),
        P(("parts", "group"), None, None),
        P(("parts", "group")),
        P(("parts", "group")),
        P("parts"),
    )
    return jax.shard_map(
        body,
        mesh=mesh,
        in_specs=placed,
        out_specs=(P(("parts", "group"), None, None), P(("parts", "group"), None, None)),
        check_vma=False,
    )
```

```python
import functools
import math

import jax
import jax.numpy as jnp
from jax import lax
from jax.experimental import pallas as pl
from jax.experimental.pallas import tpu as pltpu
from jax.sharding import PartitionSpec as P

SWAP = [(0, 1), (1, 0)]
FAR = -1e30
PER = 16


def nt_dot(a, b):
    return lax.dot_general(a, b, (((1,), (1,)), ((), ())), preferred_element_type=jnp.float32)


def copy_all(copies, sems):
    started = [pltpu.make_async_copy(source, target, sems.at[k]) for k, (source, target) in enumerate(copies)]
    for copy in started:
        copy.start()
    for copy in started:
        copy.wait()


def block_kernel(
    where_ref, query_ref, kept_ref, given_ref, up_ref, up_beside_ref, a_ref, b_ref, sems
):
    part, core = where_ref[2], where_ref[3]
    count, width = kept_ref.shape[0], query_ref.shape[1] // 2
    chunks = [ref.at[:, :width] for ref in (a_ref, b_ref)]
    ups = [(up_ref, a_ref.at[:, width:]), (up_beside_ref, b_ref.at[:, width:])]

    @pl.when(part == 0)
    def _():
        copy_all([(query_ref.at[:, k * width : (k + 1) * width], chunks[k]) for k in range(2)] + ups, sems)

    for own in range(2):

        @pl.when(jnp.logical_and(part != 0, core == own))
        def _():
            copies = []
            for k in range(2):
                features = slice((2 * own + k) * width, (2 * own + k + 1) * width)
                for owner in range(2):
                    source = kept_ref if owner == own else given_ref
                    target = (a_ref, b_ref)[k].at[owner * count : (owner + 1) * count, :width]
                    copies.append((source.at[:, features], target))
            copy_all(copies + ups, sems)


def block_of(where, query, kept, given, up, up_beside):
    vmem = pl.BlockSpec(memory_space=pltpu.VMEM)
    shape = jax.ShapeDtypeStruct((query.shape[0], query.shape[1] // 2 + up.shape[1]), query.dtype)
    return pl.pallas_call(
        block_kernel,
        out_shape=(shape, shape),
        in_specs=[pl.BlockSpec(memory_space=pltpu.SMEM)] + [pl.BlockSpec(memory_space=pl.ANY)] * 5,
        out_specs=(vmem, vmem),
        scratch_shapes=[pltpu.SemaphoreType.DMA((6,))],
        compiler_params=pltpu.CompilerParams(vmem_limit_bytes=2 << 20),
    )(where, query, kept, given, up, up_beside)


def rows_kernel(x_ref, out_ref):
    out_ref[...] = x_ref[...].reshape(out_ref.shape)


def rows_of(x):
    return pl.pallas_call(
        rows_kernel,
        out_shape=jax.ShapeDtypeStruct((x.shape[0] * x.shape[1], x.shape[2]), x.dtype),
        compiler_params=pltpu.CompilerParams(vmem_limit_bytes=4 << 20),
    )(x)


def ready_kernel(
    where_ref, lengths_ref, adapter_ref, owner_ref, mine_ref, other_ref, fresh_ref,
    low_ref, high_ref, new_ref, limits_ref, holder_ref, sems,
):
    core = where_ref[3]
    half = new_ref.shape[0]
    requests = lengths_ref.shape[0] // 2
    steps = half // requests
    many = low_ref.shape[0]
    for k, (low, high) in enumerate(((mine_ref, other_ref), (other_ref, mine_ref))):

        @pl.when(core == k)
        def _():
            rows = slice(k * many, (k + 1) * many)
            copy_all([(low.at[rows], low_ref), (high.at[rows], high_ref)], sems)
            new_ref[...] = fresh_ref[k * requests : (k + 1) * requests].reshape(new_ref.shape)

    first = core * requests
    per = limits_ref.shape[1] // (many // requests)
    column = lax.broadcasted_iota(jnp.int32, (1, limits_ref.shape[1]), 1) // (many // requests)
    for b in range(requests // per):
        limit = jnp.zeros(column.shape, jnp.int32)
        for r in range(per):
            limit = jnp.where(column == r, lengths_ref[first + b * per + r], limit)
        limits_ref[b : b + 1, :] = limit
    row = lax.broadcasted_iota(jnp.int32, holder_ref.shape, 0) // steps
    holder = jnp.zeros(holder_ref.shape, jnp.int32)
    for r in range(requests):
        holder = jnp.where(row == r, owner_ref[adapter_ref[first + r]], holder)
    holder_ref[...] = holder


def ready(where, lengths, adapter, owner, mine, other, fresh, steps):
    requests, count = lengths.shape[0] // 2, mine.shape[0] // lengths.shape[0]
    smem, vmem = (pl.BlockSpec(memory_space=m) for m in (pltpu.SMEM, pltpu.VMEM))
    anywhere = pl.BlockSpec(memory_space=pl.ANY)
    cache = jax.ShapeDtypeStruct((requests * count, mine.shape[1]), mine.dtype)
    return pl.pallas_call(
        ready_kernel,
        out_shape=(
            cache,
            cache,
            jax.ShapeDtypeStruct((requests * steps, fresh.shape[2]), fresh.dtype),
            jax.ShapeDtypeStruct((8, PER * count), jnp.int32),
            jax.ShapeDtypeStruct((requests * steps, 128), jnp.int32),
        ),
        in_specs=[smem] * 4 + [anywhere] * 2 + [vmem],
        out_specs=(vmem,) * 5,
        scratch_shapes=[pltpu.SemaphoreType.DMA((2,))],
        compiler_params=pltpu.CompilerParams(vmem_limit_bytes=4 << 20),
    )(where, lengths, adapter, owner, mine, other, fresh)


def products_kernel(sets, *refs):
    rows, weights, out_ref = refs[:sets], refs[sets:-1], refs[-1]
    width = rows[0].shape[1] // 2
    firsts, seconds = (
        jnp.concatenate([w[:, :width] for w in weights[k::2]], axis=0) for k in range(2)
    )
    known = seconds.shape[0]
    total = nt_dot(jnp.concatenate([r[:, :width] for r in rows], axis=0), firsts)
    more = nt_dot(jnp.concatenate([r[:, width:] for r in rows], axis=0), seconds)
    out_ref[:, :known] = total[:, :known] + more
    out_ref[:, known:] = total[:, known:]


def products(sets, weights):
    rows, columns = sum(r.shape[0] for r in sets), (len(weights) + 1) // 2 * weights[0].shape[0]
    return pl.pallas_call(
        functools.partial(products_kernel, len(sets)),
        out_shape=jax.ShapeDtypeStruct((rows, columns), jnp.float32),
        cost_estimate=pl.CostEstimate(
            flops=2 * rows * columns * sets[0].shape[1],
            bytes_accessed=(rows + columns) * sets[0].shape[1] * 2,
            transcendentals=0,
        ),
        compiler_params=pltpu.CompilerParams(vmem_limit_bytes=12 << 20),
    )(*sets, *weights)


def late_kernel(where_ref, *refs):
    sets, weights = refs[:5], refs[5:-5]
    t_ref, corner_ref, kept_ref, given_ref, up_ref = refs[-5:]
    half, width = sets[-1].shape[0], sets[-1].shape[1] // 2
    count = weights[0].shape[0]
    for k, ref in enumerate(weights):
        at = (k % 2) * (len(weights) // 2 * count) + (k // 2) * count
        up_ref[at : at + count] = ref[:, width:]
    last = nt_dot(jnp.concatenate([r[:, width:] for r in sets], axis=0), weights[-1][:, :width])
    first = where_ref[3] == 0
    known = t_ref.shape[1] - count
    for k in range(4):
        ref, base = (t_ref, 2 * k * half) if k < 3 else (corner_ref, 0)
        low, high = (
            jnp.concatenate(
                [
                    ref[base + p * half : base + (p + 1) * half, :known],
                    ref[base + p * half : base + (p + 1) * half, known:]
                    + last[(2 * k + p) * half : (2 * k + p + 1) * half],
                ],
                axis=1,
            )
            for p in range(2)
        )
        kept_ref[k] = jnp.where(first, low, high)
        given_ref[k] = jnp.where(first, high, low)


def late_products(where, sets, weights, t, corner):
    smem, vmem = (pl.BlockSpec(memory_space=m) for m in (pltpu.SMEM, pltpu.VMEM))
    count, lanes = weights[0].shape
    half, features = sets[-1].shape
    shape = jax.ShapeDtypeStruct((4, half, len(weights) // 2 * count), jnp.float32)
    up = (len(weights) * count, lanes - features // 2)
    return pl.pallas_call(
        late_kernel,
        out_shape=(shape, shape, jax.ShapeDtypeStruct(up, sets[0].dtype)),
        in_specs=[smem] + [vmem] * (len(sets) + len(weights) + 2),
        out_specs=(vmem,) * 3,
        compiler_params=pltpu.CompilerParams(vmem_limit_bytes=12 << 20),
    )(where, *sets, *weights, t, corner)


def join_kernel(where_ref, mine_ref, other_ref, queries_ref, attended_ref, sems):
    core = where_ref[3]
    count = mine_ref.shape[1]
    mine, other = pl.ds(core * count, count), pl.ds((1 - core) * count, count)
    copy_all(
        [
            (mine_ref.at[0], queries_ref.at[mine]), (mine_ref.at[1], attended_ref.at[mine]),
            (other_ref.at[0], queries_ref.at[other]), (other_ref.at[1], attended_ref.at[other]),
        ],
        sems,
    )


def join(where, mine, other):
    anywhere = pl.BlockSpec(memory_space=pl.ANY)
    shape = jax.ShapeDtypeStruct((2 * mine.shape[1],) + mine.shape[2:], mine.dtype)
    return pl.pallas_call(
        join_kernel,
        out_shape=(shape, shape),
        in_specs=[pl.BlockSpec(memory_space=pltpu.SMEM), anywhere, anywhere],
        out_specs=(anywhere, anywhere),
        scratch_shapes=[pltpu.SemaphoreType.DMA((4,))],
        compiler_params=pltpu.CompilerParams(vmem_limit_bytes=2 << 20),
    )(where, mine, other)


def add_kernel(a_ref, b_ref, *outs):
    for k, out in enumerate(outs):
        out[...] = a_ref[k + 1] + b_ref[k + 1]


def add_halves(a, b):
    shape = jax.ShapeDtypeStruct(a.shape[1:], a.dtype)
    return pl.pallas_call(
        add_kernel,
        out_shape=(shape,) * (a.shape[0] - 1),
        compiler_params=pltpu.CompilerParams(vmem_limit_bytes=2 << 20),
    )(a, b)


def attend_block(queries, keys, values, mask, scaling):
    scores = jnp.where(mask, nt_dot(queries, keys) * scaling, FAR)
    highest = scores.max(axis=1, keepdims=True)
    weights = jnp.exp(scores - highest)
    totals = weights.sum(axis=1, keepdims=True)
    sums = jnp.dot(weights.astype(jnp.bfloat16), values, preferred_element_type=jnp.float32)
    return sums / totals


def attend(queries, caches, fresh_ref, limit_of, put, steps, head, per):
    rows = queries.shape[0]
    requests = rows // steps
    heads = queries.shape[1] // head
    scaling = 1.0 / math.sqrt(head)
    take = per * steps
    for b in range(requests // per):
        part = queries[b * take : (b + 1) * take, :]
        stacked = jnp.concatenate([part[:, h * head : (h + 1) * head] for h in range(heads)], axis=0)
        limit = limit_of(b)
        keys, values, masks = [], [], []
        for c, cache_ref in enumerate(caches):
            count = cache_ref.shape[0] // requests
            block = cache_ref[b * per * count : (b + 1) * per * count, :]
            shape = (heads * take, per * count)
            request = lax.rem(lax.broadcasted_iota(jnp.int32, shape, 0), take) // steps
            column = lax.broadcasted_iota(jnp.int32, shape, 1)
            position = lax.rem(column, count) + c * count
            masks.append(jnp.logical_and(column // count == request, position < limit))
            keys.append(block[:, :head])
            values.append(block[:, head:])
        block = fresh_ref[b * take : (b + 1) * take, :]
        shape = (heads * take, take)
        row = lax.rem(lax.broadcasted_iota(jnp.int32, shape, 0), take)
        column = lax.broadcasted_iota(jnp.int32, shape, 1)
        masks.append(jnp.logical_and(row // steps == column // steps, column <= row))
        keys.append(block[:, :head])
        values.append(block[:, head:])
        mixed = attend_block(
            stacked, *(jnp.concatenate(a, axis=0) for a in (keys, values)),
            jnp.concatenate(masks, axis=1), scaling,
        ).astype(jnp.bfloat16)
        put(
            b,
            jnp.concatenate([mixed[h * take : (h + 1) * take] for h in range(heads)], axis=1),
        )


def finish_kernel(
    steps, where_ref, own_ref, other_ref, beside_ref, across_ref, both_ref, holder_ref,
    up_ref, up_other_ref, low_ref, high_ref, fresh_ref, limits_ref, out_ref,
):
    rows = own_ref.shape[1]
    x, part = where_ref[1], where_ref[2]
    width = 128
    half = width // 2
    own = own_ref[0] + other_ref[0]
    beside, across, both = beside_ref[...], across_ref[...], both_ref[...]
    queries_here = part == 0
    columns = jnp.where(queries_here, own, across), jnp.where(queries_here, beside, both)
    ranks = jnp.where(queries_here, across, own), jnp.where(queries_here, both, beside)
    low_lanes = lax.broadcasted_iota(jnp.int32, (rows, width), 1) < half
    even = jnp.where(x == 0, columns[0], columns[1])
    odd = jnp.where(x == 0, columns[1], columns[0])

    def spaced(wide):
        out = []
        for j in range(4):
            pair = wide[:, (j // 2) * width : (j // 2 + 1) * width]
            out.append((pair, pltpu.roll(pair, half, 1)) if j % 2 == 0 else (pltpu.roll(pair, half, 1), pair))
        return out

    even, odd = spaced(even), spaced(odd)
    merged = [jnp.where(low_lanes, e[0], o[1]) for e, o in zip(even, odd)]
    groups = []
    for k in range(4):
        group = merged[3]
        for j in range(3):
            group = jnp.where(where_ref[4 + j] == 2 * k + x, merged[j], group)
        groups.append(group)
    base = jnp.concatenate(groups, axis=1)
    holder = holder_ref[...]
    spread = []
    for m in range(4):
        lane_owner = jnp.where(low_lanes, where_ref[4 + 2 * m], where_ref[5 + 2 * m])
        shrink = ranks[m // 2][:, (m % 2) * width : (m % 2 + 1) * width]
        spread.append(jnp.where(holder == lane_owner, shrink, 0.0).astype(jnp.bfloat16))
    spread = jnp.concatenate(spread, axis=1)
    mine, other = (
        jnp.dot(spread, ref[...], preferred_element_type=jnp.float32) for ref in (up_ref, up_other_ref)
    )
    first = where_ref[3] == 0
    adapted = jnp.concatenate([jnp.where(first, mine, other), jnp.where(first, other, mine)], axis=1)
    queries = (base + adapted).astype(jnp.bfloat16)
    requests = rows // steps
    out_ref[0] = queries.reshape(requests, steps, -1)
    head = fresh_ref.shape[1] // 2

    def put(b, mixed):
        out_ref[1, b * PER : (b + 1) * PER] = mixed.reshape(PER, steps, -1)

    attend(
        queries, (low_ref, high_ref), fresh_ref, lambda b: limits_ref[b : b + 1, :], put, steps, head, PER
    )


def finish(steps, where, *arrays):
    rows, up = arrays[0].shape[1], arrays[6]
    vmem = pl.BlockSpec(memory_space=pltpu.VMEM)
    return pl.pallas_call(
        functools.partial(finish_kernel, steps),
        out_shape=jax.ShapeDtypeStruct((2, rows // steps, steps, 2 * up.shape[1]), jnp.bfloat16),
        in_specs=[pl.BlockSpec(memory_space=pltpu.SMEM)] + [vmem] * len(arrays),
        out_specs=vmem,
        compiler_params=pltpu.CompilerParams(vmem_limit_bytes=8 << 20),
    )(where, *arrays)


def attend_kernel(steps, q_ref, low_ref, high_ref, fresh_ref, limits_ref, out_ref):
    head = fresh_ref.shape[1] // 2
    take = PER * steps

    def put(b, mixed):
        out_ref[b * take : (b + 1) * take, :] = mixed

    attend(
        q_ref[...], (low_ref, high_ref), fresh_ref, lambda b: limits_ref[b : b + 1, :], put, steps, head, PER
    )


def line_pairs(groups, moves):
    return [(a * 2 + x, b * 2 + x) for a, b in moves for x in range(2)]


def holders_of(request_adapter, adapter_owner):
    ids = jnp.arange(adapter_owner.shape[0], dtype=jnp.int32)
    lookup = request_adapter[:, None] == ids[None, :]
    return jnp.sum(jnp.where(lookup, adapter_owner[None, :], 0), axis=1)


def body(
    normed_hidden_states,
    query_matrix,
    factor_down,
    factor_up,
    kv_cache,
    incoming_key_value,
    kv_lengths,
    request_adapter,
    adapter_owner,
):
    groups = lax.axis_size("group")
    core = lax.axis_index("tensor")
    requests, steps, features = normed_hidden_states.shape
    rows = requests * steps

    down = factor_down[0].T
    down_other = lax.ppermute(factor_down, "tensor", SWAP)[0].T
    query_block = query_matrix.T
    width = query_matrix.shape[1] * groups
    out_shape = (requests, steps, width)

    if groups == 8 and lax.axis_size("parts") == 2 and query_matrix.shape[1] == 2 * down.shape[0]:
        place = lax.axis_index("group")
        z, x, part = place // 2, lax.rem(place, 2), lax.axis_index("parts")
        order = z ^ (z // 2)
        steps_back = [lax.rem(order + k, 4) for k in range(4)]
        places = [k ^ (k // 2) for k in steps_back]
        where = [z, x, part, core] + [p * 2 + x for p in places] + [p * 2 + 1 - x for p in places]
        where = jnp.stack(where).astype(jnp.int32)
        bar = lambda *a: lax.optimization_barrier(a)
        along = lambda a, moves: lax.ppermute(a, "group", line_pairs(groups, moves))
        across = lambda a: lax.ppermute(a, "parts", SWAP)
        beside = lambda a: lax.ppermute(a, "group", [(i, i ^ 1) for i in range(groups)])
        inside = lambda a: lax.ppermute(a, "tensor", SWAP)
        corner = [(p * groups + i, (1 - p) * groups + (i ^ 1)) for p in range(2) for i in range(groups)]
        ring = ((1, 0), (3, 1), (2, 3), (0, 2))

        half = rows // 2
        mine = rows_of(normed_hidden_states)
        up_beside = beside(factor_up[0])
        a0, b0 = block_of(where, query_block, down, down_other, factor_up[0], up_beside)
        a0, b0, mine = bar(a0, b0, mine)
        a1, b1 = along(a0, ring), along(b0, ring)
        x_beside, x_across = beside(mine), across(mine)
        a2 = along(a1, ring)
        b2 = along(b1, ring)
        a3 = along(a2, ring)
        low, high = beside(x_across[:half]), across(x_beside[half:])
        cache = kv_cache.reshape(-1, kv_cache.shape[2])
        prepared = ready(
            where, kv_lengths, request_adapter, adapter_owner, cache, inside(cache), incoming_key_value, steps
        )
        b2, x_across, prepared = bar(b2, x_across, prepared)
        b3 = along(b2, ring)
        weights = a0, b0, a1, b1, a2, b2, a3, b3
        sets = mine, x_beside, x_across
        t, corner_t = products(sets, weights[:-1]), products((low, high), weights[:-1])

        t, corner_t, prepared = bar(t, corner_t, prepared)
        kept, given, up = late_products(where, sets + (low, high), weights, t, corner_t)
        got = inside(given)
        t_beside, t_across, t_both = add_halves(kept, got)
        t_beside, t_across = beside(t_beside), across(t_across)
        t_both = lax.ppermute(t_both, ("parts", "group"), corner)
        cache_low, cache_high, fresh, limits, holder_rows = prepared
        done = finish(
            steps, where, kept, got, t_beside, t_across, t_both, holder_rows, up, inside(up),
            cache_low, cache_high, fresh, limits,
        )
        return join(where, done, inside(done))

    mine_down = lax.dynamic_slice_in_dim(down, core * features, features, 1)
    other_down = lax.dynamic_slice_in_dim(down_other, core * features, features, 1)
    down_block = jnp.where(
        core == 0,
        jnp.concatenate([mine_down, other_down], 0),
        jnp.concatenate([other_down, mine_down], 0),
    )
    holder = holders_of(request_adapter, adapter_owner)
    holder_rows = jnp.repeat(holder, steps)[:, None]
    limits = jnp.repeat(kv_lengths, kv_cache.shape[1]).reshape(requests // PER, -1)
    own = normed_hidden_states.reshape(rows, features)
    other_cache = lax.ppermute(kv_cache, "tensor", SWAP)
    low = jnp.where(core == 0, kv_cache, other_cache).reshape(-1, kv_cache.shape[2])
    high = jnp.where(core == 0, other_cache, kv_cache).reshape(-1, kv_cache.shape[2])
    fresh = incoming_key_value.reshape(rows, -1)
    up = lax.all_gather(factor_up[0], "group", axis=0, tiled=True)
    up_other = lax.ppermute(up, "tensor", SWAP)
    up_full = jnp.where(
        core == 0, jnp.concatenate([up, up_other], 1), jnp.concatenate([up_other, up], 1)
    )

    place = lax.axis_index("group")
    ring = [(i, (i + 1) % groups) for i in range(groups)]

    def step(k, carry):
        q_part, d_part, base, shrink = carry
        at = lax.rem(place - k + groups, groups)
        base = lax.dynamic_update_slice_in_dim(base, nt_dot(own, q_part), at * q_part.shape[0], 1)
        shrink = shrink + jnp.where(holder_rows == at, nt_dot(own, d_part), 0.0)
        q_part, d_part = (lax.ppermute(w, "group", ring) for w in (q_part, d_part))
        return q_part, d_part, base, shrink

    start = (
        query_block,
        down_block,
        jnp.zeros((rows, width), jnp.float32),
        jnp.zeros((rows, down_block.shape[0]), jnp.float32),
    )
    _, _, base, shrink = lax.fori_loop(0, groups, step, start)
    base = base + lax.ppermute(base, "tensor", SWAP)
    shrink = (shrink + lax.ppermute(shrink, "tensor", SWAP)).astype(jnp.bfloat16)
    named = holder_rows == jnp.arange(groups, dtype=jnp.int32)[None, :]
    spread = jnp.where(named[:, :, None], shrink[:, None, :], 0).reshape(rows, -1)
    adapted = jnp.dot(spread, up_full, preferred_element_type=jnp.float32)
    queries = (base + adapted).astype(jnp.bfloat16)
    attended = pl.pallas_call(
        functools.partial(attend_kernel, steps),
        out_shape=jax.ShapeDtypeStruct(queries.shape, jnp.bfloat16),
        compiler_params=pltpu.CompilerParams(vmem_limit_bytes=24 << 20),
    )(queries, low, high, fresh, limits)
    return queries.reshape(out_shape), attended.reshape(out_shape)


def solution(mesh):
    placed = (
        P(("parts", "group"), None, "tensor"),
        P("tensor", "group"),
        P("group", None, "tensor"),
        P("group", None, "tensor"),
        P(("parts", "group"), "tensor", None),
        P(("parts", "group"), None, None),
        P(("parts", "group")),
        P(("parts", "group")),
        P("parts"),
    )
    return jax.shard_map(
        body,
        mesh=mesh,
        in_specs=placed,
        out_specs=(P(("parts", "group"), None, None), P(("parts", "group"), None, None)),
        check_vma=False,
    )
```
